32 devices in a mesh: dp: 16 (over z, x, core), tensor: 2 (over y).
Axes of the slice: x: 2, y: 2, z: 4, core: 2. Of those that a mesh axis runs over, the one named last changes fastest.
Arguments:
- features: bfloat16 [65536, 512], P('dp', 'tensor'), may hold values from -6 to 6
- tangents: bfloat16 [3, 65536, 512], P(None, 'dp', 'tensor'), may hold values from -6 to 6
- weight_in: bfloat16 [2, 512, 512], P(None, None, 'tensor'), may hold values from -0.25 to 0.25
- bias_in: float32 [2, 512], P(None, 'tensor'), may hold values from -3 to 3
- weight_out: bfloat16 [2, 512, 512], P(None, 'tensor'), may hold values from -0.25 to 0.25
- bias_out: float32 [2, 512], P(None, 'tensor'), may hold values from -3 to 3
- true_counts: int32 [256], P('dp'), may hold values from 33 to 256, as said below
- cotangent_values: bfloat16 [65536, 512], P('dp', 'tensor'), may hold values from -6 to 6
- cotangent_tangents: bfloat16 [3, 65536, 512], P(None, 'dp', 'tensor'), may hold values from -6 to 6
Outputs:
- values_out: bfloat16 [65536, 512], P('dp', 'tensor')
- tangents_out: bfloat16 [3, 65536, 512], P(None, 'dp', 'tensor')
- values_grad: bfloat16 [65536, 512], P('dp', 'tensor')
- tangents_grad: bfloat16 [3, 65536, 512], P(None, 'dp', 'tensor')
- weight_in_grad: float32 [2, 512, 512], P(None, None, 'tensor')
- bias_in_grad: float32 [2, 512], P(None, 'tensor')
- weight_out_grad: float32 [2, 512, 512], P(None, 'tensor')
- bias_out_grad: float32 [2, 512], P(None, 'tensor')
The draws below stay inside these ranges and needn't reach their ends.
Inputs may be any that keep to these rules, and one draw needn't show every extreme that they name: `true_counts`: each source has between 33 and 256 live rows; some source is full in every draw.
All inputs are finite; a program needn't handle non-finite values.
Results may differ from the reference program's by a relative error of at most 0.0065.
Values may be sent and summed in bfloat16 or wider, within the bound.
No kernel may reach another device: no remote copies, remote signals or barrier semaphores. Data moves between devices by JAX's collectives and lax.ppermute only.
A program may use at most 448 MiB of HBM per device.

```python
import math
import jax
import jax.numpy as jnp
from jax import lax

D = 512
SLOT = 256
SOURCES = 256
ROWS = 65536


def draw_true_counts(key, part):
    key = jax.random.fold_in(key, 7)
    key_counts, key_chosen = jax.random.split(key)
    counts = jax.random.randint(key_counts, (SOURCES,), SLOT // 8 + 1, SLOT + 1)
    chosen = jax.random.randint(key_chosen, (), 0, SOURCES)
    return jnp.where(jnp.arange(SOURCES) == chosen, SLOT, counts).astype(jnp.int32)


def block_levels(stream_key, dims, cuts, low, top_value):
    gain, own = 1.0, jax.random.fold_in(stream_key, 6)
    for position, blocks in cuts:
        steps = jnp.exp(jax.random.uniform(jax.random.fold_in(own, position), (blocks,), jnp.float32, low / len(cuts), top_value / len(cuts)))
        gain = gain * jnp.repeat(steps, dims[position] // blocks).reshape([-1 if axis == position else 1 for axis in range(len(dims))])
    return gain


def noise(key, dims, deviation, reach, cuts=(), held_as=jnp.bfloat16):
    array = jax.random.normal(key, dims, jnp.float32) * deviation
    if len(cuts) > 0:
        array = block_levels(key, dims, cuts, -0.22, 0.18) * array
    return jnp.clip(array, min=-reach, max=reach).astype(held_as)


def setup_inputs(seed: int = 0) -> dict:
    streams_of = jax.random.split(jax.random.key(seed), 10)
    features = noise(streams_of[0], (ROWS, D), 1.0, 6.0, ((0, 16), (1, 2)))
    tangents = noise(streams_of[1], (3, ROWS, D), 1.0, 6.0, ((1, 16), (2, 2)))
    weight_in = noise(streams_of[2], (2, D, D), D ** -0.5, 0.25, ((2, 2),))
    bias_in = noise(streams_of[3], (2, D), 0.5, 3.0, ((1, 2),), jnp.float32)
    weight_out = noise(streams_of[4], (2, D, D), D ** -0.5, 0.25, ((1, 2),))
    bias_out = noise(streams_of[5], (2, D), 0.5, 3.0, ((1, 2),), jnp.float32)
    true_counts = draw_true_counts(jax.random.fold_in(streams_of[9], 71), 0)
    cotangent_values = noise(streams_of[7], (ROWS, D), 1.0, 6.0, ((0, 16), (1, 2)))
    cotangent_tangents = noise(streams_of[8], (3, ROWS, D), 1.0, 6.0, ((1, 16), (2, 2)))
    return {"features": features, "tangents": tangents, "weight_in": weight_in, "bias_in": bias_in, "weight_out": weight_out, "bias_out": bias_out, "true_counts": true_counts, "cotangent_values": cotangent_values, "cotangent_tangents": cotangent_tangents}


@jax.custom_vjp
def low(v):
    return lax.optimization_barrier(v.astype(jnp.bfloat16)).astype(jnp.float32)

@jax.custom_vjp
def low_back(v):
    return v

def low_keep(v):
    return (low(v), None)

def low_pass(kept, grad):
    return (grad,)

def back_keep(v):
    return (v, None)

def back_low(kept, grad):
    return (low(grad),)
low.defvjp(low_keep, low_pass)
low_back.defvjp(back_keep, back_low)
log_two = math.log(2.0)
highest = lax.Precision.HIGHEST

def shifted(value):
    return jax.nn.softplus(value) - log_two

def residual_block(values, tangents, weight_in, bias_in, weight_out, bias_out):
    pre_act = low_back(jnp.dot(low(values), weight_in, precision=highest) + bias_in)
    linear = low_back(jnp.einsum('jrd,dh->jrh', low(tangents), weight_in, precision=highest))
    slopes = jax.nn.sigmoid(pre_act)
    branch = low_back(jnp.dot(low(shifted(pre_act)), weight_out, precision=highest))
    carried = low_back(jnp.einsum('jrh,hd->jrd', low(slopes[None] * linear), weight_out, precision=highest))
    return (values + branch + bias_out, tangents + carried)

def forward(weight_in, bias_in, weight_out, bias_out, values, tangents, live_rows):
    for block_id in range(2):
        values, tangents = residual_block(values, tangents, weight_in[block_id], bias_in[block_id], weight_out[block_id], bias_out[block_id])
    return (values * live_rows[:, None], tangents * live_rows[None, :, None])

def reference(features, tangents, weight_in, bias_in, weight_out, bias_out, true_counts, cotangent_values, cotangent_tangents):
    live_rows = (jnp.arange(SLOT, dtype=jnp.int32)[None, :] < true_counts[:, None]).reshape(-1).astype(jnp.float32)
    params = (weight_in.astype(jnp.float32), bias_in, weight_out.astype(jnp.float32), bias_out)
    group_rows = math.gcd(ROWS, 4096)
    groups = ROWS // group_rows
    value_groups = features.astype(jnp.float32).reshape(groups, group_rows, D)
    tangent_groups = jnp.transpose(tangents.astype(jnp.float32).reshape(3, groups, group_rows, D), (1, 0, 2, 3))
    live_groups = live_rows.reshape(groups, group_rows)
    cot_value_groups = cotangent_values.astype(jnp.float32).reshape(groups, group_rows, D)
    cot_tangent_groups = jnp.transpose(cotangent_tangents.astype(jnp.float32).reshape(3, groups, group_rows, D), (1, 0, 2, 3))

    def step(totals, pieces):
        vals, tans, live, cot_vals, cot_tans = pieces
        outputs, pullback = jax.vjp(lambda a, b, c, d, e, f: forward(a, b, c, d, e, f, live), *params, vals, tans)
        grads = pullback((cot_vals, cot_tans))
        totals = tuple((total + grad_piece for total, grad_piece in zip(totals, grads[:4])))
        return (totals, (outputs[0], outputs[1], grads[4], grads[5]))
    zeros = tuple((jnp.zeros_like(item) for item in params))
    totals, (out_vals, out_tans, grad_vals, grad_tans) = lax.scan(step, zeros, (value_groups, tangent_groups, live_groups, cot_value_groups, cot_tangent_groups))
    values_out = out_vals.reshape(ROWS, D).astype(jnp.bfloat16)
    tangents_out = jnp.transpose(out_tans, (1, 0, 2, 3)).reshape(3, ROWS, D).astype(jnp.bfloat16)
    values_grad = grad_vals.reshape(ROWS, D).astype(jnp.bfloat16)
    tangents_grad = jnp.transpose(grad_tans, (1, 0, 2, 3)).reshape(3, ROWS, D).astype(jnp.bfloat16)
    return (values_out, tangents_out, values_grad, tangents_grad, totals[0], totals[1], totals[2], totals[3])
```

```python
import functools
import math

import jax
import jax.numpy as jnp
from jax import lax
from jax.experimental import pallas as pl
from jax.experimental.pallas import tpu as pltpu
from jax.sharding import PartitionSpec as P

LOG_TWO = math.log(2.0)
GROUP = 16
BF16, F32 = jnp.bfloat16, jnp.float32
ANY = pl.BlockSpec(memory_space=pl.ANY)
ON_CHIP = pl.BlockSpec(memory_space=pltpu.VMEM)
MIB = 1 << 20


def aligned(value):
    return pl.multiple_of(value, GROUP)


def make_table(counts, side):
    padded = (counts + GROUP - 1) // GROUP * GROUP
    starts = jnp.cumsum(padded) - padded
    table = jnp.concatenate([starts, padded, counts, side[None]]).astype(jnp.int32)
    return table, jnp.sum(padded)


def run_of(table, sources, slot, source, low, rows):
    start, padded = table[source], table[sources + source]
    first = jnp.maximum(start, low)
    size = jnp.maximum(jnp.minimum(start + padded, low + rows) - first, 0)
    return aligned(source * slot + first - start), aligned(first - low), aligned(size)


def each_run(table, sources, slot, low, rows, visit):
    def step(source, carry):
        row, place, size = run_of(table, sources, slot, source, low, rows)

        @pl.when(size > 0)
        def _():
            visit(source, row, place, size)

        return carry

    lax.fori_loop(0, sources, step, 0)


def start_and_wait(moves):
    for wait in (False, True):
        for table, sources, slot, low, rows, copies in moves:

            def visit(source, row, place, size, copies=copies):
                for copy in copies(source, row, place, size):
                    copy.wait() if wait else copy.start()

            each_run(table, sources, slot, low, rows, visit)


def pack_kernel(sources, slot, base, rows, table, values, tangents, keep, send, sems):
    side = table[3 * sources]

    def move(which, target, low):
        def copies(source, row, place, size):
            return (
                pltpu.make_async_copy(
                    values.at[pl.ds(row, size)], target.at[0, pl.ds(place, size)], sems.at[which, 0, source]
                ),
                pltpu.make_async_copy(
                    tangents.at[:, pl.ds(row, size)],
                    target.at[pl.ds(1, 3), pl.ds(place, size)],
                    sems.at[which, 1, source],
                ),
            )

        return (table, sources, slot, low, rows, copies)

    start_and_wait(
        [move(0, send, base + (1 - side) * rows), move(1, keep, base + side * rows)]
    )


def pack(table, values, tangents, base, rows, sources):
    half = values.shape[1]
    shape = jax.ShapeDtypeStruct((4, rows, half), BF16)
    return pl.pallas_call(
        functools.partial(pack_kernel, sources, values.shape[0] // sources, base, rows),
        out_shape=(shape, shape),
        in_specs=[pl.BlockSpec(memory_space=pltpu.SMEM), ANY, ANY],
        out_specs=(ON_CHIP, ON_CHIP),
        scratch_shapes=[pltpu.SemaphoreType.DMA((2, 2, sources))],
        cost_estimate=pl.CostEstimate(flops=0, bytes_accessed=32 * rows * half, transcendentals=0),
        compiler_params=pltpu.CompilerParams(vmem_limit_bytes=40 * MIB),
        name="pack",
    )(table, values, tangents)


def unpack_kernel(sources, slot, base, rows, table, mine, theirs, _v, _t, values, tangents, sems):
    side = table[3 * sources]

    def move(which, origin, low):
        def copies(source, row, place, size):
            return (
                pltpu.make_async_copy(
                    origin.at[0, pl.ds(place, size)], values.at[pl.ds(row, size)], sems.at[which, 0, source]
                ),
                pltpu.make_async_copy(
                    origin.at[pl.ds(1, 3), pl.ds(place, size)],
                    tangents.at[:, pl.ds(row, size)],
                    sems.at[which, 1, source],
                ),
            )

        return (table, sources, slot, low, rows, copies)

    start_and_wait(
        [move(0, theirs, base + (1 - side) * rows), move(1, mine, base + side * rows)]
    )


def unpack(table, mine, theirs, values, tangents, base, rows, sources):
    half = values.shape[1]
    return pl.pallas_call(
        functools.partial(unpack_kernel, sources, values.shape[0] // sources, base, rows),
        out_shape=(
            jax.ShapeDtypeStruct(values.shape, BF16),
            jax.ShapeDtypeStruct(tangents.shape, BF16),
        ),
        in_specs=[pl.BlockSpec(memory_space=pltpu.SMEM), ON_CHIP, ON_CHIP, ANY, ANY],
        out_specs=(ANY, ANY),
        input_output_aliases={3: 0, 4: 1},
        scratch_shapes=[pltpu.SemaphoreType.DMA((2, 2, sources))],
        cost_estimate=pl.CostEstimate(flops=0, bytes_accessed=32 * rows * half, transcendentals=0),
        compiler_params=pltpu.CompilerParams(vmem_limit_bytes=40 * MIB),
        name="unpack",
    )(table, mine, theirs, values, tangents)


def blank_kernel(sources, slot, table, values, tangents, other_values, other_tangents, zeros, sems):
    zeros[...] = jnp.zeros_like(zeros)

    for wait in (False, True):

        def step(source, carry, wait=wait):
            padded = table[sources + source]
            size = aligned(slot - padded)
            row = aligned(source * slot + padded)

            @pl.when(size > 0)
            def _():
                for place, (low, high) in enumerate(
                    ((values, tangents), (other_values, other_tangents))
                ):
                    for copy in (
                        pltpu.make_async_copy(
                            zeros.at[0, pl.ds(0, size)], low.at[pl.ds(row, size)], sems.at[place, 0, source]
                        ),
                        pltpu.make_async_copy(
                            zeros.at[:, pl.ds(0, size)], high.at[:, pl.ds(row, size)], sems.at[place, 1, source]
                        ),
                    ):
                        copy.wait() if wait else copy.start()

            return carry

        lax.fori_loop(0, sources, step, 0)


def blank(table, row_count, half, sources):
    slot = row_count // sources
    values = jax.ShapeDtypeStruct((row_count, half), BF16)
    tangents = jax.ShapeDtypeStruct((3, row_count, half), BF16)
    return pl.pallas_call(
        functools.partial(blank_kernel, sources, slot),
        out_shape=(values, tangents, values, tangents),
        in_specs=[pl.BlockSpec(memory_space=pltpu.SMEM)],
        out_specs=(ANY, ANY, ANY, ANY),
        scratch_shapes=[
            pltpu.VMEM((3, slot, half), BF16),
            pltpu.SemaphoreType.DMA((2, 2, sources)),
        ],
        cost_estimate=pl.CostEstimate(flops=0, bytes_accessed=8 * row_count * half, transcendentals=0),
        name="blank",
    )(table)


NN = (((1,), (0,)), ((), ()))
TN = (((0,), (0,)), ((), ()))


def dot(a, b, dims=NN):
    return lax.dot_general(a, b, dims, preferred_element_type=F32)


def blocks_kernel(
    sources,
    base,
    rows,
    tile,
    first,
    table,
    x_own,
    x_got,
    g_own,
    g_got,
    w_in,
    w_out,
    w_in_t,
    w_out_t,
    b_in,
    b_out,
    *rest,
):
    if first:
        grads_before = bias_before = None
    else:
        grads_before, bias_before, *rest = rest
    (y_own, y_send, d_own, d_send, grads, biases, x_low, acts, slopes, lin) = rest
    step = pl.program_id(0)
    side = table[3 * sources]
    wide = w_in.shape[1]
    half = wide // 2
    flat = 4 * tile

    @pl.when(step == 0)
    def _():
        if first:
            grads[...] = jnp.zeros_like(grads)
            biases[...] = jnp.zeros_like(biases)
        else:
            grads[...] = grads_before[...]
            biases[...] = bias_before[...]

    packed = base + side * rows + step * tile + lax.broadcasted_iota(jnp.int32, (tile, 128), 0)
    live = jnp.zeros((tile, 128), F32)
    for source in range(sources):
        start, count = table[source], table[2 * sources + source]
        live = jnp.where((packed >= start) & (packed < start + count), 1.0, live)
    live = jnp.concatenate([live] * (wide // 128), axis=1)
    is_live = live > 0.0

    def load(own, got, stream):
        own, got = own[stream].astype(F32), got[stream].astype(F32)
        left = jnp.where(side == 0, own, got)
        right = jnp.where(side == 0, got, own)
        return jnp.where(is_live, jnp.concatenate([left, right], axis=1), 0.0)

    def store(own, send, stream, value):
        left, right = value[:, :half].astype(BF16), value[:, half:].astype(BF16)
        own[stream] = jnp.where(side == 0, left, right)
        send[stream] = jnp.where(side == 0, right, left)

    def add_grad(place, value):
        rows_in = value.shape[0]
        for part in range(2):
            grads[part, place : place + rows_in, :] += value[:, part * half : (part + 1) * half]

    def add_bias(place, value):
        biases[place] += jnp.sum(value.reshape(tile // 8, 8, wide), axis=0)

    x = [load(x_own, x_got, stream) for stream in range(4)]
    for block in range(2):
        for stream in range(4):
            x_low[block, stream * tile : (stream + 1) * tile] = x[stream].astype(BF16)
        pre = dot(x_low[block], w_in[block])
        z = pre[:tile] + b_in[block][None, :]
        small = jnp.exp(-jnp.abs(z))
        whole = 1.0 / (1.0 + small)
        slope = jnp.where(z >= 0.0, whole, small * whole)
        slopes[block] = slope
        acts[block, :tile] = (jnp.maximum(z, 0.0) + jnp.log1p(small) - LOG_TWO).astype(BF16)
        for stream in range(1, 4):
            part = pre[stream * tile : (stream + 1) * tile]
            lin[block, stream - 1] = part
            acts[block, stream * tile : (stream + 1) * tile] = (slope * part).astype(BF16)
        out = dot(acts[block], w_out[block])
        x = [x[stream] + out[stream * tile : (stream + 1) * tile] for stream in range(4)]
        x[0] = x[0] + b_out[block][None, :]
    for stream in range(4):
        store(y_own, y_send, stream, x[stream] * live)

    g = [load(g_own, g_got, stream) for stream in range(4)]
    for block in (1, 0):
        add_bias(2 + block, g[0])
        g_low = jnp.concatenate([part.astype(BF16) for part in g], axis=0)
        value = dot(acts[block], g_low, TN)
        for part in range(2):
            place = 2 * wide + block * wide + part * half
            grads[0, place : place + half, :] += value[:half, part * half : (part + 1) * half]
            grads[1, place : place + half, :] += value[half:, part * half : (part + 1) * half]
        mixed = dot(g_low, w_out_t[block])
        slope = slopes[block]
        total = jnp.zeros((tile, wide), F32)
        lower = []
        for stream in range(1, 4):
            part = mixed[stream * tile : (stream + 1) * tile]
            total = total + part * lin[block, stream - 1]
            lower.append((part * slope).astype(BF16))
        g_pre = (mixed[:tile] * slope + slope * (1.0 - slope) * total).astype(BF16)
        add_bias(block, g_pre.astype(F32))
        stack = jnp.concatenate([g_pre] + lower, axis=0)
        add_grad(block * wide, dot(x_low[block], stack, TN))
        back = dot(stack, w_in_t[block])
        g = [g[stream] + back[stream * tile : (stream + 1) * tile] for stream in range(4)]
    for stream in range(4):
        store(d_own, d_send, stream, g[stream])


def tile_of(rows):
    best = GROUP
    for tile in range(GROUP, 161, GROUP):
        if rows % tile == 0:
            best = tile
    return best


def run_blocks(table, x_own, x_got, g_own, g_got, weights, biases, sums, base, sources):
    rows, half = x_own.shape[1:]
    wide = 2 * half
    tile = tile_of(rows)
    first = sums is None
    piece = pl.BlockSpec((4, tile, half), lambda i: (0, i, 0))

    def whole(array):
        return pl.BlockSpec(
            array.shape, lambda i, rank=len(array.shape): (0,) * rank, pipeline_mode=pl.Buffered(1)
        )

    sum_shapes = (
        jax.ShapeDtypeStruct((2, 4 * wide, half), F32),
        jax.ShapeDtypeStruct((4, 8, wide), F32),
    )
    out_piece = jax.ShapeDtypeStruct((4, rows, half), BF16)
    extra = () if first else sums
    operands = (table, x_own, x_got, g_own, g_got, *weights, *biases, *extra)
    return pl.pallas_call(
        functools.partial(blocks_kernel, sources, base, rows, tile, first),
        grid=(rows // tile,),
        out_shape=(out_piece,) * 4 + sum_shapes,
        in_specs=[pl.BlockSpec(memory_space=pltpu.SMEM)]
        + [piece] * 4
        + [whole(item) for item in operands[5:]],
        out_specs=[piece] * 4 + [whole(item) for item in sum_shapes],
        input_output_aliases={} if first else {len(operands) - 2: 4, len(operands) - 1: 5},
        scratch_shapes=[
            pltpu.VMEM((2, 4 * tile, wide), BF16),
            pltpu.VMEM((2, 4 * tile, wide), BF16),
            pltpu.VMEM((2, tile, wide), F32),
            pltpu.VMEM((2, 3, tile, wide), F32),
        ],
        cost_estimate=pl.CostEstimate(
            flops=12 * 2 * 4 * rows * wide * wide,
            bytes_accessed=16 * 2 * rows * wide + 16 * wide * wide,
            transcendentals=4 * rows * wide,
        ),
        compiler_params=pltpu.CompilerParams(vmem_limit_bytes=56 * MIB),
        name="blocks",
    )(*operands)


def swap_tensor(value):
    return lax.ppermute(value, "tensor", [(0, 1), (1, 0)])


def swap_bit(value, bit, size):
    return lax.ppermute(value, "dp", [(i, i ^ (1 << bit)) for i in range(size)])


def in_order(flag, mine, other, axis):
    return jnp.where(
        flag == 0, jnp.concatenate([mine, other], axis), jnp.concatenate([other, mine], axis)
    )


def partner_weights_start(weight_in, weight_out, place, size):
    half = weight_in.shape[2]
    flat = jnp.concatenate([weight_in.reshape(-1, half), weight_out.reshape(-1, half)], 0)
    rows = flat.shape[0] // 4
    quarter = (place & 1) * 2 + ((place >> 1) & 1)
    return swap_tensor(lax.dynamic_slice_in_dim(flat, quarter * rows, rows, 0))


def partner_weights_finish(piece, weight_in, weight_out, place, size):
    piece = in_order((place >> 1) & 1, piece, swap_bit(piece, 1, size), 0)
    piece = in_order(place & 1, piece, swap_bit(piece, 0, size), 0)
    rows = weight_in.shape[0] * weight_in.shape[1]
    return piece[:rows].reshape(weight_in.shape), piece[rows:].reshape(weight_out.shape)


def reduce_over_dp(grads, place, size):
    for bit in range(size.bit_length() - 1):
        flag = (place >> bit) & 1
        rows = grads.shape[1] // 2
        kept = lax.dynamic_slice_in_dim(grads, flag * rows, rows, 1)
        sent = lax.dynamic_slice_in_dim(grads, (1 - flag) * rows, rows, 1)
        if bit > 0:
            sent = sent.astype(BF16)
        grads = kept + swap_bit(sent, bit, size).astype(F32)
    return grads


def gather_over_dp(total, place, size):
    for bit in reversed(range(size.bit_length() - 1)):
        total = in_order((place >> bit) & 1, total, swap_bit(total, bit, size), 0)
    return total


def bias_rows(biases, half, size):
    flat = jnp.swapaxes(jnp.sum(biases, 1).reshape(4, 2, half), 0, 1)
    return jnp.pad(flat, ((0, 0), (0, 8 * size - 4), (0, 0)))


def local(
    dp_size,
    features,
    tangents,
    weight_in,
    bias_in,
    weight_out,
    bias_out,
    true_counts,
    cotangent_values,
    cotangent_tangents,
):
    row_count, half = features.shape
    sources = true_counts.shape[0]
    side = lax.axis_index("tensor")
    place = lax.axis_index("dp")
    table, packed_rows = make_table(true_counts, side)
    most = lax.pmax(packed_rows, "dp")
    quarter = partner_weights_start(weight_in, weight_out, place, dp_size)
    bias_pair = jnp.stack([bias_in, bias_out])
    bias_got = swap_tensor(bias_pair)
    unit = row_count // 32
    levels = [unit * k for k in LEVELS]

    def at_level(level):
        first = min(level, (level * 5 // 8 + 127) // 128 * 128)
        chunks = [(0, first)]
        if first < level:
            chunks.append((2 * first, level - first))

        def branch(
            table,
            features,
            tangents,
            weight_in,
            weight_out,
            cotangent_values,
            cotangent_tangents,
            quarter,
            bias_pair,
            bias_got,
        ):
            got_in, got_out = partner_weights_finish(quarter, weight_in, weight_out, place, dp_size)
            w_in = in_order(side, weight_in, got_in, 2)
            w_out = in_order(side, weight_out, got_out, 1)
            weights = (w_in, w_out, jnp.swapaxes(w_in, 1, 2), jnp.swapaxes(w_out, 1, 2))
            b_in, b_out = in_order(side, bias_pair, bias_got, 2)
            outs = blank(table, row_count, half, sources)
            arrived = []
            for base, rows in chunks:
                x_own, x_send = pack(table, features, tangents, base, rows, sources)
                if base > 0:
                    x_send, outs = lax.optimization_barrier((x_send, outs))
                x_got = swap_tensor(x_send)
                g_own, g_send = pack(
                    table, cotangent_values, cotangent_tangents, base, rows, sources
                )
                arrived.append((base, rows, x_own, x_got, g_own, swap_tensor(g_send)))
            sums = None
            results = []
            for base, rows, x_own, x_got, g_own, g_got in arrived:
                y_own, y_send, d_own, d_send, *sums = run_blocks(
                    table, x_own, x_got, g_own, g_got, weights, (b_in, b_out), sums, base, sources
                )
                results.append((base, rows, y_own, y_send, d_own, d_send))
            grads, biases = sums
            grads = jnp.concatenate([grads, bias_rows(biases, half, dp_size)], 1)
            grads = reduce_over_dp(grads, place, dp_size)
            mine = lax.dynamic_index_in_dim(grads, side, 0, keepdims=False)
            other = lax.dynamic_index_in_dim(grads, 1 - side, 0, keepdims=False).astype(BF16)
            values, slants, values_grad, slants_grad = outs
            for base, rows, y_own, y_send, d_own, d_send in results:
                if base > 0 or len(chunks) == 1:
                    other, y_send, d_send = lax.optimization_barrier((other, y_send, d_send))
                y_got = swap_tensor(y_send)
                d_got = swap_tensor(d_send)
                values, slants = unpack(table, y_own, y_got, values, slants, base, rows, sources)
                values_grad, slants_grad = unpack(
                    table, d_own, d_got, values_grad, slants_grad, base, rows, sources
                )
            total = (mine + swap_tensor(other).astype(F32)).astype(BF16)
            total = gather_over_dp(total, place, dp_size)
            return values, slants, values_grad, slants_grad, total

        return branch

    index = sum((most > 2 * level).astype(jnp.int32) for level in levels[:-1])
    values, slants, values_grad, slants_grad, total = lax.switch(
        index,
        [at_level(level) for level in levels],
        table,
        features,
        tangents,
        weight_in,
        weight_out,
        cotangent_values,
        cotangent_tangents,
        quarter,
        bias_pair,
        bias_got,
    )
    wide = 2 * half
    total = total.astype(F32)
    grad_in = total[: 2 * wide].reshape(2, wide, half)
    grad_out = (
        total[2 * wide : 4 * wide].reshape(2, 2, half, half).transpose(0, 2, 1, 3).reshape(2, half, wide)
    )
    bias_in_grad = total[4 * wide : 4 * wide + 2]
    bias_out_grad = total[4 * wide + 2 : 4 * wide + 4]
    return (
        values,
        slants,
        values_grad,
        slants_grad,
        grad_in,
        bias_in_grad,
        grad_out,
        bias_out_grad,
    )


LEVELS = (6, 10, 11, 12, 13, 16)


def solution(mesh):
    in_specs = (
        P("dp", "tensor"),
        P(None, "dp", "tensor"),
        P(None, None, "tensor"),
        P(None, "tensor"),
        P(None, "tensor", None),
        P(None, "tensor"),
        P("dp"),
        P("dp", "tensor"),
        P(None, "dp", "tensor"),
    )
    out_specs = (
        P("dp", "tensor"),
        P(None, "dp", "tensor"),
        P("dp", "tensor"),
        P(None, "dp", "tensor"),
        P(None, None, "tensor"),
        P(None, "tensor"),
        P(None, "tensor", None),
        P(None, "tensor"),
    )
    return jax.shard_map(
        functools.partial(local, mesh.shape["dp"]),
        mesh=mesh,
        in_specs=in_specs,
        out_specs=out_specs,
        check_vma=False,
    )
```

```python
import functools
import math

import jax
import jax.numpy as jnp
import numpy as np
from jax import lax
from jax.experimental import pallas as pl
from jax.experimental.pallas import tpu as pltpu
from jax.sharding import PartitionSpec as P

LOG_TWO = math.log(2.0)
GROUP = 16
BF16, F32 = jnp.bfloat16, jnp.float32
SCALARS = pl.BlockSpec(memory_space=pltpu.SMEM)
HBM = pl.BlockSpec(memory_space=pltpu.HBM)
MIB = 1 << 20

ROWS, FIRST, MOVED, EXTRA = 80, 36, 28, 8
OVER = -1

PLACE, SIDE, TOTAL, QUARTER, TAILS = range(5)
ROUNDS, OUT_LEFT, IN_LEFT, OUT_RIGHT, IN_RIGHT, KEPT, OVER_FIRST, OVER_LEFT = range(8)


def aligned(value):
    return pl.multiple_of(value, GROUP)


def round_up(count):
    return (count + GROUP - 1) // GROUP * GROUP


NO_COST = pl.CostEstimate(flops=0, bytes_accessed=1024, transcendentals=0)
COST_PER_ROW = 7 * 10**7


PARAMS = pltpu.CompilerParams(vmem_limit_bytes=60 * MIB)


def chain_order(size):
    around = (0, 1, 3, 2)
    order = []
    for block in range(size // 4):
        order += [4 * block + i for i in (around if block % 2 == 0 else around[::-1])]
    return order


def plan_kernel(order, most, early, moved, extra, who, totals, plan, flows):
    size = len(order)

    def most_out(total):
        return jnp.clip((total - early) // 2 // GROUP * GROUP, 0, moved)

    def total_of(i):
        return totals[order[i]]

    flow, rounds = jnp.int32(0), jnp.int32(0)
    flows[0] = flow
    for i in range(size):
        here = total_of(i) + flow
        if i + 1 < size:
            flow = jnp.clip(here - most, -most_out(total_of(i + 1)), most_out(total_of(i)))
        else:
            flow = jnp.int32(0)
        flows[i + 1] = flow
        over = jnp.maximum(here - flow - most, 0)
        rounds = jnp.maximum(rounds, (over + extra - 1) // extra)
    place = who[PLACE]
    left, right, total = flows[place], flows[place + 1], who[TOTAL]
    out_left, out_right = jnp.maximum(-left, 0), jnp.maximum(right, 0)
    over = jnp.maximum(total + left - right - most, 0)
    kept = total - out_left - out_right - over
    plan[ROUNDS] = rounds
    plan[OUT_LEFT] = out_left
    plan[IN_LEFT] = jnp.maximum(left, 0)
    plan[OUT_RIGHT] = out_right
    plan[IN_RIGHT] = jnp.maximum(-right, 0)
    plan[KEPT] = kept
    plan[OVER_FIRST] = kept
    plan[OVER_LEFT] = over


def make_plan(who, totals, order, level, early, moved, extra):
    return pl.pallas_call(
        functools.partial(plan_kernel, order, 2 * level, early, moved, 2 * extra),
        out_shape=jax.ShapeDtypeStruct((8,), jnp.int32),
        in_specs=[SCALARS] * 2,
        out_specs=SCALARS,
        scratch_shapes=[pltpu.SMEM((len(order) + 1,), jnp.int32)],
        cost_estimate=NO_COST,
        name="plan",
    )(who, totals)


def own_piece(limit, plan, base, rows):
    if base == OVER:
        first, size = plan[OVER_FIRST], jnp.clip(plan[OVER_LEFT], 0, 2 * rows)
    else:
        first, size = jnp.int32(base), jnp.clip(limit - base, 0, 2 * rows)
    return first, first + size, size


def moved_pieces(dims, plan, base, rows):
    top = 2 * dims[2] - base
    left, right = plan[IN_LEFT], plan[IN_RIGHT]
    return (aligned(top - left - right), aligned(left)), (aligned(top - right), aligned(right))


def sent_pieces(who, plan):
    left, right, total = plan[OUT_LEFT], plan[OUT_RIGHT], who[TOTAL]
    return (total - right - left, total - right, left), (total - right, total, right)


def whole_groups(count):
    return count // GROUP * GROUP


def each_run(dims, who, counts, piece, visit):
    sources, slot = dims[:2]
    first, end = piece[:2]

    def step(source, start):
        after = start + whole_groups(counts[source])
        begin = jnp.maximum(start, first)
        stop = jnp.minimum(after, end)

        @pl.when(stop > begin)
        def _():
            row = source * slot + begin - start
            visit(aligned(row), aligned(begin - first), aligned(stop - begin))

        return after

    lax.fori_loop(0, sources, step, who[TAILS])


def copies_between(held, streams, place, values, tangents, row, size):
    return (
        (values.at[pl.ds(row, size)], held.at[streams, pl.ds(place, size)]),
        (tangents.at[:, pl.ds(row, size)], held.at[pl.ds(streams + 1, 3), pl.ds(place, size)]),
    )


def wait_for(held, streams, size, sem):
    @pl.when(size > 0)
    def _():
        part = held.at[streams, pl.ds(0, aligned(size))]
        pltpu.make_async_copy(part, part, sem).wait()


def each_tail(dims, counts, visit):
    sources, slot = dims[:2]

    def step(source, found):
        left = counts[source] % GROUP
        row = source * slot + jnp.minimum(whole_groups(counts[source]), slot - GROUP)
        visit(source, aligned(row), left)
        return found + jnp.minimum(left, 1)

    return lax.fori_loop(0, sources, step, jnp.int32(0))


def tail_matrix(dims, counts):
    wide = dims[0] * GROUP
    lane = lax.broadcasted_iota(jnp.int32, (8, wide), 1)
    target = jnp.full((8, wide), -1, jnp.int32)
    start = jnp.int32(0)
    for source in range(dims[0]):
        left = counts[source] % GROUP
        row = lane - source * GROUP
        target = jnp.where((row >= 0) & (row < left), start + row, target)
        start = start + left
    number = lax.broadcasted_iota(jnp.int32, (wide, wide), 0)
    return jnp.where(number == target[:1], 1.0, 0.0).astype(BF16)


def make_who(dims, counts, who):
    place = lax.axis_index("dp")
    around = (place & 3) ^ ((place & 3) >> 1)
    back = (place >> 2) & 1
    who[PLACE] = (place >> 2) * 4 + around * (1 - back) + (3 - around) * back
    who[SIDE] = lax.axis_index("tensor")
    who[QUARTER] = my_quarter()

    def step(source, carry):
        whole, left = carry
        return whole + whole_groups(counts[source]), left + counts[source] % GROUP

    whole, left = lax.fori_loop(0, dims[0], step, (jnp.int32(0), jnp.int32(0)))
    left = (left + GROUP - 1) // GROUP * GROUP
    who[TOTAL] = whole + left
    who[TAILS] = left


def start_copies(held, place, sources, row, size, sem):
    for streams, (values, tangents) in zip((0, 4), sources):
        for copy in copies_between(held, streams, place, values, tangents, row, size):
            pltpu.make_async_copy(*copy, sem).start()


def pack_kernel(dims, base, rows, moving, who, counts, *refs):
    plan = None
    if moving or base == OVER:
        plan, *refs = refs
    sources, refs = (refs[:2], refs[2:4]), refs[4:]
    neighbours = ()
    if moving:
        neighbours, refs = refs[:2], refs[2:]
    keep, send, held, sems, *tails = refs
    side = who[SIDE]
    piece = own_piece(plan[KEPT] if moving else who[TOTAL], plan, base, rows)
    size = piece[2]

    if base == 0:
        ends, packed = tails

        def start_tail(source, row, left):
            start_copies(ends, aligned(source * GROUP), sources, row, GROUP, sems.at[1])

        each_tail(dims, counts, start_tail)
        size = size - who[TAILS]

    def start(row, place, size):
        start_copies(held, place, sources, row, size, sems.at[0])

    each_run(dims, who, counts, piece, start)
    arrivals = []
    if moving:
        pieces = moved_pieces(dims, plan, base, rows)
        for number, neighbour in enumerate(neighbours):
            place, moved = pieces[number]
            copy = pltpu.make_async_copy(
                neighbour.at[:, pl.ds(0, moved)], held.at[:, pl.ds(place, moved)], sems.at[1 + number]
            )
            arrivals.append((moved, copy))
        for moved, copy in arrivals:
            pl.when(moved > 0)(copy.start)
    if base == 0:
        matrix = tail_matrix(dims, counts)
        wait_for(ends, slice(0, 8), jnp.int32(dims[0] * GROUP), sems.at[1])
        for stream in range(8):
            packed[stream] = dot(matrix, ends[stream]).astype(BF16)

        def put(group, carry):
            here = pl.ds(aligned(group * GROUP), GROUP)
            held[:, here, :] = packed[:, here, :]
            return carry

        lax.fori_loop(0, who[TAILS] // GROUP, put, 0)
    wait_for(held, slice(0, 8), size, sems.at[0])
    for moved, copy in arrivals:
        pl.when(moved > 0)(copy.wait)
    out = [
        pltpu.make_async_copy(
            held.at[:, pl.ds(aligned(part * rows), rows)], target, sems.at[5 + number]
        )
        for number, (part, target) in enumerate(((1 - side, send), (side, keep)))
    ]
    for copy in out:
        copy.start()
    for copy in out:
        copy.wait()


def pack(dims, who, counts, plan, arrays, base, rows, neighbours=()):
    half = arrays[0].shape[1]
    shape = jax.ShapeDtypeStruct((8, rows, half), BF16)
    plans = (plan,) if neighbours or base == OVER else ()
    tails = [pltpu.VMEM((8, dims[0] * GROUP, half), BF16)] * 2 if base == 0 else []
    return pl.pallas_call(
        functools.partial(pack_kernel, dims, base, rows, len(neighbours) > 0),
        out_shape=(shape, shape),
        in_specs=[SCALARS] * (2 + len(plans)) + [HBM] * (4 + len(neighbours)),
        out_specs=(HBM, HBM),
        scratch_shapes=[pltpu.VMEM((8, 2 * rows, half), BF16), pltpu.SemaphoreType.DMA((7,))] + tails,
        cost_estimate=NO_COST,
        compiler_params=PARAMS,
        name="pack",
    )(who, counts, *plans, *arrays, *neighbours)


def export_kernel(dims, moved, who, counts, plan, x, x3, g, g3, *refs):
    targets, (held, sems) = refs[:2], refs[2:]
    pieces = sent_pieces(who, plan)
    for number, piece in enumerate(pieces):

        def start(row, place, size, number=number):
            place = aligned(number * moved + place)
            start_copies(held, place, ((x, x3), (g, g3)), row, size, sems.at[number])

        @pl.when(piece[2] > 0)
        def _(piece=piece, start=start):
            each_run(dims, who, counts, piece, start)

    for number, piece in enumerate(pieces):
        wait_for(held, slice(0, 8), piece[2], sems.at[number])
    out = [
        pltpu.make_async_copy(
            held.at[:, pl.ds(number * moved, moved)], target, sems.at[2 + number]
        )
        for number, target in enumerate(targets)
    ]
    for copy in out:
        copy.start()
    for copy in out:
        copy.wait()


def export(dims, who, counts, plan, x, x3, g, g3, moved):
    half = x.shape[1]
    return pl.pallas_call(
        functools.partial(export_kernel, dims, moved),
        out_shape=(jax.ShapeDtypeStruct((8, moved, half), BF16),) * 2,
        in_specs=[SCALARS] * 3 + [HBM] * 4,
        out_specs=(HBM,) * 2,
        scratch_shapes=[pltpu.VMEM((8, 2 * moved, half), BF16), pltpu.SemaphoreType.DMA((4,))],
        cost_estimate=NO_COST,
        compiler_params=PARAMS,
        name="export",
    )(who, counts, plan, x, x3, g, g3)


def load_results(held, rows, side, mine, theirs, sems):
    loads = [
        pltpu.make_async_copy(
            origin, held.at[:, pl.ds(aligned(part * rows), rows)], sems.at[number]
        )
        for number, (part, origin) in enumerate(((1 - side, theirs), (side, mine)))
    ]
    for load in loads:
        load.start()
    for load in loads:
        load.wait()


def handback_kernel(dims, base, rows, who, plan, mine, theirs, to_left, to_right, held, sems):
    load_results(held, rows, who[SIDE], mine, theirs, sems)
    copies = []
    pieces = moved_pieces(dims, plan, base, rows)
    for number, ((place, size), target) in enumerate(zip(pieces, (to_left, to_right))):
        copy = pltpu.make_async_copy(
            held.at[:, pl.ds(place, size)], target.at[:, pl.ds(0, size)], sems.at[2 + number]
        )
        copies.append((size, copy))
    for size, copy in copies:
        pl.when(size > 0)(copy.start)
    for size, copy in copies:
        pl.when(size > 0)(copy.wait)


def handback(dims, who, plan, mine, theirs, base, rows, moved):
    half = mine.shape[2]
    shape = jax.ShapeDtypeStruct((4, moved, half), BF16)
    return pl.pallas_call(
        functools.partial(handback_kernel, dims, base, rows),
        out_shape=(shape, shape),
        in_specs=[SCALARS] * 2 + [HBM] * 2,
        out_specs=(HBM, HBM),
        scratch_shapes=[pltpu.VMEM((4, 2 * rows, half), BF16), pltpu.SemaphoreType.DMA((4,))],
        cost_estimate=NO_COST,
        compiler_params=PARAMS,
        name="handback",
    )(who, plan, mine, theirs)


def unpack_kernel(dims, base, rows, streams, who, counts, plan, *refs):
    pairs = streams // 4
    mine, theirs, refs = refs[:pairs], refs[pairs], refs[pairs + 1 :]
    outs, (held, sems, *tails) = refs[2 * pairs : 4 * pairs], refs[4 * pairs :]
    side = 1 if base is None else who[SIDE]
    loads = [(pl.ds(0, streams), 1 - side, theirs)]
    loads += [(pl.ds(4 * number, 4), side, part) for number, part in enumerate(mine)]
    loads = [
        pltpu.make_async_copy(
            origin, held.at[where, pl.ds(aligned(part * rows), rows)], sems.at[number]
        )
        for number, (where, part, origin) in enumerate(loads)
    ]
    for load in loads:
        load.start()
    for load in loads:
        load.wait()
    pieces = sent_pieces(who, plan)
    if base is not None:
        pieces = (own_piece(plan[KEPT], plan, base, rows),)
    sizes = [piece[2] for piece in pieces]
    if base == 0:
        sizes = [sizes[0] - who[TAILS]]

    def start_out(origin, place, row, size, sem):
        for number in range(pairs):
            copies = copies_between(
                origin, 4 * number, place, outs[2 * number], outs[2 * number + 1], row, size
            )
            for there, here in copies:
                pltpu.make_async_copy(here, there, sem).start()

    for number, piece in enumerate(pieces):

        def start(row, place, size, number=number):
            start_out(held, aligned(number * rows + place), row, size, sems.at[3 + number])

        @pl.when(piece[2] > 0)
        def _(piece=piece, start=start):
            each_run(dims, who, counts, piece, start)

    if base == 0:
        (ends,) = tails
        matrix = tail_matrix(dims, counts)
        for stream in range(streams):
            packed = held[stream, : dims[0] * GROUP, :]
            ends[stream] = dot(matrix, packed, TN).astype(BF16)

        def start_tail(source, row, left):
            @pl.when(left > 0)
            def _():
                start_out(ends, aligned(source * GROUP), row, GROUP, sems.at[4])

        found = each_tail(dims, counts, start_tail)
        wait_for(ends, slice(0, streams), found * GROUP, sems.at[4])
    for number, size in enumerate(sizes):
        wait_for(held, slice(0, streams), size, sems.at[3 + number])


def unpack(dims, who, counts, plan, mine, theirs, outs, base, rows):
    half = outs[0].shape[1]
    streams = theirs.shape[0]
    tails = [pltpu.VMEM((streams, dims[0] * GROUP, half), BF16)] if base == 0 else []
    first = 4 + len(mine)
    return pl.pallas_call(
        functools.partial(unpack_kernel, dims, base, rows, streams),
        out_shape=[jax.ShapeDtypeStruct(out.shape, BF16) for out in outs],
        in_specs=[SCALARS] * 3 + [HBM] * (len(mine) + 1 + len(outs)),
        out_specs=[HBM] * len(outs),
        input_output_aliases={first + number: number for number in range(len(outs))},
        scratch_shapes=[
            pltpu.VMEM((streams, 2 * rows, half), BF16),
            pltpu.SemaphoreType.DMA((5,)),
        ]
        + tails,
        cost_estimate=NO_COST,
        compiler_params=PARAMS,
        name="unpack",
    )(who, counts, plan, *mine, theirs, *outs)


def blank_kernel(sources, slot, counts, values, tangents, other_values, other_tangents, zeros, sem):
    zeros[...] = jnp.zeros_like(zeros)

    def step(source, total):
        padded = round_up(counts[source])
        size = aligned(slot - padded)
        row = aligned(source * slot + padded)

        @pl.when(size > 0)
        def _():
            for low, high in ((values, tangents), (other_values, other_tangents)):
                for here, there in (
                    (zeros.at[0, pl.ds(0, size)], low.at[pl.ds(row, size)]),
                    (zeros.at[:, pl.ds(0, size)], high.at[:, pl.ds(row, size)]),
                ):
                    pltpu.make_async_copy(here, there, sem).start()

        return total + size

    total = lax.fori_loop(0, sources, step, jnp.int32(0))
    for low, high in ((values, tangents), (other_values, other_tangents)):

        @pl.when(total > 0)
        def _():
            low_part, high_part = low.at[pl.ds(0, aligned(total))], high.at[:, pl.ds(0, aligned(total))]
            pltpu.make_async_copy(low_part, low_part, sem).wait()
            pltpu.make_async_copy(high_part, high_part, sem).wait()


def blank(counts, row_count, half, sources):
    slot = row_count // sources
    values = jax.ShapeDtypeStruct((row_count, half), BF16)
    tangents = jax.ShapeDtypeStruct((3, row_count, half), BF16)
    return pl.pallas_call(
        functools.partial(blank_kernel, sources, slot),
        out_shape=(values, tangents, values, tangents),
        in_specs=[SCALARS],
        out_specs=(HBM, HBM, HBM, HBM),
        scratch_shapes=[pltpu.VMEM((3, slot, half), BF16), pltpu.SemaphoreType.DMA],
        cost_estimate=NO_COST,
        compiler_params=PARAMS,
        name="blank",
    )(counts)


NN = (((1,), (0,)), ((), ()))
TN = (((0,), (0,)), ((), ()))


def dot(a, b, dims=NN):
    return lax.dot_general(a, b, dims, preferred_element_type=F32)


def blocks_kernel(
    dims,
    base,
    rows,
    tile,
    first,
    final,
    merged,
    who,
    own,
    got,
    w_in,
    w_out,
    w_in_t,
    w_out_t,
    bias,
    *rest,
):
    if base != 0:
        plan, *rest = rest
    if first:
        grads_before = bias_before = None
    else:
        grads_before, bias_before, *rest = rest
    y_own, d_own, *rest = rest
    if merged:
        send, *rest = rest
        y_send, d_send = send.at[pl.ds(0, 4)], send.at[pl.ds(4, 4)]
    else:
        y_send, d_send, *rest = rest
    if final:
        kept, *rest = rest
        sent, rest = rest[:2], rest[2:]
    grads, biases, x_low, acts, slopes, lin = rest
    step = pl.program_id(0)
    side = who[SIDE]
    wide = w_in.shape[1]
    half = wide // 2

    @pl.when(step == 0)
    def _():
        if first:
            grads[...] = jnp.zeros_like(grads)
            biases[...] = jnp.zeros_like(biases)
        else:
            grads[...] = grads_before[...]
            biases[...] = bias_before[...]

    packed = side * rows + step * tile + lax.broadcasted_iota(jnp.int32, (tile, 128), 0)
    if base == OVER:
        filled = packed < plan[OVER_LEFT]
    elif base == 0:
        filled = packed < who[TOTAL]
    else:
        packed = packed + base
        top = 2 * dims[2] - plan[IN_LEFT] - plan[IN_RIGHT]
        filled = (packed < plan[KEPT]) | (packed >= top)
    filled = jnp.where(filled, 1.0, 0.0)
    is_filled = jnp.concatenate([filled] * (wide // 128), axis=1) > 0.0

    def load(stream):
        mine, theirs = own[stream].astype(F32), got[stream].astype(F32)
        left = jnp.where(side == 0, mine, theirs)
        right = jnp.where(side == 0, theirs, mine)
        return jnp.where(is_filled, jnp.concatenate([left, right], axis=1), 0.0)

    def store(own, send, stream, value):
        left, right = value[:, :half].astype(BF16), value[:, half:].astype(BF16)
        own[stream] = jnp.where(side == 0, left, right)
        send[stream] = jnp.where(side == 0, right, left)

    def add_bias(place, value):
        biases[place] += jnp.sum(value.reshape(tile // 8, 8, wide), axis=0)

    x = [load(stream) for stream in range(4)]
    for block in range(2):
        for stream in range(4):
            x_low[block, stream * tile : (stream + 1) * tile] = x[stream].astype(BF16)
        pre = dot(x_low[block], w_in[block])
        z = pre[:tile] + bias[0, block][None, :]
        small = jnp.exp(-jnp.abs(z))
        whole = 1.0 / (1.0 + small)
        slope = jnp.where(z >= 0.0, whole, small * whole)
        slopes[block] = slope
        acts[block, :tile] = (jnp.maximum(z, 0.0) + jnp.log1p(small) - LOG_TWO).astype(BF16)
        for stream in range(1, 4):
            part = pre[stream * tile : (stream + 1) * tile]
            lin[block, stream - 1] = part
            acts[block, stream * tile : (stream + 1) * tile] = (slope * part).astype(BF16)
        out = dot(acts[block], w_out[block])
        x = [x[stream] + out[stream * tile : (stream + 1) * tile] for stream in range(4)]
        x[0] = x[0] + bias[1, block][None, :]
    for stream in range(4):
        store(y_own, y_send, stream, x[stream])

    g = [load(4 + stream) for stream in range(4)]
    for block in (1, 0):
        add_bias(2 + block, g[0])
        g_low = jnp.concatenate([part.astype(BF16) for part in g], axis=0)
        value = dot(acts[block], g_low, TN)
        for part in range(2):
            place = 2 * wide + block * wide + part * half
            grads[0, place : place + half, :] += value[:half, part * half : (part + 1) * half]
            grads[1, place : place + half, :] += value[half:, part * half : (part + 1) * half]
        mixed = dot(g_low, w_out_t[block])
        slope = slopes[block]
        total = jnp.zeros((tile, wide), F32)
        lower = []
        for stream in range(1, 4):
            part = mixed[stream * tile : (stream + 1) * tile]
            total = total + part * lin[block, stream - 1]
            lower.append((part * slope).astype(BF16))
        g_pre = (mixed[:tile] * slope + slope * (1.0 - slope) * total).astype(BF16)
        add_bias(block, g_pre.astype(F32))
        stack = jnp.concatenate([g_pre] + lower, axis=0)
        value = dot(x_low[block], stack, TN)
        for part in range(2):
            grads[part, block * wide : (block + 1) * wide, :] += value[:, part * half : (part + 1) * half]
        back = dot(stack, w_in_t[block])
        g = [g[stream] + back[stream * tile : (stream + 1) * tile] for stream in range(4)]
    for stream in range(4):
        store(d_own, d_send, stream, g[stream])

    if final:

        @pl.when(step == rows // tile - 1)
        def _():
            total = jnp.sum(biases[...], axis=1)
            for part in range(2):
                grads[part, 4 * wide : 4 * wide + 4, :] = total[:, part * half : (part + 1) * half]
            flag = who[QUARTER] >> 1
            size = kept.shape[1]
            kept[...] = grads[:, pl.ds(aligned(flag * size), size), :]
            for part in range(2):
                other = grads[part, pl.ds(aligned((1 - flag) * size), size), :]
                sent[part][...] = other.astype(BF16)


def tile_of(rows):
    return max(tile for tile in range(GROUP, 193, GROUP) if rows % tile == 0)


def run_blocks(dims, who, plan, own, got, weights, sums, base, final, merged):
    rows, half = own.shape[1:]
    wide = 2 * half
    tile = tile_of(rows)
    first = sums is None
    piece = pl.BlockSpec((8, tile, half), lambda i: (0, i, 0))

    def whole(array):
        return pl.BlockSpec(
            array.shape, lambda i, rank=len(array.shape): (0,) * rank, pipeline_mode=pl.Buffered(1)
        )

    sum_rows = 4 * wide + dims[3]
    sums_held = [((2, sum_rows, half), F32), ((4, 8, wide), F32)]
    if final:
        results = [((2, sum_rows // 2, half), F32)] + [((sum_rows // 2, half), BF16)] * 2
        scratch = [pltpu.VMEM(*item) for item in sums_held]
    else:
        results, scratch = sums_held, []
    results = [jax.ShapeDtypeStruct(*item) for item in results]
    sizes = (4, 4, 8) if merged else (4, 4, 4, 4)
    out_shapes = [jax.ShapeDtypeStruct((size, rows, half), BF16) for size in sizes]
    out_pieces = [pl.BlockSpec((size, tile, half), lambda i: (0, i, 0)) for size in sizes]
    plans = () if base == 0 else (plan,)
    extra = () if first else sums
    operands = (who, own, got, *weights, *plans, *extra)
    aliases = {}
    if not first and not final:
        aliases = {len(operands) - 2 + i: len(sizes) + i for i in range(2)}
    return pl.pallas_call(
        functools.partial(blocks_kernel, dims, base, rows, tile, first, final, merged),
        grid=(rows // tile,),
        out_shape=out_shapes + results,
        in_specs=[SCALARS]
        + [piece] * 2
        + [whole(item) for item in weights]
        + [SCALARS] * len(plans)
        + [whole(item) for item in extra],
        out_specs=out_pieces + [whole(item) for item in results],
        input_output_aliases=aliases,
        scratch_shapes=scratch
        + [
            pltpu.VMEM((2, 4 * tile, wide), BF16),
            pltpu.VMEM((2, 4 * tile, wide), BF16),
            pltpu.VMEM((2, tile, wide), F32),
            pltpu.VMEM((2, 3, tile, wide), F32),
        ],
        cost_estimate=pl.CostEstimate(
            flops=rows * COST_PER_ROW if base == 0 else 0, bytes_accessed=1024, transcendentals=0
        ),
        compiler_params=PARAMS,
        name="blocks",
    )(*operands)


def swap_tensor(value):
    return lax.ppermute(value, "tensor", [(0, 1), (1, 0)])


def shift(value, order, step):
    pairs = list(zip(order[:-1], order[1:]))
    return lax.ppermute(value, "dp", pairs if step == 1 else [(b, a) for a, b in pairs])


def in_order(flag, mine, other, axis):
    return jnp.where(
        flag == 0, jnp.concatenate([mine, other], axis), jnp.concatenate([other, mine], axis)
    )


def my_quarter():
    place = lax.axis_index("dp")
    return (place & 1) * 2 + ((place >> 1) & 1)


def quarter_kernel(dims, counts, w_in, w_out, who, piece, sems):
    half = w_in.shape[2]
    mine = my_quarter()
    make_who(dims, counts, who)
    for number in range(4):

        @pl.when(mine == number)
        def _(number=number):
            if number < 2:
                copies = [pltpu.make_async_copy(w_in.at[number], piece, sems.at[0])]
            else:
                copies = [
                    pltpu.make_async_copy(
                        w_out.at[number - 2, :, pl.ds(part * half, half)],
                        piece.at[pl.ds(part * half, half)],
                        sems.at[part],
                    )
                    for part in range(2)
                ]
            for copy in copies:
                copy.start()
            for copy in copies:
                copy.wait()


def quarter_of(dims, counts, weight_in, weight_out):
    on_chip = pl.BlockSpec(memory_space=pltpu.VMEM)
    return pl.pallas_call(
        functools.partial(quarter_kernel, dims),
        out_shape=(
            jax.ShapeDtypeStruct((8,), jnp.int32),
            jax.ShapeDtypeStruct(weight_in.shape[1:], BF16),
        ),
        in_specs=[SCALARS] + [on_chip] * 2,
        out_specs=(SCALARS, on_chip),
        scratch_shapes=[pltpu.SemaphoreType.DMA((2,))],
        cost_estimate=NO_COST,
        name="quarter",
    )(counts, weight_in, weight_out)


def assemble_kernel(
    who, w_in, w_out, b_in, b_out, b_got, *refs
):
    pieces, (in_all, out_all, in_turned, out_turned, b_all, held, sems) = refs[:4], refs[4:]
    side, own = who[SIDE], who[QUARTER]
    half = w_in.shape[2]
    copies = [
        pltpu.make_async_copy(piece, held.at[own ^ number], sems.at[number])
        for number, piece in enumerate(pieces)
    ]
    for copy in copies:
        copy.start()
    for copy in copies:
        copy.wait()

    def ordered(mine, other, axis):
        return jnp.where(
            side == 0,
            jnp.concatenate([mine, other], axis),
            jnp.concatenate([other, mine], axis),
        )

    for block in range(2):
        value = ordered(w_in[block], held[block], 1)
        in_all[block] = value
        in_turned[block] = value.T
        other = jnp.concatenate([held[2 + block, :half], held[2 + block, half:]], axis=1)
        value = ordered(w_out[block], other, 0)
        out_all[block] = value
        out_turned[block] = value.T
    for number, mine in enumerate((b_in, b_out)):
        b_all[number] = ordered(mine[...], b_got[number], 1)


def assemble(who, weight_in, weight_out, bias_in, bias_out, bias_got, pieces):
    blocks, wide, half = weight_in.shape
    whole = jax.ShapeDtypeStruct((blocks, wide, wide), BF16)
    on_chip = pl.BlockSpec(memory_space=pltpu.VMEM)
    return pl.pallas_call(
        assemble_kernel,
        out_shape=(whole,) * 4 + (jax.ShapeDtypeStruct((2, blocks, wide), F32),),
        in_specs=[SCALARS] + [on_chip] * 5 + [HBM] * 4,
        out_specs=(on_chip,) * 5,
        scratch_shapes=[pltpu.VMEM((4, wide, half), BF16), pltpu.SemaphoreType.DMA((4,))],
        cost_estimate=NO_COST,
        compiler_params=PARAMS,
        name="assemble",
    )(who, weight_in, weight_out, bias_in, bias_out, bias_got, *pieces)


def flipped(value, flip, size):
    return lax.ppermute(value, "dp", [(i, i ^ flip) for i in range(size)])


def groups_of(bits):
    return [(0, 1), (1, 1)] + [(bit, min(2, bits - bit)) for bit in range(2, bits, 2)]


def reduce_step(grads, group, place, size):
    bit, many = group
    mine = (place >> bit) & ((1 << many) - 1)
    rows = grads.shape[1] >> many
    kept = lax.dynamic_slice_in_dim(grads, mine * rows, rows, 1)
    for flip in range(1, 1 << many):
        sent = lax.dynamic_slice_in_dim(grads, (mine ^ flip) * rows, rows, 1).astype(BF16)
        kept = kept + flipped(sent, flip << bit, size).astype(F32)
    return kept


def join_kernel(mine, *refs):
    parts, (whole, sems) = refs[:-2], refs[-2:]
    rows = parts[0].shape[0]
    copies = [
        pltpu.make_async_copy(
            part, whole.at[pl.ds(aligned((mine[0] ^ flip) * rows), rows)], sems.at[flip]
        )
        for flip, part in enumerate(parts)
    ]
    for copy in copies:
        copy.start()
    for copy in copies:
        copy.wait()


def gather_step(total, group, place, size):
    bit, many = group
    mine = (place >> bit) & ((1 << many) - 1)
    parts = [total] + [flipped(total, flip << bit, size) for flip in range(1, 1 << many)]
    rows, half = total.shape
    return pl.pallas_call(
        join_kernel,
        out_shape=jax.ShapeDtypeStruct((rows << many, half), BF16),
        in_specs=[SCALARS] + [HBM] * len(parts),
        out_specs=pl.BlockSpec(memory_space=pltpu.VMEM),
        scratch_shapes=[pltpu.SemaphoreType.DMA((len(parts),))],
        cost_estimate=NO_COST,
        name="join",
    )(mine.astype(jnp.int32)[None], *parts)


def sum_in_fours(values, step, size):
    flips = (step, 2 * step, 3 * step) if 2 * step < size else (step,)
    return values + sum(
        flipped(values, flip, size) for flip in flips
    )


def finish_kernel(flag, mine, other, grad_in, grad_out, bias_in, bias_out, held, sems):
    rows, half = mine.shape
    copies = [
        pltpu.make_async_copy(part, held.at[pl.ds(aligned(which * rows), rows)], sems.at[number])
        for number, (which, part) in enumerate(((flag[0], mine), (1 - flag[0], other)))
    ]
    for copy in copies:
        copy.start()
    for copy in copies:
        copy.wait()
    wide = 2 * half
    for block in range(2):
        grad_in[block] = held[block * wide : (block + 1) * wide, :].astype(F32)
        for part in range(2):
            first = (2 + block) * wide + part * half
            grad_out[block, :, part * half : (part + 1) * half] = held[first : first + half, :].astype(F32)
    last = held[4 * wide : 4 * wide + GROUP, :].astype(F32)
    bias_in[...] = last[:2]
    bias_out[...] = last[2:4]


def finish(flag, mine, other):
    rows, half = mine.shape
    on_chip = pl.BlockSpec(memory_space=pltpu.VMEM)
    return pl.pallas_call(
        finish_kernel,
        out_shape=(
            jax.ShapeDtypeStruct((2, 2 * half, half), F32),
            jax.ShapeDtypeStruct((2, half, 2 * half), F32),
            jax.ShapeDtypeStruct((2, half), F32),
            jax.ShapeDtypeStruct((2, half), F32),
        ),
        in_specs=[SCALARS] + [HBM] * 2,
        out_specs=(on_chip,) * 4,
        scratch_shapes=[pltpu.VMEM((2 * rows, half), BF16), pltpu.SemaphoreType.DMA((2,))],
        cost_estimate=NO_COST,
        compiler_params=PARAMS,
        name="finish",
    )(flag, mine, other)


def together(*values):
    return lax.optimization_barrier(values)


def local(
    dp_size,
    features,
    tangents,
    weight_in,
    bias_in,
    weight_out,
    bias_out,
    counts,
    cotangent_values,
    cotangent_tangents,
):
    row_count, half = features.shape
    sources = counts.shape[0]
    unit = row_count // 256
    level, first, moved, extra = (unit * part for part in (ROWS, FIRST, MOVED, EXTRA))
    order = chain_order(dp_size)
    bits = dp_size.bit_length() - 1
    dims = (sources, row_count // sources, level, 8 * dp_size)
    side = lax.axis_index("tensor")
    place = lax.axis_index("dp")
    arrays = (features, tangents, cotangent_values, cotangent_tangents)
    middle = (2 * first, level - first - moved)
    last = (2 * (level - moved), moved)

    who, piece = quarter_of(dims, counts, weight_in, weight_out)
    piece_got = swap_tensor(piece)
    bias_got = swap_tensor(jnp.stack([bias_in, bias_out]))
    totals = jnp.where(jnp.arange(dp_size, dtype=jnp.int32) == place, who[TOTAL], 0)
    totals = sum_in_fours(totals, 1, dp_size)
    who, totals = together(who, totals)
    own1, send1 = pack(dims, who, counts, None, arrays, 0, first)
    send1, piece_got, bias_got = together(send1, piece_got, bias_got)
    got1 = swap_tensor(send1)
    pieces = [piece_got] + [flipped(piece_got, flip, dp_size) for flip in (2, 1, 3)]
    who, own1 = together(who, own1)
    own2, send2 = pack(dims, who, counts, None, arrays, *middle)
    got2 = swap_tensor(send2)
    for step in range(2, bits, 2):
        totals = sum_in_fours(totals, 1 << step, dp_size)
    totals, own2 = together(totals, own2)
    plan = make_plan(who, totals, order, level, 2 * first, moved, extra)
    plan, pieces = together(plan, pieces)
    to_left, to_right = export(dims, who, counts, plan, *arrays, moved)
    neighbours = (shift(to_right, order, 1), shift(to_left, order, -1))
    pieces, to_left = together(pieces, to_left)
    weights = assemble(who, weight_in, weight_out, bias_in, bias_out, bias_got, pieces)
    who, weights, neighbours = together(who, weights, neighbours)
    own3, send3 = pack(dims, who, counts, plan, arrays, *last, neighbours)
    got3 = swap_tensor(send3)
    own3, weights, got2 = together(own3, weights, got2)

    def blocks(base, plan, arrived, sums, final=False, merged=False):
        results = run_blocks(dims, who, plan, *arrived, weights, sums, base, final, merged)
        count = 3 if merged else 4
        return results[:count], tuple(results[count:])

    def place_all(outs, base, rows, plan, result, got):
        return unpack(dims, who, counts, plan, result[:2], got, outs, base, rows)

    def place_values(outs, base, rows, own, got):
        return (*unpack(dims, who, counts, plan, [own], got, outs[:2], base, rows), *outs[2:])

    def place_grads(outs, base, rows, own, got):
        return (*outs[:2], *unpack(dims, who, counts, plan, [own], got, outs[2:], base, rows))

    result1, sums = blocks(0, plan, (own1, got1), None)
    later_counts, sums = together(counts, sums)
    outs = blank(later_counts, row_count, half, sources)

    def more(carry):
        return carry[0] < plan[ROUNDS]

    def extra_round(carry):
        number, sums, outs = carry
        done = number * (2 * extra)
        here = plan + jnp.zeros((8,), jnp.int32).at[OVER_FIRST].set(done).at[OVER_LEFT].set(-done)
        own, send = pack(dims, who, counts, here, arrays, OVER, extra)
        result, sums = blocks(OVER, here, (own, swap_tensor(send)), sums, merged=True)
        outs = place_all(outs, OVER, extra, here, result, swap_tensor(result[2]))
        return number + 1, sums, tuple(outs)

    _, sums, outs = lax.while_loop(more, extra_round, (jnp.int32(0), sums, tuple(outs)))
    y1_got, d1_got = swap_tensor(result1[2]), swap_tensor(result1[3])
    result2, sums = blocks(middle[0], plan, (own2, got2), sums, merged=True)
    sums, outs = together(sums, outs)
    result3, sums = blocks(last[0], plan, (own3, got3), sums, final=True)

    sums, y1_got = together(sums, y1_got)
    kept, *sent = sums
    core, across, *others = groups_of(bits)
    came = jnp.stack([flipped(part, 1, dp_size) for part in sent])
    grads = kept + came.astype(F32)
    grads = reduce_step(grads, across, place, dp_size)
    outs = place_values(outs, 0, first, result1[0], y1_got)
    grads, d1_got, outs = together(grads, d1_got, outs)
    for group in others:
        grads = reduce_step(grads, group, place, dp_size)
    outs = place_grads(outs, 0, first, result1[1], d1_got)
    grads, outs = together(grads, outs)
    y3_got = swap_tensor(result3[2])
    mine = lax.dynamic_index_in_dim(grads, side, 0, keepdims=False)
    other = lax.dynamic_index_in_dim(grads, 1 - side, 0, keepdims=False).astype(BF16)
    total = (mine + swap_tensor(other).astype(F32)).astype(BF16)
    total, d3_send, y3_got = together(total, result3[3], y3_got)
    d3_got = swap_tensor(d3_send)
    y_left, y_right = handback(dims, who, plan, result3[0], y3_got, *last, moved)
    y_back = (shift(y_left, order, -1), shift(y_right, order, 1))
    outs = place_values(outs, *last, result3[0], y3_got)
    for group in reversed(others):
        total = gather_step(total, group, place, dp_size)
    total, d3_got, outs = together(total, d3_got, outs)
    yd2_got = swap_tensor(result2[2])
    d_left, d_right = handback(dims, who, plan, result3[1], d3_got, *last, moved)
    d_back = (shift(d_left, order, -1), shift(d_right, order, 1))
    total = gather_step(total, across, place, dp_size)
    outs = place_grads(outs, *last, result3[1], d3_got)
    total, outs = together(total, outs)
    total_got = flipped(total, 1, dp_size)
    outs = place_values(outs, None, moved, *y_back)
    sums = finish((place & 1).astype(jnp.int32)[None], total, total_got)
    outs, sums = together(outs, sums)
    outs = place_grads(outs, None, moved, *d_back)
    outs = place_all(outs, *middle, plan, result2, yd2_got)
    grad_in, grad_out, bias_in_grad, bias_out_grad = sums
    return (*outs, grad_in, bias_in_grad, grad_out, bias_out_grad)


def solution(mesh):
    in_specs = (
        P("dp", "tensor"),
        P(None, "dp", "tensor"),
        P(None, None, "tensor"),
        P(None, "tensor"),
        P(None, "tensor", None),
        P(None, "tensor"),
        P("dp"),
        P("dp", "tensor"),
        P(None, "dp", "tensor"),
    )
    out_specs = (
        P("dp", "tensor"),
        P(None, "dp", "tensor"),
        P("dp", "tensor"),
        P(None, "dp", "tensor"),
        P(None, None, "tensor"),
        P(None, "tensor"),
        P(None, "tensor", None),
        P(None, "tensor"),
    )
    return jax.shard_map(
        functools.partial(local, mesh.shape["dp"]),
        mesh=mesh,
        in_specs=in_specs,
        out_specs=out_specs,
        check_vma=False,
    )
```

```python
import functools
import math

import jax
import jax.numpy as jnp
import numpy as np
from jax import lax
from jax.experimental import pallas as pl
from jax.experimental.pallas import tpu as pltpu
from jax.sharding import PartitionSpec as P

LOG_TWO = math.log(2.0)
GROUP = 16
BF16, F32 = jnp.bfloat16, jnp.float32
SCALARS = pl.BlockSpec(memory_space=pltpu.SMEM)
HBM = pl.BlockSpec(memory_space=pltpu.HBM)
MIB = 1 << 20

ROWS, FIRST, MOVED, EXTRA = 79, 36, 28, 8
OVER = -1

PLACE, SIDE, TOTAL, QUARTER, TAILS = range(5)
ROUNDS, OUT_LEFT, IN_LEFT, OUT_RIGHT, IN_RIGHT, KEPT, OVER_FIRST, OVER_LEFT = range(8)


def aligned(value):
    return pl.multiple_of(value, GROUP)


def round_up(count):
    return (count + GROUP - 1) // GROUP * GROUP


NO_COST = pl.CostEstimate(flops=0, bytes_accessed=1024, transcendentals=0)
SOME_COST = pl.CostEstimate(flops=10**10, bytes_accessed=1024, transcendentals=0)
COST_PER_ROW = 7 * 10**7


PARAMS = pltpu.CompilerParams(vmem_limit_bytes=60 * MIB)


def chain_order(size):
    around = (0, 1, 3, 2)
    order = []
    for block in range(size // 4):
        order += [4 * block + i for i in (around if block % 2 == 0 else around[::-1])]
    return order


def plan_kernel(order, most, early, moved, extra, who, totals, plan, flows):
    size = len(order)

    def most_out(total):
        return jnp.clip((total - early) // 2 // GROUP * GROUP, 0, moved)

    def total_of(i):
        return totals[order[i]]

    flow, rounds = jnp.int32(0), jnp.int32(0)
    flows[0] = flow
    for i in range(size):
        here = total_of(i) + flow
        if i + 1 < size:
            flow = jnp.clip(here - most, -most_out(total_of(i + 1)), most_out(total_of(i)))
        else:
            flow = jnp.int32(0)
        flows[i + 1] = flow
        over = jnp.maximum(here - flow - most, 0)
        rounds = jnp.maximum(rounds, (over + extra - 1) // extra)
    place = who[PLACE]
    left, right, total = flows[place], flows[place + 1], who[TOTAL]
    out_left, out_right = jnp.maximum(-left, 0), jnp.maximum(right, 0)
    over = jnp.maximum(total + left - right - most, 0)
    kept = total - out_left - out_right - over
    plan[ROUNDS] = rounds
    plan[OUT_LEFT] = out_left
    plan[IN_LEFT] = jnp.maximum(left, 0)
    plan[OUT_RIGHT] = out_right
    plan[IN_RIGHT] = jnp.maximum(-right, 0)
    plan[KEPT] = kept
    plan[OVER_FIRST] = kept
    plan[OVER_LEFT] = over


def make_plan(who, totals, order, level, early, moved, extra):
    return pl.pallas_call(
        functools.partial(plan_kernel, order, 2 * level, early, moved, 2 * extra),
        out_shape=jax.ShapeDtypeStruct((8,), jnp.int32),
        in_specs=[SCALARS] * 2,
        out_specs=SCALARS,
        scratch_shapes=[pltpu.SMEM((len(order) + 1,), jnp.int32)],
        cost_estimate=NO_COST,
        name="plan",
    )(who, totals)


def own_piece(limit, plan, base, rows):
    if base == OVER:
        first, size = plan[OVER_FIRST], jnp.clip(plan[OVER_LEFT], 0, 2 * rows)
    else:
        first, size = jnp.int32(base), jnp.clip(limit - base, 0, 2 * rows)
    return first, first + size, size


def moved_pieces(dims, plan, base, rows):
    top = 2 * dims[2] - base
    left, right = plan[IN_LEFT], plan[IN_RIGHT]
    return (aligned(top - left - right), aligned(left)), (aligned(top - right), aligned(right))


def sent_pieces(who, plan):
    left, right, total = plan[OUT_LEFT], plan[OUT_RIGHT], who[TOTAL]
    return (total - right - left, total - right, left), (total - right, total, right)


def whole_groups(count):
    return count // GROUP * GROUP


def each_run(dims, who, counts, piece, visit):
    sources, slot = dims[:2]
    first, end = piece[:2]

    def step(source, start):
        after = start + whole_groups(counts[source])
        begin = jnp.maximum(start, first)
        stop = jnp.minimum(after, end)

        @pl.when(stop > begin)
        def _():
            row = source * slot + begin - start
            visit(aligned(row), aligned(begin - first), aligned(stop - begin))

        return after

    lax.fori_loop(0, sources, step, who[TAILS])


def copies_between(held, streams, place, values, tangents, row, size):
    return (
        (values.at[pl.ds(row, size)], held.at[streams, pl.ds(place, size)]),
        (tangents.at[:, pl.ds(row, size)], held.at[pl.ds(streams + 1, 3), pl.ds(place, size)]),
    )


def wait_for(held, streams, size, sem):
    @pl.when(size > 0)
    def _():
        part = held.at[streams, pl.ds(0, aligned(size))]
        pltpu.make_async_copy(part, part, sem).wait()


def each_tail(dims, counts, visit):
    sources, slot = dims[:2]

    def step(source, found):
        left = counts[source] % GROUP
        row = source * slot + jnp.minimum(whole_groups(counts[source]), slot - GROUP)
        visit(source, aligned(row), left)
        return found + jnp.minimum(left, 1)

    return lax.fori_loop(0, sources, step, jnp.int32(0))


def tail_matrix(dims, counts):
    wide = dims[0] * GROUP
    lane = lax.broadcasted_iota(jnp.int32, (8, wide), 1)
    target = jnp.full((8, wide), -1, jnp.int32)
    start = jnp.int32(0)
    for source in range(dims[0]):
        left = counts[source] % GROUP
        row = lane - source * GROUP
        target = jnp.where((row >= 0) & (row < left), start + row, target)
        start = start + left
    number = lax.broadcasted_iota(jnp.int32, (wide, wide), 0)
    return jnp.where(number == target[:1], 1.0, 0.0).astype(BF16)


def make_who(dims, counts, who):
    place = lax.axis_index("dp")
    around = (place & 3) ^ ((place & 3) >> 1)
    back = (place >> 2) & 1
    who[PLACE] = (place >> 2) * 4 + around * (1 - back) + (3 - around) * back
    who[SIDE] = lax.axis_index("tensor")
    who[QUARTER] = my_quarter()

    def step(source, carry):
        whole, left = carry
        return whole + whole_groups(counts[source]), left + counts[source] % GROUP

    whole, left = lax.fori_loop(0, dims[0], step, (jnp.int32(0), jnp.int32(0)))
    left = (left + GROUP - 1) // GROUP * GROUP
    who[TOTAL] = whole + left
    who[TAILS] = left


def start_copies(held, place, sources, row, size, sem):
    for streams, (values, tangents) in zip((0, 4), sources):
        for copy in copies_between(held, streams, place, values, tangents, row, size):
            pltpu.make_async_copy(*copy, sem).start()


def pack_kernel(dims, base, rows, moving, who, counts, *refs):
    plan = None
    if moving or base == OVER:
        plan, *refs = refs
    sources, refs = (refs[:2], refs[2:4]), refs[4:]
    neighbours = ()
    if moving:
        neighbours, refs = refs[:2], refs[2:]
    keep, send, held, sems, *tails = refs
    side = who[SIDE]
    piece = own_piece(plan[KEPT] if moving else who[TOTAL], plan, base, rows)
    size = piece[2]

    if base == 0:
        ends, packed = tails

        def start_tail(source, row, left):
            start_copies(ends, aligned(source * GROUP), sources, row, GROUP, sems.at[1])

        each_tail(dims, counts, start_tail)
        size = size - who[TAILS]

    def start(row, place, size):
        start_copies(held, place, sources, row, size, sems.at[0])

    each_run(dims, who, counts, piece, start)
    arrivals = []
    if moving:
        pieces = moved_pieces(dims, plan, base, rows)
        for number, neighbour in enumerate(neighbours):
            place, moved = pieces[number]
            copy = pltpu.make_async_copy(
                neighbour.at[:, pl.ds(0, moved)], held.at[:, pl.ds(place, moved)], sems.at[1 + number]
            )
            arrivals.append((moved, copy))
        for moved, copy in arrivals:
            pl.when(moved > 0)(copy.start)
    if base == 0:
        matrix = tail_matrix(dims, counts)
        wait_for(ends, slice(0, 8), jnp.int32(dims[0] * GROUP), sems.at[1])
        for stream in range(8):
            packed[stream] = dot(matrix, ends[stream]).astype(BF16)

        def put(group, carry):
            here = pl.ds(aligned(group * GROUP), GROUP)
            held[:, here, :] = packed[:, here, :]
            return carry

        lax.fori_loop(0, who[TAILS] // GROUP, put, 0)
    wait_for(held, slice(0, 8), size, sems.at[0])
    for moved, copy in arrivals:
        pl.when(moved > 0)(copy.wait)
    out = [
        pltpu.make_async_copy(
            held.at[:, pl.ds(aligned(part * rows), rows)], target, sems.at[5 + number]
        )
        for number, (part, target) in enumerate(((1 - side, send), (side, keep)))
    ]
    for copy in out:
        copy.start()
    for copy in out:
        copy.wait()


def pack(dims, who, counts, plan, arrays, base, rows, neighbours=()):
    half = arrays[0].shape[1]
    shape = jax.ShapeDtypeStruct((8, rows, half), BF16)
    plans = (plan,) if neighbours or base == OVER else ()
    tails = [pltpu.VMEM((8, dims[0] * GROUP, half), BF16)] * 2 if base == 0 else []
    return pl.pallas_call(
        functools.partial(pack_kernel, dims, base, rows, len(neighbours) > 0),
        out_shape=(shape, shape),
        in_specs=[SCALARS] * (2 + len(plans)) + [HBM] * (4 + len(neighbours)),
        out_specs=(HBM, HBM),
        scratch_shapes=[pltpu.VMEM((8, 2 * rows, half), BF16), pltpu.SemaphoreType.DMA((7,))] + tails,
        cost_estimate=NO_COST,
        compiler_params=PARAMS,
        name="pack",
    )(who, counts, *plans, *arrays, *neighbours)


def export_kernel(dims, moved, who, counts, plan, x, x3, g, g3, *refs):
    targets, (held, sems) = refs[:2], refs[2:]
    pieces = sent_pieces(who, plan)
    for number, piece in enumerate(pieces):

        def start(row, place, size, number=number):
            place = aligned(number * moved + place)
            start_copies(held, place, ((x, x3), (g, g3)), row, size, sems.at[number])

        @pl.when(piece[2] > 0)
        def _(piece=piece, start=start):
            each_run(dims, who, counts, piece, start)

    for number, piece in enumerate(pieces):
        wait_for(held, slice(0, 8), piece[2], sems.at[number])
    out = [
        pltpu.make_async_copy(
            held.at[:, pl.ds(number * moved, moved)], target, sems.at[2 + number]
        )
        for number, target in enumerate(targets)
    ]
    for copy in out:
        copy.start()
    for copy in out:
        copy.wait()


def export(dims, who, counts, plan, x, x3, g, g3, moved):
    half = x.shape[1]
    return pl.pallas_call(
        functools.partial(export_kernel, dims, moved),
        out_shape=(jax.ShapeDtypeStruct((8, moved, half), BF16),) * 2,
        in_specs=[SCALARS] * 3 + [HBM] * 4,
        out_specs=(HBM,) * 2,
        scratch_shapes=[pltpu.VMEM((8, 2 * moved, half), BF16), pltpu.SemaphoreType.DMA((4,))],
        cost_estimate=NO_COST,
        compiler_params=PARAMS,
        name="export",
    )(who, counts, plan, x, x3, g, g3)


def load_results(held, rows, side, mine, theirs, sems):
    loads = [(0, 1 - side, part) for part in theirs[:1]] + [(4, 1 - side, part) for part in theirs[1:]]
    loads += [(4 * number, side, part) for number, part in enumerate(mine)]
    loads = [
        pltpu.make_async_copy(
            origin,
            held.at[pl.ds(first, origin.shape[0]), pl.ds(aligned(part * rows), rows)],
            sems.at[number],
        )
        for number, (first, part, origin) in enumerate(loads)
    ]
    for load in loads:
        load.start()
    for load in loads:
        load.wait()


def handback_kernel(dims, base, rows, who, plan, *refs):
    mine, theirs, targets, (held, sems) = refs[:2], refs[2:4], refs[4:6], refs[6:]
    load_results(held, rows, who[SIDE], mine, theirs, sems)
    copies = []
    pieces = moved_pieces(dims, plan, base, rows)
    for number, ((place, size), target) in enumerate(zip(pieces, targets)):
        copy = pltpu.make_async_copy(
            held.at[:, pl.ds(place, size)], target.at[:, pl.ds(0, size)], sems.at[4 + number]
        )
        copies.append((size, copy))
    for size, copy in copies:
        pl.when(size > 0)(copy.start)
    for size, copy in copies:
        pl.when(size > 0)(copy.wait)


def handback(dims, who, plan, mine, theirs, base, rows, moved):
    half = mine[0].shape[2]
    shape = jax.ShapeDtypeStruct((8, moved, half), BF16)
    return pl.pallas_call(
        functools.partial(handback_kernel, dims, base, rows),
        out_shape=(shape, shape),
        in_specs=[SCALARS] * 2 + [HBM] * 4,
        out_specs=(HBM, HBM),
        scratch_shapes=[pltpu.VMEM((8, 2 * rows, half), BF16), pltpu.SemaphoreType.DMA((6,))],
        cost_estimate=SOME_COST,
        compiler_params=PARAMS,
        name="handback",
    )(who, plan, *mine, *theirs)


def unpack_kernel(dims, base, rows, streams, parts, who, counts, plan, *refs):
    pairs = streams // 4
    mine, theirs, refs = refs[:parts], refs[parts], refs[parts + 1 :]
    outs, (held, sems, *tails) = refs[2 * pairs : 4 * pairs], refs[4 * pairs :]
    load_results(held, rows, 1 if base is None else who[SIDE], mine, [theirs], sems)
    pieces = sent_pieces(who, plan)
    if base is not None:
        pieces = (own_piece(plan[KEPT], plan, base, rows),)
    sizes = [piece[2] for piece in pieces]
    if base == 0:
        sizes = [sizes[0] - who[TAILS]]

    def start_out(origin, place, row, size, sem):
        for number in range(pairs):
            copies = copies_between(
                origin, 4 * number, place, outs[2 * number], outs[2 * number + 1], row, size
            )
            for there, here in copies:
                pltpu.make_async_copy(here, there, sem).start()

    for number, piece in enumerate(pieces):

        def start(row, place, size, number=number):
            start_out(held, aligned(number * rows + place), row, size, sems.at[3 + number])

        @pl.when(piece[2] > 0)
        def _(piece=piece, start=start):
            each_run(dims, who, counts, piece, start)

    if base == 0:
        (ends,) = tails
        matrix = tail_matrix(dims, counts)
        for stream in range(streams):
            packed = held[stream, : dims[0] * GROUP, :]
            ends[stream] = dot(matrix, packed, TN).astype(BF16)

        def start_tail(source, row, left):
            @pl.when(left > 0)
            def _():
                start_out(ends, aligned(source * GROUP), row, GROUP, sems.at[4])

        found = each_tail(dims, counts, start_tail)
        wait_for(ends, slice(0, streams), found * GROUP, sems.at[4])
    for number, size in enumerate(sizes):
        wait_for(held, slice(0, streams), size, sems.at[3 + number])


def unpack(dims, who, counts, plan, mine, theirs, outs, base, rows):
    half = outs[0].shape[1]
    streams = theirs.shape[0]
    tails = [pltpu.VMEM((streams, dims[0] * GROUP, half), BF16)] if base == 0 else []
    first = 4 + len(mine)
    return pl.pallas_call(
        functools.partial(unpack_kernel, dims, base, rows, streams, len(mine)),
        out_shape=[jax.ShapeDtypeStruct(out.shape, BF16) for out in outs],
        in_specs=[SCALARS] * 3 + [HBM] * (len(mine) + 1 + len(outs)),
        out_specs=[HBM] * len(outs),
        input_output_aliases={first + number: number for number in range(len(outs))},
        scratch_shapes=[
            pltpu.VMEM((streams, 2 * rows, half), BF16),
            pltpu.SemaphoreType.DMA((5,)),
        ]
        + tails,
        cost_estimate=NO_COST,
        compiler_params=PARAMS,
        name="unpack",
    )(who, counts, plan, *mine, theirs, *outs)


def blank_kernel(sources, slot, counts, values, tangents, other_values, other_tangents, zeros, sem):
    zeros[...] = jnp.zeros_like(zeros)

    def step(source, total):
        padded = round_up(counts[source])
        size = aligned(slot - padded)
        row = aligned(source * slot + padded)

        @pl.when(size > 0)
        def _():
            for low, high in ((values, tangents), (other_values, other_tangents)):
                for here, there in (
                    (zeros.at[0, pl.ds(0, size)], low.at[pl.ds(row, size)]),
                    (zeros.at[:, pl.ds(0, size)], high.at[:, pl.ds(row, size)]),
                ):
                    pltpu.make_async_copy(here, there, sem).start()

        return total + size

    total = lax.fori_loop(0, sources, step, jnp.int32(0))
    for low, high in ((values, tangents), (other_values, other_tangents)):

        @pl.when(total > 0)
        def _():
            low_part, high_part = low.at[pl.ds(0, aligned(total))], high.at[:, pl.ds(0, aligned(total))]
            pltpu.make_async_copy(low_part, low_part, sem).wait()
            pltpu.make_async_copy(high_part, high_part, sem).wait()


def blank(counts, row_count, half, sources):
    slot = row_count // sources
    values = jax.ShapeDtypeStruct((row_count, half), BF16)
    tangents = jax.ShapeDtypeStruct((3, row_count, half), BF16)
    return pl.pallas_call(
        functools.partial(blank_kernel, sources, slot),
        out_shape=(values, tangents, values, tangents),
        in_specs=[SCALARS],
        out_specs=(HBM, HBM, HBM, HBM),
        scratch_shapes=[pltpu.VMEM((3, slot, half), BF16), pltpu.SemaphoreType.DMA],
        cost_estimate=NO_COST,
        compiler_params=PARAMS,
        name="blank",
    )(counts)


NN = (((1,), (0,)), ((), ()))
TN = (((0,), (0,)), ((), ()))


def dot(a, b, dims=NN):
    return lax.dot_general(a, b, dims, preferred_element_type=F32)


def blocks_kernel(
    dims,
    base,
    rows,
    tile,
    first,
    final,
    merged,
    who,
    own,
    got,
    w_in,
    w_out,
    w_in_t,
    w_out_t,
    bias,
    *rest,
):
    if base != 0:
        plan, *rest = rest
    if first:
        grads_before = bias_before = None
    else:
        grads_before, bias_before, *rest = rest
    y_own, d_own, *rest = rest
    if merged:
        send, *rest = rest
        y_send, d_send = send.at[pl.ds(0, 4)], send.at[pl.ds(4, 4)]
    else:
        y_send, d_send, *rest = rest
    if final:
        kept, *rest = rest
        sent, rest = rest[:2], rest[2:]
    grads, biases, x_low, acts, slopes, lin = rest
    step = pl.program_id(0)
    side = who[SIDE]
    wide = w_in.shape[1]
    half = wide // 2

    @pl.when(step == 0)
    def _():
        if first:
            grads[...] = jnp.zeros_like(grads)
            biases[...] = jnp.zeros_like(biases)
        else:
            grads[...] = grads_before[...]
            biases[...] = bias_before[...]

    packed = side * rows + step * tile + lax.broadcasted_iota(jnp.int32, (tile, 128), 0)
    if base == OVER:
        filled = packed < plan[OVER_LEFT]
    elif base == 0:
        filled = packed < who[TOTAL]
    else:
        packed = packed + base
        top = 2 * dims[2] - plan[IN_LEFT] - plan[IN_RIGHT]
        filled = (packed < plan[KEPT]) | (packed >= top)
    filled = jnp.where(filled, 1.0, 0.0)
    is_filled = jnp.concatenate([filled] * (wide // 128), axis=1) > 0.0

    def load(stream):
        mine, theirs = own[stream].astype(F32), got[stream].astype(F32)
        left = jnp.where(side == 0, mine, theirs)
        right = jnp.where(side == 0, theirs, mine)
        return jnp.where(is_filled, jnp.concatenate([left, right], axis=1), 0.0)

    def store(own, send, stream, value):
        left, right = value[:, :half].astype(BF16), value[:, half:].astype(BF16)
        own[stream] = jnp.where(side == 0, left, right)
        send[stream] = jnp.where(side == 0, right, left)

    def add_bias(place, value):
        biases[place] += jnp.sum(value.reshape(tile // 8, 8, wide), axis=0)

    x = [load(stream) for stream in range(4)]
    for block in range(2):
        for stream in range(4):
            x_low[block, stream * tile : (stream + 1) * tile] = x[stream].astype(BF16)
        pre = dot(x_low[block], w_in[block])
        z = pre[:tile] + bias[0, block][None, :]
        small = jnp.exp(-jnp.abs(z))
        whole = 1.0 / (1.0 + small)
        slope = jnp.where(z >= 0.0, whole, small * whole)
        slopes[block] = slope
        acts[block, :tile] = (jnp.maximum(z, 0.0) + jnp.log1p(small) - LOG_TWO).astype(BF16)
        for stream in range(1, 4):
            part = pre[stream * tile : (stream + 1) * tile]
            lin[block, stream - 1] = part
            acts[block, stream * tile : (stream + 1) * tile] = (slope * part).astype(BF16)
        out = dot(acts[block], w_out[block])
        x = [x[stream] + out[stream * tile : (stream + 1) * tile] for stream in range(4)]
        x[0] = x[0] + bias[1, block][None, :]
    for stream in range(4):
        store(y_own, y_send, stream, x[stream])

    g = [load(4 + stream) for stream in range(4)]
    for block in (1, 0):
        add_bias(2 + block, g[0])
        g_low = jnp.concatenate([part.astype(BF16) for part in g], axis=0)
        value = dot(acts[block], g_low, TN)
        for part in range(2):
            place = 2 * wide + block * wide + part * half
            grads[0, place : place + half, :] += value[:half, part * half : (part + 1) * half]
            grads[1, place : place + half, :] += value[half:, part * half : (part + 1) * half]
        mixed = dot(g_low, w_out_t[block])
        slope = slopes[block]
        total = jnp.zeros((tile, wide), F32)
        lower = []
        for stream in range(1, 4):
            part = mixed[stream * tile : (stream + 1) * tile]
            total = total + part * lin[block, stream - 1]
            lower.append((part * slope).astype(BF16))
        g_pre = (mixed[:tile] * slope + slope * (1.0 - slope) * total).astype(BF16)
        add_bias(block, g_pre.astype(F32))
        stack = jnp.concatenate([g_pre] + lower, axis=0)
        value = dot(x_low[block], stack, TN)
        for part in range(2):
            grads[part, block * wide : (block + 1) * wide, :] += value[:, part * half : (part + 1) * half]
        back = dot(stack, w_in_t[block])
        g = [g[stream] + back[stream * tile : (stream + 1) * tile] for stream in range(4)]
    for stream in range(4):
        store(d_own, d_send, stream, g[stream])

    if final:

        @pl.when(step == rows // tile - 1)
        def _():
            total = jnp.sum(biases[...], axis=1)
            for part in range(2):
                grads[part, 4 * wide : 4 * wide + 4, :] = total[:, part * half : (part + 1) * half]
            flag = who[QUARTER] >> 1
            size = kept.shape[1]
            kept[...] = grads[:, pl.ds(aligned(flag * size), size), :]
            for part in range(2):
                other = grads[part, pl.ds(aligned((1 - flag) * size), size), :]
                sent[part][...] = other.astype(BF16)


def tile_of(rows):
    return max(tile for tile in range(GROUP, 193, GROUP) if rows % tile == 0)


def run_blocks(dims, who, plan, own, got, weights, sums, base, final, merged):
    rows, half = own.shape[1:]
    wide = 2 * half
    tile = tile_of(rows)
    first = sums is None
    piece = pl.BlockSpec((8, tile, half), lambda i: (0, i, 0))

    def whole(array):
        return pl.BlockSpec(
            array.shape, lambda i, rank=len(array.shape): (0,) * rank, pipeline_mode=pl.Buffered(1)
        )

    sum_rows = 4 * wide + dims[3]
    sums_held = [((2, sum_rows, half), F32), ((4, 8, wide), F32)]
    if final:
        results = [((2, sum_rows // 2, half), F32)] + [((sum_rows // 2, half), BF16)] * 2
        scratch = [pltpu.VMEM(*item) for item in sums_held]
    else:
        results, scratch = sums_held, []
    results = [jax.ShapeDtypeStruct(*item) for item in results]
    sizes = (4, 4, 8) if merged else (4, 4, 4, 4)
    out_shapes = [jax.ShapeDtypeStruct((size, rows, half), BF16) for size in sizes]
    out_pieces = [pl.BlockSpec((size, tile, half), lambda i: (0, i, 0)) for size in sizes]
    plans = () if base == 0 else (plan,)
    extra = () if first else sums
    operands = (who, own, got, *weights, *plans, *extra)
    aliases = {}
    if not first and not final:
        aliases = {len(operands) - 2 + i: len(sizes) + i for i in range(2)}
    return pl.pallas_call(
        functools.partial(blocks_kernel, dims, base, rows, tile, first, final, merged),
        grid=(rows // tile,),
        out_shape=out_shapes + results,
        in_specs=[SCALARS]
        + [piece] * 2
        + [whole(item) for item in weights]
        + [SCALARS] * len(plans)
        + [whole(item) for item in extra],
        out_specs=out_pieces + [whole(item) for item in results],
        input_output_aliases=aliases,
        scratch_shapes=scratch
        + [
            pltpu.VMEM((2, 4 * tile, wide), BF16),
            pltpu.VMEM((2, 4 * tile, wide), BF16),
            pltpu.VMEM((2, tile, wide), F32),
            pltpu.VMEM((2, 3, tile, wide), F32),
        ],
        cost_estimate=pl.CostEstimate(
            flops=rows * COST_PER_ROW if base == 0 else 0, bytes_accessed=1024, transcendentals=0
        ),
        compiler_params=PARAMS,
        name="blocks",
    )(*operands)


def swap_tensor(value):
    return lax.ppermute(value, "tensor", [(0, 1), (1, 0)])


def shift(value, order, step):
    pairs = list(zip(order[:-1], order[1:]))
    return lax.ppermute(value, "dp", pairs if step == 1 else [(b, a) for a, b in pairs])


def in_order(flag, mine, other, axis):
    return jnp.where(
        flag == 0, jnp.concatenate([mine, other], axis), jnp.concatenate([other, mine], axis)
    )


def my_quarter():
    place = lax.axis_index("dp")
    return (place & 1) * 2 + ((place >> 1) & 1)


def quarter_kernel(dims, counts, w_in, w_out, who, piece, sems):
    half = w_in.shape[2]
    mine = my_quarter()
    make_who(dims, counts, who)
    for number in range(4):

        @pl.when(mine == number)
        def _(number=number):
            if number < 2:
                copies = [pltpu.make_async_copy(w_in.at[number], piece, sems.at[0])]
            else:
                copies = [
                    pltpu.make_async_copy(
                        w_out.at[number - 2, :, pl.ds(part * half, half)],
                        piece.at[pl.ds(part * half, half)],
                        sems.at[part],
                    )
                    for part in range(2)
                ]
            for copy in copies:
                copy.start()
            for copy in copies:
                copy.wait()


def quarter_of(dims, counts, weight_in, weight_out):
    on_chip = pl.BlockSpec(memory_space=pltpu.VMEM)
    return pl.pallas_call(
        functools.partial(quarter_kernel, dims),
        out_shape=(
            jax.ShapeDtypeStruct((8,), jnp.int32),
            jax.ShapeDtypeStruct(weight_in.shape[1:], BF16),
        ),
        in_specs=[SCALARS] + [on_chip] * 2,
        out_specs=(SCALARS, on_chip),
        scratch_shapes=[pltpu.SemaphoreType.DMA((2,))],
        cost_estimate=NO_COST,
        name="quarter",
    )(counts, weight_in, weight_out)


def assemble_kernel(
    who, w_in, w_out, b_in, b_out, b_got, *refs
):
    pieces, (in_all, out_all, in_turned, out_turned, b_all, held, sems) = refs[:4], refs[4:]
    side, own = who[SIDE], who[QUARTER]
    half = w_in.shape[2]
    copies = [
        pltpu.make_async_copy(piece, held.at[own ^ number], sems.at[number])
        for number, piece in enumerate(pieces)
    ]
    for copy in copies:
        copy.start()
    for copy in copies:
        copy.wait()

    def ordered(mine, other, axis):
        return jnp.where(
            side == 0,
            jnp.concatenate([mine, other], axis),
            jnp.concatenate([other, mine], axis),
        )

    for block in range(2):
        value = ordered(w_in[block], held[block], 1)
        in_all[block] = value
        in_turned[block] = value.T
        other = jnp.concatenate([held[2 + block, :half], held[2 + block, half:]], axis=1)
        value = ordered(w_out[block], other, 0)
        out_all[block] = value
        out_turned[block] = value.T
    for number, mine in enumerate((b_in, b_out)):
        b_all[number] = ordered(mine[...], b_got[number], 1)


def assemble(who, weight_in, weight_out, bias_in, bias_out, bias_got, pieces):
    blocks, wide, half = weight_in.shape
    whole = jax.ShapeDtypeStruct((blocks, wide, wide), BF16)
    on_chip = pl.BlockSpec(memory_space=pltpu.VMEM)
    return pl.pallas_call(
        assemble_kernel,
        out_shape=(whole,) * 4 + (jax.ShapeDtypeStruct((2, blocks, wide), F32),),
        in_specs=[SCALARS] + [on_chip] * 5 + [HBM] * 4,
        out_specs=(on_chip,) * 5,
        scratch_shapes=[pltpu.VMEM((4, wide, half), BF16), pltpu.SemaphoreType.DMA((4,))],
        cost_estimate=NO_COST,
        compiler_params=PARAMS,
        name="assemble",
    )(who, weight_in, weight_out, bias_in, bias_out, bias_got, *pieces)


def flipped(value, flip, size):
    return lax.ppermute(value, "dp", [(i, i ^ flip) for i in range(size)])


def groups_of(bits):
    return [(0, 1), (1, 1)] + [(bit, min(2, bits - bit)) for bit in range(2, bits, 2)]


def reduce_step(grads, group, place, size):
    bit, many = group
    mine = (place >> bit) & ((1 << many) - 1)
    rows = grads.shape[1] >> many
    kept = lax.dynamic_slice_in_dim(grads, mine * rows, rows, 1)
    for flip in range(1, 1 << many):
        sent = lax.dynamic_slice_in_dim(grads, (mine ^ flip) * rows, rows, 1).astype(BF16)
        kept = kept + flipped(sent, flip << bit, size).astype(F32)
    return kept


def join_kernel(mine, *refs):
    parts, (whole, sems) = refs[:-2], refs[-2:]
    rows = parts[0].shape[0]
    copies = [
        pltpu.make_async_copy(
            part, whole.at[pl.ds(aligned((mine[0] ^ flip) * rows), rows)], sems.at[flip]
        )
        for flip, part in enumerate(parts)
    ]
    for copy in copies:
        copy.start()
    for copy in copies:
        copy.wait()


def gather_step(total, group, place, size):
    bit, many = group
    mine = (place >> bit) & ((1 << many) - 1)
    parts = [total] + [flipped(total, flip << bit, size) for flip in range(1, 1 << many)]
    rows, half = total.shape
    return pl.pallas_call(
        join_kernel,
        out_shape=jax.ShapeDtypeStruct((rows << many, half), BF16),
        in_specs=[SCALARS] + [HBM] * len(parts),
        out_specs=pl.BlockSpec(memory_space=pltpu.VMEM),
        scratch_shapes=[pltpu.SemaphoreType.DMA((len(parts),))],
        cost_estimate=NO_COST,
        name="join",
    )(mine.astype(jnp.int32)[None], *parts)


def sum_in_fours(values, step, size):
    flips = (step, 2 * step, 3 * step) if 2 * step < size else (step,)
    return values + sum(
        flipped(values, flip, size) for flip in flips
    )


def finish_kernel(flag, mine, other, grad_in, grad_out, bias_in, bias_out, held, sems):
    rows, half = mine.shape
    copies = [
        pltpu.make_async_copy(part, held.at[pl.ds(aligned(which * rows), rows)], sems.at[number])
        for number, (which, part) in enumerate(((flag[0], mine), (1 - flag[0], other)))
    ]
    for copy in copies:
        copy.start()
    for copy in copies:
        copy.wait()
    wide = 2 * half
    for block in range(2):
        grad_in[block] = held[block * wide : (block + 1) * wide, :].astype(F32)
        for part in range(2):
            first = (2 + block) * wide + part * half
            grad_out[block, :, part * half : (part + 1) * half] = held[first : first + half, :].astype(F32)
    last = held[4 * wide : 4 * wide + GROUP, :].astype(F32)
    bias_in[...] = last[:2]
    bias_out[...] = last[2:4]


def finish(flag, mine, other):
    rows, half = mine.shape
    on_chip = pl.BlockSpec(memory_space=pltpu.VMEM)
    return pl.pallas_call(
        finish_kernel,
        out_shape=(
            jax.ShapeDtypeStruct((2, 2 * half, half), F32),
            jax.ShapeDtypeStruct((2, half, 2 * half), F32),
            jax.ShapeDtypeStruct((2, half), F32),
            jax.ShapeDtypeStruct((2, half), F32),
        ),
        in_specs=[SCALARS] + [HBM] * 2,
        out_specs=(on_chip,) * 4,
        scratch_shapes=[pltpu.VMEM((2 * rows, half), BF16), pltpu.SemaphoreType.DMA((2,))],
        cost_estimate=NO_COST,
        compiler_params=PARAMS,
        name="finish",
    )(flag, mine, other)


def together(*values):
    return lax.optimization_barrier(values)


def local(
    dp_size,
    features,
    tangents,
    weight_in,
    bias_in,
    weight_out,
    bias_out,
    counts,
    cotangent_values,
    cotangent_tangents,
):
    row_count, half = features.shape
    sources = counts.shape[0]
    unit = row_count // 256
    level, first, moved, extra = (unit * part for part in (ROWS, FIRST, MOVED, EXTRA))
    order = chain_order(dp_size)
    bits = dp_size.bit_length() - 1
    dims = (sources, row_count // sources, level, 8 * dp_size)
    side = lax.axis_index("tensor")
    place = lax.axis_index("dp")
    arrays = (features, tangents, cotangent_values, cotangent_tangents)
    middle = (2 * first, level - first - moved)
    last = (2 * (level - moved), moved)

    who, piece = quarter_of(dims, counts, weight_in, weight_out)
    piece_got = swap_tensor(piece)
    bias_got = swap_tensor(jnp.stack([bias_in, bias_out]))
    totals = jnp.where(jnp.arange(dp_size, dtype=jnp.int32) == place, who[TOTAL], 0)
    totals = sum_in_fours(totals, 1, dp_size)
    own1, send1 = pack(dims, who, counts, None, arrays, 0, first)
    send1, piece_got, bias_got = together(send1, piece_got, bias_got)
    got1 = swap_tensor(send1)
    pieces = [piece_got] + [flipped(piece_got, flip, dp_size) for flip in (2, 1, 3)]
    who, own1, totals = together(who, own1, totals)
    own2, send2 = pack(dims, who, counts, None, arrays, *middle)
    got2 = swap_tensor(send2)
    for step in range(2, bits, 2):
        totals = sum_in_fours(totals, 1 << step, dp_size)
    totals, own2 = together(totals, own2)
    plan = make_plan(who, totals, order, level, 2 * first, moved, extra)
    plan, pieces = together(plan, pieces)
    to_left, to_right = export(dims, who, counts, plan, *arrays, moved)
    neighbours = (shift(to_right, order, 1), shift(to_left, order, -1))
    pieces, to_left = together(pieces, to_left)
    weights = assemble(who, weight_in, weight_out, bias_in, bias_out, bias_got, pieces)
    later_counts, weights = together(counts, weights)
    outs = tuple(blank(later_counts, row_count, half, sources))
    who, weights, neighbours, outs = together(who, weights, neighbours, outs)
    own3, send3 = pack(dims, who, counts, plan, arrays, *last, neighbours)
    got3 = swap_tensor(send3)
    own3, weights, got2 = together(own3, weights, got2)

    def blocks(base, plan, arrived, sums, final=False, merged=False):
        results = run_blocks(dims, who, plan, *arrived, weights, sums, base, final, merged)
        count = 3 if merged else 4
        return results[:count], tuple(results[count:])

    def place_all(outs, base, rows, plan, result, got):
        return unpack(dims, who, counts, plan, result[:2], got, outs, base, rows)

    def place_values(outs, base, rows, own, got):
        return (*unpack(dims, who, counts, plan, [own], got, outs[:2], base, rows), *outs[2:])

    def place_grads(outs, base, rows, own, got):
        return (*outs[:2], *unpack(dims, who, counts, plan, [own], got, outs[2:], base, rows))

    result1, sums = blocks(0, plan, (own1, got1), None, merged=True)

    def more(carry):
        return carry[0] < plan[ROUNDS]

    def extra_round(carry):
        number, sums, outs = carry
        done = number * (2 * extra)
        here = plan + jnp.zeros((8,), jnp.int32).at[OVER_FIRST].set(done).at[OVER_LEFT].set(-done)
        own, send = pack(dims, who, counts, here, arrays, OVER, extra)
        result, sums = blocks(OVER, here, (own, swap_tensor(send)), sums, merged=True)
        outs = place_all(outs, OVER, extra, here, result, swap_tensor(result[2]))
        return number + 1, sums, tuple(outs)

    _, sums, outs = lax.while_loop(more, extra_round, (jnp.int32(0), sums, outs))
    result2, sums = blocks(middle[0], plan, (own2, got2), sums, merged=True)
    yd2_got = swap_tensor(result2[2])
    sums, outs = together(sums, outs)
    result3, sums = blocks(last[0], plan, (own3, got3), sums, final=True)
    sums, yd2_got = together(sums, yd2_got)

    kept, *sent = sums
    core, across, *others = groups_of(bits)
    y3_got = swap_tensor(result3[2])
    d3_got = swap_tensor(result3[3])
    came = jnp.stack([flipped(part, 1, dp_size) for part in sent])
    grads = kept + came.astype(F32)
    grads = reduce_step(grads, across, place, dp_size)
    outs = place_all(outs, *middle, plan, result2, yd2_got)
    grads, y3_got, outs = together(grads, y3_got, outs)
    for group in others:
        grads = reduce_step(grads, group, place, dp_size)
    outs = place_values(outs, *last, result3[0], y3_got)
    grads, d3_got, outs = together(grads, d3_got, outs)
    mine = lax.dynamic_index_in_dim(grads, side, 0, keepdims=False)
    other = lax.dynamic_index_in_dim(grads, 1 - side, 0, keepdims=False).astype(BF16)
    total = (mine + swap_tensor(other).astype(F32)).astype(BF16)
    total, yd1_send = together(total, result1[2])
    yd1_got = swap_tensor(yd1_send)
    plan, total = together(plan, total)
    to_left, to_right = handback(
        dims, who, plan, result3[:2], (y3_got, d3_got), *last, moved
    )
    total, to_left = together(total, to_left)
    back = (shift(to_left, order, -1), shift(to_right, order, 1))
    for bit, many in reversed(others):
        for step in range(bit, bit + many):
            total = gather_step(total, (step, 1), place, dp_size)
    outs = place_grads(outs, *last, result3[1], d3_got)
    total, outs = together(total, outs)
    total = gather_step(total, across, place, dp_size)
    outs = unpack(dims, who, counts, plan, back[:1], back[1], outs, None, moved)
    total, outs, yd1_got = together(total, outs, yd1_got)
    total_got = flipped(total, 1, dp_size)
    outs = place_all(outs, 0, first, plan, result1, yd1_got)
    outs, total_got = together(outs, total_got)
    sums = finish((place & 1).astype(jnp.int32)[None], total, total_got)
    grad_in, grad_out, bias_in_grad, bias_out_grad = sums
    return (*outs, grad_in, bias_in_grad, grad_out, bias_out_grad)


def solution(mesh):
    in_specs = (
        P("dp", "tensor"),
        P(None, "dp", "tensor"),
        P(None, None, "tensor"),
        P(None, "tensor"),
        P(None, "tensor", None),
        P(None, "tensor"),
        P("dp"),
        P("dp", "tensor"),
        P(None, "dp", "tensor"),
    )
    out_specs = (
        P("dp", "tensor"),
        P(None, "dp", "tensor"),
        P("dp", "tensor"),
        P(None, "dp", "tensor"),
        P(None, None, "tensor"),
        P(None, "tensor"),
        P(None, "tensor", None),
        P(None, "tensor"),
    )
    return jax.shard_map(
        functools.partial(local, mesh.shape["dp"]),
        mesh=mesh,
        in_specs=in_specs,
        out_specs=out_specs,
        check_vma=False,
    )
```

```python
import functools
import math

import jax
import jax.numpy as jnp
import numpy as np
from jax import lax
from jax.experimental import pallas as pl
from jax.experimental.pallas import tpu as pltpu
from jax.sharding import PartitionSpec as P

LOG_TWO = math.log(2.0)
GROUP = 16
BF16, F32 = jnp.bfloat16, jnp.float32
SCALARS = pl.BlockSpec(memory_space=pltpu.SMEM)
HBM = pl.BlockSpec(memory_space=pltpu.HBM)
MIB = 1 << 20

ROWS, FIRST, MOVED, EXTRA = 79, 36, 28, 8
OVER = -1

PLACE, SIDE, TOTAL, QUARTER, TAILS = range(5)
ROUNDS, OUT_LEFT, IN_LEFT, OUT_RIGHT, IN_RIGHT, KEPT, OVER_FIRST, OVER_LEFT = range(8)


def aligned(value):
    return pl.multiple_of(value, GROUP)


def round_up(count):
    return (count + GROUP - 1) // GROUP * GROUP


NO_COST = pl.CostEstimate(flops=0, bytes_accessed=1024, transcendentals=0)
SOME_COST = pl.CostEstimate(flops=10**10, bytes_accessed=1024, transcendentals=0)
LAST_COST = pl.CostEstimate(flops=2 * 10**10, bytes_accessed=1024, transcendentals=0)
COST_PER_ROW = 7 * 10**7


PARAMS = pltpu.CompilerParams(vmem_limit_bytes=60 * MIB)


def chain_order(size):
    around = (0, 1, 3, 2)
    order = []
    for block in range(size // 4):
        order += [4 * block + i for i in (around if block % 2 == 0 else around[::-1])]
    return order


def plan_kernel(order, most, early, moved, extra, who, totals, plan, flows):
    size = len(order)

    def most_out(total):
        return jnp.clip((total - early) // 2 // GROUP * GROUP, 0, moved)

    def total_of(i):
        return totals[order[i]]

    flow, rounds = jnp.int32(0), jnp.int32(0)
    flows[0] = flow
    for i in range(size):
        here = total_of(i) + flow
        if i + 1 < size:
            flow = jnp.clip(here - most, -most_out(total_of(i + 1)), most_out(total_of(i)))
        else:
            flow = jnp.int32(0)
        flows[i + 1] = flow
        over = jnp.maximum(here - flow - most, 0)
        rounds = jnp.maximum(rounds, (over + extra - 1) // extra)
    place = who[PLACE]
    left, right, total = flows[place], flows[place + 1], who[TOTAL]
    out_left, out_right = jnp.maximum(-left, 0), jnp.maximum(right, 0)
    over = jnp.maximum(total + left - right - most, 0)
    kept = total - out_left - out_right - over
    plan[ROUNDS] = rounds
    plan[OUT_LEFT] = out_left
    plan[IN_LEFT] = jnp.maximum(left, 0)
    plan[OUT_RIGHT] = out_right
    plan[IN_RIGHT] = jnp.maximum(-right, 0)
    plan[KEPT] = kept
    plan[OVER_FIRST] = kept
    plan[OVER_LEFT] = over


def make_plan(who, totals, order, level, early, moved, extra):
    return pl.pallas_call(
        functools.partial(plan_kernel, order, 2 * level, early, moved, 2 * extra),
        out_shape=jax.ShapeDtypeStruct((8,), jnp.int32),
        in_specs=[SCALARS] * 2,
        out_specs=SCALARS,
        scratch_shapes=[pltpu.SMEM((len(order) + 1,), jnp.int32)],
        cost_estimate=NO_COST,
        name="plan",
    )(who, totals)


def own_piece(limit, plan, base, rows):
    if base == OVER:
        first, size = plan[OVER_FIRST], jnp.clip(plan[OVER_LEFT], 0, 2 * rows)
    else:
        first, size = jnp.int32(base), jnp.clip(limit - base, 0, 2 * rows)
    return first, first + size, size


def moved_pieces(dims, plan, base, rows):
    top = 2 * dims[2] - base
    left, right = plan[IN_LEFT], plan[IN_RIGHT]
    return (aligned(top - left - right), aligned(left)), (aligned(top - right), aligned(right))


def sent_pieces(who, plan):
    left, right, total = plan[OUT_LEFT], plan[OUT_RIGHT], who[TOTAL]
    return (total - right - left, total - right, left), (total - right, total, right)


def whole_groups(count):
    return count // GROUP * GROUP


def each_run(dims, who, counts, piece, visit):
    sources, slot = dims[:2]
    first, end = piece[:2]

    def step(source, start):
        after = start + whole_groups(counts[source])
        begin = jnp.maximum(start, first)
        stop = jnp.minimum(after, end)

        @pl.when(stop > begin)
        def _():
            row = source * slot + begin - start
            visit(aligned(row), aligned(begin - first), aligned(stop - begin))

        return after

    lax.fori_loop(0, sources, step, who[TAILS])


def copies_between(held, streams, place, values, tangents, row, size):
    return (
        (values.at[pl.ds(row, size)], held.at[streams, pl.ds(place, size)]),
        (tangents.at[:, pl.ds(row, size)], held.at[pl.ds(streams + 1, 3), pl.ds(place, size)]),
    )


def wait_for(held, streams, size, sem):
    @pl.when(size > 0)
    def _():
        part = held.at[streams, pl.ds(0, aligned(size))]
        pltpu.make_async_copy(part, part, sem).wait()


def each_tail(dims, counts, visit):
    sources, slot = dims[:2]

    def step(source, found):
        left = counts[source] % GROUP
        row = source * slot + jnp.minimum(whole_groups(counts[source]), slot - GROUP)
        visit(source, aligned(row), left)
        return found + jnp.minimum(left, 1)

    return lax.fori_loop(0, sources, step, jnp.int32(0))


def tail_matrix(dims, counts):
    wide = dims[0] * GROUP
    lane = lax.broadcasted_iota(jnp.int32, (8, wide), 1)
    target = jnp.full((8, wide), -1, jnp.int32)
    start = jnp.int32(0)
    for source in range(dims[0]):
        left = counts[source] % GROUP
        row = lane - source * GROUP
        target = jnp.where((row >= 0) & (row < left), start + row, target)
        start = start + left
    number = lax.broadcasted_iota(jnp.int32, (wide, wide), 0)
    return jnp.where(number == target[:1], 1.0, 0.0).astype(BF16)


def make_who(dims, counts, who):
    place = lax.axis_index("dp")
    around = (place & 3) ^ ((place & 3) >> 1)
    back = (place >> 2) & 1
    who[PLACE] = (place >> 2) * 4 + around * (1 - back) + (3 - around) * back
    who[SIDE] = lax.axis_index("tensor")
    who[QUARTER] = my_quarter()

    def step(source, carry):
        whole, left = carry
        return whole + whole_groups(counts[source]), left + counts[source] % GROUP

    whole, left = lax.fori_loop(0, dims[0], step, (jnp.int32(0), jnp.int32(0)))
    left = (left + GROUP - 1) // GROUP * GROUP
    who[TOTAL] = whole + left
    who[TAILS] = left


def start_copies(held, place, sources, row, size, sem):
    for streams, (values, tangents) in zip((0, 4), sources):
        for copy in copies_between(held, streams, place, values, tangents, row, size):
            pltpu.make_async_copy(*copy, sem).start()


def pack_kernel(dims, base, rows, moving, who, counts, *refs):
    plan = None
    if moving or base == OVER:
        plan, *refs = refs
    sources, refs = (refs[:2], refs[2:4]), refs[4:]
    neighbours = ()
    if moving:
        neighbours, refs = refs[:2], refs[2:]
    keep, send, held, sems, *tails = refs
    side = who[SIDE]
    piece = own_piece(plan[KEPT] if moving else who[TOTAL], plan, base, rows)
    size = piece[2]

    if base == 0:
        ends, packed = tails

        def start_tail(source, row, left):
            start_copies(ends, aligned(source * GROUP), sources, row, GROUP, sems.at[1])

        each_tail(dims, counts, start_tail)
        size = size - who[TAILS]

    def start(row, place, size):
        start_copies(held, place, sources, row, size, sems.at[0])

    each_run(dims, who, counts, piece, start)
    arrivals = []
    if moving:
        pieces = moved_pieces(dims, plan, base, rows)
        for number, neighbour in enumerate(neighbours):
            place, moved = pieces[number]
            copy = pltpu.make_async_copy(
                neighbour.at[:, pl.ds(0, moved)], held.at[:, pl.ds(place, moved)], sems.at[1 + number]
            )
            arrivals.append((moved, copy))
        for moved, copy in arrivals:
            pl.when(moved > 0)(copy.start)
    if base == 0:
        matrix = tail_matrix(dims, counts)
        wait_for(ends, slice(0, 8), jnp.int32(dims[0] * GROUP), sems.at[1])
        for stream in range(8):
            packed[stream] = dot(matrix, ends[stream]).astype(BF16)

        def put(group, carry):
            here = pl.ds(aligned(group * GROUP), GROUP)
            held[:, here, :] = packed[:, here, :]
            return carry

        lax.fori_loop(0, who[TAILS] // GROUP, put, 0)
    wait_for(held, slice(0, 8), size, sems.at[0])
    for moved, copy in arrivals:
        pl.when(moved > 0)(copy.wait)
    out = [
        pltpu.make_async_copy(
            held.at[:, pl.ds(aligned(part * rows), rows)], target, sems.at[5 + number]
        )
        for number, (part, target) in enumerate(((1 - side, send), (side, keep)))
    ]
    for copy in out:
        copy.start()
    for copy in out:
        copy.wait()


def pack(dims, who, counts, plan, arrays, base, rows, neighbours=()):
    half = arrays[0].shape[1]
    shape = jax.ShapeDtypeStruct((8, rows, half), BF16)
    plans = (plan,) if neighbours or base == OVER else ()
    tails = [pltpu.VMEM((8, dims[0] * GROUP, half), BF16)] * 2 if base == 0 else []
    return pl.pallas_call(
        functools.partial(pack_kernel, dims, base, rows, len(neighbours) > 0),
        out_shape=(shape, shape),
        in_specs=[SCALARS] * (2 + len(plans)) + [HBM] * (4 + len(neighbours)),
        out_specs=(HBM, HBM),
        scratch_shapes=[pltpu.VMEM((8, 2 * rows, half), BF16), pltpu.SemaphoreType.DMA((7,))] + tails,
        cost_estimate=NO_COST,
        compiler_params=PARAMS,
        name="pack",
    )(who, counts, *plans, *arrays, *neighbours)


def export_kernel(dims, moved, who, counts, plan, x, x3, g, g3, *refs):
    targets, (held, sems) = refs[:2], refs[2:]
    pieces = sent_pieces(who, plan)
    for number, piece in enumerate(pieces):

        def start(row, place, size, number=number):
            place = aligned(number * moved + place)
            start_copies(held, place, ((x, x3), (g, g3)), row, size, sems.at[number])

        @pl.when(piece[2] > 0)
        def _(piece=piece, start=start):
            each_run(dims, who, counts, piece, start)

    for number, piece in enumerate(pieces):
        wait_for(held, slice(0, 8), piece[2], sems.at[number])
    out = [
        pltpu.make_async_copy(
            held.at[:, pl.ds(number * moved, moved)], target, sems.at[2 + number]
        )
        for number, target in enumerate(targets)
    ]
    for copy in out:
        copy.start()
    for copy in out:
        copy.wait()


def export(dims, who, counts, plan, x, x3, g, g3, moved):
    half = x.shape[1]
    return pl.pallas_call(
        functools.partial(export_kernel, dims, moved),
        out_shape=(jax.ShapeDtypeStruct((8, moved, half), BF16),) * 2,
        in_specs=[SCALARS] * 3 + [HBM] * 4,
        out_specs=(HBM,) * 2,
        scratch_shapes=[pltpu.VMEM((8, 2 * moved, half), BF16), pltpu.SemaphoreType.DMA((4,))],
        cost_estimate=NO_COST,
        compiler_params=PARAMS,
        name="export",
    )(who, counts, plan, x, x3, g, g3)


def load_results(held, rows, side, mine, theirs, sems):
    loads = [(0, 1 - side, part) for part in theirs[:1]] + [(4, 1 - side, part) for part in theirs[1:]]
    loads += [(4 * number, side, part) for number, part in enumerate(mine)]
    loads = [
        pltpu.make_async_copy(
            origin,
            held.at[pl.ds(first, origin.shape[0]), pl.ds(aligned(part * rows), rows)],
            sems.at[number],
        )
        for number, (first, part, origin) in enumerate(loads)
    ]
    for load in loads:
        load.start()
    for load in loads:
        load.wait()


def handback_kernel(dims, base, rows, who, plan, *refs):
    mine, theirs, targets, (held, sems) = refs[:2], refs[2:4], refs[4:6], refs[6:]
    load_results(held, rows, who[SIDE], mine, theirs, sems)
    copies = []
    pieces = moved_pieces(dims, plan, base, rows)
    for number, ((place, size), target) in enumerate(zip(pieces, targets)):
        copy = pltpu.make_async_copy(
            held.at[:, pl.ds(place, size)], target.at[:, pl.ds(0, size)], sems.at[4 + number]
        )
        copies.append((size, copy))
    for size, copy in copies:
        pl.when(size > 0)(copy.start)
    for size, copy in copies:
        pl.when(size > 0)(copy.wait)


def handback(dims, who, plan, mine, theirs, base, rows, moved):
    half = mine[0].shape[2]
    shape = jax.ShapeDtypeStruct((8, moved, half), BF16)
    return pl.pallas_call(
        functools.partial(handback_kernel, dims, base, rows),
        out_shape=(shape, shape),
        in_specs=[SCALARS] * 2 + [HBM] * 4,
        out_specs=(HBM, HBM),
        scratch_shapes=[pltpu.VMEM((8, 2 * rows, half), BF16), pltpu.SemaphoreType.DMA((6,))],
        cost_estimate=SOME_COST,
        compiler_params=PARAMS,
        name="handback",
    )(who, plan, *mine, *theirs)


def unpack_kernel(dims, base, rows, streams, parts, who, counts, plan, *refs):
    pairs = streams // 4
    mine, theirs, refs = refs[:parts], refs[parts], refs[parts + 1 :]
    outs, (held, sems, *tails) = refs[2 * pairs : 4 * pairs], refs[4 * pairs :]
    load_results(held, rows, 1 if base is None else who[SIDE], mine, [theirs], sems)
    pieces = sent_pieces(who, plan)
    if base is not None:
        pieces = (own_piece(plan[KEPT], plan, base, rows),)
    sizes = [piece[2] for piece in pieces]
    if base == 0:
        sizes = [sizes[0] - who[TAILS]]

    def start_out(origin, place, row, size, sem):
        for number in range(pairs):
            copies = copies_between(
                origin, 4 * number, place, outs[2 * number], outs[2 * number + 1], row, size
            )
            for there, here in copies:
                pltpu.make_async_copy(here, there, sem).start()

    for number, piece in enumerate(pieces):

        def start(row, place, size, number=number):
            start_out(held, aligned(number * rows + place), row, size, sems.at[3 + number])

        @pl.when(piece[2] > 0)
        def _(piece=piece, start=start):
            each_run(dims, who, counts, piece, start)

    if base == 0:
        (ends,) = tails
        matrix = tail_matrix(dims, counts)
        for stream in range(streams):
            packed = held[stream, : dims[0] * GROUP, :]
            ends[stream] = dot(matrix, packed, TN).astype(BF16)

        def start_tail(source, row, left):
            @pl.when(left > 0)
            def _():
                start_out(ends, aligned(source * GROUP), row, GROUP, sems.at[4])

        found = each_tail(dims, counts, start_tail)
        wait_for(ends, slice(0, streams), found * GROUP, sems.at[4])
    for number, size in enumerate(sizes):
        wait_for(held, slice(0, streams), size, sems.at[3 + number])


def unpack(dims, who, counts, plan, mine, theirs, outs, base, rows):
    half = outs[0].shape[1]
    streams = theirs.shape[0]
    tails = [pltpu.VMEM((streams, dims[0] * GROUP, half), BF16)] if base == 0 else []
    first = 4 + len(mine)
    return pl.pallas_call(
        functools.partial(unpack_kernel, dims, base, rows, streams, len(mine)),
        out_shape=[jax.ShapeDtypeStruct(out.shape, BF16) for out in outs],
        in_specs=[SCALARS] * 3 + [HBM] * (len(mine) + 1 + len(outs)),
        out_specs=[HBM] * len(outs),
        input_output_aliases={first + number: number for number in range(len(outs))},
        scratch_shapes=[
            pltpu.VMEM((streams, 2 * rows, half), BF16),
            pltpu.SemaphoreType.DMA((5,)),
        ]
        + tails,
        cost_estimate=LAST_COST if base == 0 else NO_COST,
        compiler_params=PARAMS,
        name="unpack",
    )(who, counts, plan, *mine, theirs, *outs)


def blank_kernel(sources, slot, counts, values, tangents, other_values, other_tangents, zeros, sem):
    zeros[...] = jnp.zeros_like(zeros)

    def step(source, total):
        padded = round_up(counts[source])
        size = aligned(slot - padded)
        row = aligned(source * slot + padded)

        @pl.when(size > 0)
        def _():
            for low, high in ((values, tangents), (other_values, other_tangents)):
                for here, there in (
                    (zeros.at[0, pl.ds(0, size)], low.at[pl.ds(row, size)]),
                    (zeros.at[:, pl.ds(0, size)], high.at[:, pl.ds(row, size)]),
                ):
                    pltpu.make_async_copy(here, there, sem).start()

        return total + size

    total = lax.fori_loop(0, sources, step, jnp.int32(0))
    for low, high in ((values, tangents), (other_values, other_tangents)):

        @pl.when(total > 0)
        def _():
            low_part, high_part = low.at[pl.ds(0, aligned(total))], high.at[:, pl.ds(0, aligned(total))]
            pltpu.make_async_copy(low_part, low_part, sem).wait()
            pltpu.make_async_copy(high_part, high_part, sem).wait()


def blank(counts, row_count, half, sources):
    slot = row_count // sources
    values = jax.ShapeDtypeStruct((row_count, half), BF16)
    tangents = jax.ShapeDtypeStruct((3, row_count, half), BF16)
    return pl.pallas_call(
        functools.partial(blank_kernel, sources, slot),
        out_shape=(values, tangents, values, tangents),
        in_specs=[SCALARS],
        out_specs=(HBM, HBM, HBM, HBM),
        scratch_shapes=[pltpu.VMEM((3, slot, half), BF16), pltpu.SemaphoreType.DMA],
        cost_estimate=NO_COST,
        compiler_params=PARAMS,
        name="blank",
    )(counts)


NN = (((1,), (0,)), ((), ()))
TN = (((0,), (0,)), ((), ()))


def dot(a, b, dims=NN):
    return lax.dot_general(a, b, dims, preferred_element_type=F32)


def blocks_kernel(
    dims,
    base,
    rows,
    tile,
    first,
    final,
    merged,
    who,
    own,
    got,
    w_in,
    w_out,
    w_in_t,
    w_out_t,
    bias,
    *rest,
):
    if base != 0:
        plan, *rest = rest
    if first:
        grads_before = bias_before = None
    else:
        grads_before, bias_before, *rest = rest
    y_own, d_own, *rest = rest
    if merged:
        send, *rest = rest
        y_send, d_send = send.at[pl.ds(0, 4)], send.at[pl.ds(4, 4)]
    else:
        y_send, d_send, *rest = rest
    if final:
        kept, *rest = rest
        sent, rest = rest[:2], rest[2:]
    grads, biases, x_low, acts, slopes, lin = rest
    step = pl.program_id(0)
    side = who[SIDE]
    wide = w_in.shape[1]
    half = wide // 2

    @pl.when(step == 0)
    def _():
        if first:
            grads[...] = jnp.zeros_like(grads)
            biases[...] = jnp.zeros_like(biases)
        else:
            grads[...] = grads_before[...]
            biases[...] = bias_before[...]

    packed = side * rows + step * tile + lax.broadcasted_iota(jnp.int32, (tile, 128), 0)
    if base == OVER:
        filled = packed < plan[OVER_LEFT]
    elif base == 0:
        filled = packed < who[TOTAL]
    else:
        packed = packed + base
        top = 2 * dims[2] - plan[IN_LEFT] - plan[IN_RIGHT]
        filled = (packed < plan[KEPT]) | (packed >= top)
    filled = jnp.where(filled, 1.0, 0.0)
    is_filled = jnp.concatenate([filled] * (wide // 128), axis=1) > 0.0

    def load(stream):
        mine, theirs = own[stream].astype(F32), got[stream].astype(F32)
        left = jnp.where(side == 0, mine, theirs)
        right = jnp.where(side == 0, theirs, mine)
        return jnp.where(is_filled, jnp.concatenate([left, right], axis=1), 0.0)

    def store(own, send, stream, value):
        left, right = value[:, :half].astype(BF16), value[:, half:].astype(BF16)
        own[stream] = jnp.where(side == 0, left, right)
        send[stream] = jnp.where(side == 0, right, left)

    def add_bias(place, value):
        biases[place] += jnp.sum(value.reshape(tile // 8, 8, wide), axis=0)

    x = [load(stream) for stream in range(4)]
    for block in range(2):
        for stream in range(4):
            x_low[block, stream * tile : (stream + 1) * tile] = x[stream].astype(BF16)
        pre = dot(x_low[block], w_in[block])
        z = pre[:tile] + bias[0, block][None, :]
        small = jnp.exp(-jnp.abs(z))
        whole = 1.0 / (1.0 + small)
        slope = jnp.where(z >= 0.0, whole, small * whole)
        slopes[block] = slope
        acts[block, :tile] = (jnp.maximum(z, 0.0) + jnp.log1p(small) - LOG_TWO).astype(BF16)
        for stream in range(1, 4):
            part = pre[stream * tile : (stream + 1) * tile]
            lin[block, stream - 1] = part
            acts[block, stream * tile : (stream + 1) * tile] = (slope * part).astype(BF16)
        out = dot(acts[block], w_out[block])
        x = [x[stream] + out[stream * tile : (stream + 1) * tile] for stream in range(4)]
        x[0] = x[0] + bias[1, block][None, :]
    for stream in range(4):
        store(y_own, y_send, stream, x[stream])

    g = [load(4 + stream) for stream in range(4)]
    for block in (1, 0):
        add_bias(2 + block, g[0])
        g_low = jnp.concatenate([part.astype(BF16) for part in g], axis=0)
        value = dot(acts[block], g_low, TN)
        for part in range(2):
            place = 2 * wide + block * wide + part * half
            grads[0, place : place + half, :] += value[:half, part * half : (part + 1) * half]
            grads[1, place : place + half, :] += value[half:, part * half : (part + 1) * half]
        mixed = dot(g_low, w_out_t[block])
        slope = slopes[block]
        total = jnp.zeros((tile, wide), F32)
        lower = []
        for stream in range(1, 4):
            part = mixed[stream * tile : (stream + 1) * tile]
            total = total + part * lin[block, stream - 1]
            lower.append((part * slope).astype(BF16))
        g_pre = (mixed[:tile] * slope + slope * (1.0 - slope) * total).astype(BF16)
        add_bias(block, g_pre.astype(F32))
        stack = jnp.concatenate([g_pre] + lower, axis=0)
        value = dot(x_low[block], stack, TN)
        for part in range(2):
            grads[part, block * wide : (block + 1) * wide, :] += value[:, part * half : (part + 1) * half]
        back = dot(stack, w_in_t[block])
        g = [g[stream] + back[stream * tile : (stream + 1) * tile] for stream in range(4)]
    for stream in range(4):
        store(d_own, d_send, stream, g[stream])

    if final:

        @pl.when(step == rows // tile - 1)
        def _():
            total = jnp.sum(biases[...], axis=1)
            for part in range(2):
                grads[part, 4 * wide : 4 * wide + 4, :] = total[:, part * half : (part + 1) * half]
            flag = who[QUARTER] >> 1
            size = kept.shape[1]
            kept[...] = grads[:, pl.ds(aligned(flag * size), size), :]
            for part in range(2):
                other = grads[part, pl.ds(aligned((1 - flag) * size), size), :]
                sent[part][...] = other.astype(BF16)


def tile_of(rows):
    return max(tile for tile in range(GROUP, 193, GROUP) if rows % tile == 0)


def run_blocks(dims, who, plan, own, got, weights, sums, base, final, merged):
    rows, half = own.shape[1:]
    wide = 2 * half
    tile = tile_of(rows)
    first = sums is None
    piece = pl.BlockSpec((8, tile, half), lambda i: (0, i, 0))

    def whole(array):
        return pl.BlockSpec(
            array.shape, lambda i, rank=len(array.shape): (0,) * rank, pipeline_mode=pl.Buffered(1)
        )

    sum_rows = 4 * wide + dims[3]
    sums_held = [((2, sum_rows, half), F32), ((4, 8, wide), F32)]
    if final:
        results = [((2, sum_rows // 2, half), F32)] + [((sum_rows // 2, half), BF16)] * 2
        scratch = [pltpu.VMEM(*item) for item in sums_held]
    else:
        results, scratch = sums_held, []
    results = [jax.ShapeDtypeStruct(*item) for item in results]
    sizes = (4, 4, 8) if merged else (4, 4, 4, 4)
    out_shapes = [jax.ShapeDtypeStruct((size, rows, half), BF16) for size in sizes]
    out_pieces = [pl.BlockSpec((size, tile, half), lambda i: (0, i, 0)) for size in sizes]
    plans = () if base == 0 else (plan,)
    extra = () if first else sums
    operands = (who, own, got, *weights, *plans, *extra)
    aliases = {}
    if not first and not final:
        aliases = {len(operands) - 2 + i: len(sizes) + i for i in range(2)}
    return pl.pallas_call(
        functools.partial(blocks_kernel, dims, base, rows, tile, first, final, merged),
        grid=(rows // tile,),
        out_shape=out_shapes + results,
        in_specs=[SCALARS]
        + [piece] * 2
        + [whole(item) for item in weights]
        + [SCALARS] * len(plans)
        + [whole(item) for item in extra],
        out_specs=out_pieces + [whole(item) for item in results],
        input_output_aliases=aliases,
        scratch_shapes=scratch
        + [
            pltpu.VMEM((2, 4 * tile, wide), BF16),
            pltpu.VMEM((2, 4 * tile, wide), BF16),
            pltpu.VMEM((2, tile, wide), F32),
            pltpu.VMEM((2, 3, tile, wide), F32),
        ],
        cost_estimate=pl.CostEstimate(
            flops=rows * COST_PER_ROW if base == 0 else 0, bytes_accessed=1024, transcendentals=0
        ),
        compiler_params=PARAMS,
        name="blocks",
    )(*operands)


def swap_tensor(value):
    return lax.ppermute(value, "tensor", [(0, 1), (1, 0)])


def shift(value, order, step):
    pairs = list(zip(order[:-1], order[1:]))
    return lax.ppermute(value, "dp", pairs if step == 1 else [(b, a) for a, b in pairs])


def in_order(flag, mine, other, axis):
    return jnp.where(
        flag == 0, jnp.concatenate([mine, other], axis), jnp.concatenate([other, mine], axis)
    )


def my_quarter():
    place = lax.axis_index("dp")
    return (place & 1) * 2 + ((place >> 1) & 1)


def quarter_kernel(dims, counts, w_in, w_out, who, piece, sems):
    half = w_in.shape[2]
    mine = my_quarter()
    make_who(dims, counts, who)
    for number in range(4):

        @pl.when(mine == number)
        def _(number=number):
            if number < 2:
                copies = [pltpu.make_async_copy(w_in.at[number], piece, sems.at[0])]
            else:
                copies = [
                    pltpu.make_async_copy(
                        w_out.at[number - 2, :, pl.ds(part * half, half)],
                        piece.at[pl.ds(part * half, half)],
                        sems.at[part],
                    )
                    for part in range(2)
                ]
            for copy in copies:
                copy.start()
            for copy in copies:
                copy.wait()


def quarter_of(dims, counts, weight_in, weight_out):
    on_chip = pl.BlockSpec(memory_space=pltpu.VMEM)
    return pl.pallas_call(
        functools.partial(quarter_kernel, dims),
        out_shape=(
            jax.ShapeDtypeStruct((8,), jnp.int32),
            jax.ShapeDtypeStruct(weight_in.shape[1:], BF16),
        ),
        in_specs=[SCALARS] + [on_chip] * 2,
        out_specs=(SCALARS, on_chip),
        scratch_shapes=[pltpu.SemaphoreType.DMA((2,))],
        cost_estimate=NO_COST,
        name="quarter",
    )(counts, weight_in, weight_out)


def assemble_kernel(
    who, w_in, w_out, b_in, b_out, b_got, *refs
):
    pieces, (in_all, out_all, in_turned, out_turned, b_all, held, sems) = refs[:4], refs[4:]
    side, own = who[SIDE], who[QUARTER]
    half = w_in.shape[2]
    copies = [
        pltpu.make_async_copy(piece, held.at[own ^ number], sems.at[number])
        for number, piece in enumerate(pieces)
    ]
    for copy in copies:
        copy.start()
    for copy in copies:
        copy.wait()

    def ordered(mine, other, axis):
        return jnp.where(
            side == 0,
            jnp.concatenate([mine, other], axis),
            jnp.concatenate([other, mine], axis),
        )

    for block in range(2):
        value = ordered(w_in[block], held[block], 1)
        in_all[block] = value
        in_turned[block] = value.T
        other = jnp.concatenate([held[2 + block, :half], held[2 + block, half:]], axis=1)
        value = ordered(w_out[block], other, 0)
        out_all[block] = value
        out_turned[block] = value.T
    for number, mine in enumerate((b_in, b_out)):
        b_all[number] = ordered(mine[...], b_got[number], 1)


def assemble(who, weight_in, weight_out, bias_in, bias_out, bias_got, pieces):
    blocks, wide, half = weight_in.shape
    whole = jax.ShapeDtypeStruct((blocks, wide, wide), BF16)
    on_chip = pl.BlockSpec(memory_space=pltpu.VMEM)
    return pl.pallas_call(
        assemble_kernel,
        out_shape=(whole,) * 4 + (jax.ShapeDtypeStruct((2, blocks, wide), F32),),
        in_specs=[SCALARS] + [on_chip] * 5 + [HBM] * 4,
        out_specs=(on_chip,) * 5,
        scratch_shapes=[pltpu.VMEM((4, wide, half), BF16), pltpu.SemaphoreType.DMA((4,))],
        cost_estimate=NO_COST,
        compiler_params=PARAMS,
        name="assemble",
    )(who, weight_in, weight_out, bias_in, bias_out, bias_got, *pieces)


def flipped(value, flip, size):
    return lax.ppermute(value, "dp", [(i, i ^ flip) for i in range(size)])


def groups_of(bits):
    return [(0, 1), (1, 1)] + [(bit, min(2, bits - bit)) for bit in range(2, bits, 2)]


def reduce_step(grads, group, place, size):
    bit, many = group
    mine = (place >> bit) & ((1 << many) - 1)
    rows = grads.shape[1] >> many
    kept = lax.dynamic_slice_in_dim(grads, mine * rows, rows, 1)
    for flip in range(1, 1 << many):
        sent = lax.dynamic_slice_in_dim(grads, (mine ^ flip) * rows, rows, 1).astype(BF16)
        kept = kept + flipped(sent, flip << bit, size).astype(F32)
    return kept


def join_kernel(mine, *refs):
    parts, (whole, sems) = refs[:-2], refs[-2:]
    rows = parts[0].shape[0]
    copies = [
        pltpu.make_async_copy(
            part, whole.at[pl.ds(aligned((mine[0] ^ flip) * rows), rows)], sems.at[flip]
        )
        for flip, part in enumerate(parts)
    ]
    for copy in copies:
        copy.start()
    for copy in copies:
        copy.wait()


def gather_step(total, group, place, size):
    bit, many = group
    mine = (place >> bit) & ((1 << many) - 1)
    parts = [total] + [flipped(total, flip << bit, size) for flip in range(1, 1 << many)]
    rows, half = total.shape
    return pl.pallas_call(
        join_kernel,
        out_shape=jax.ShapeDtypeStruct((rows << many, half), BF16),
        in_specs=[SCALARS] + [HBM] * len(parts),
        out_specs=pl.BlockSpec(memory_space=pltpu.VMEM),
        scratch_shapes=[pltpu.SemaphoreType.DMA((len(parts),))],
        cost_estimate=NO_COST,
        name="join",
    )(mine.astype(jnp.int32)[None], *parts)


def sum_in_fours(values, step, size):
    flips = (step, 2 * step, 3 * step) if 2 * step < size else (step,)
    return values + sum(
        flipped(values, flip, size) for flip in flips
    )


def finish_kernel(flag, mine, other, grad_in, grad_out, bias_in, bias_out, held, sems):
    rows, half = mine.shape
    copies = [
        pltpu.make_async_copy(part, held.at[pl.ds(aligned(which * rows), rows)], sems.at[number])
        for number, (which, part) in enumerate(((flag[0], mine), (1 - flag[0], other)))
    ]
    for copy in copies:
        copy.start()
    for copy in copies:
        copy.wait()
    wide = 2 * half
    for block in range(2):
        grad_in[block] = held[block * wide : (block + 1) * wide, :].astype(F32)
        for part in range(2):
            first = (2 + block) * wide + part * half
            grad_out[block, :, part * half : (part + 1) * half] = held[first : first + half, :].astype(F32)
    last = held[4 * wide : 4 * wide + GROUP, :].astype(F32)
    bias_in[...] = last[:2]
    bias_out[...] = last[2:4]


def finish(flag, mine, other):
    rows, half = mine.shape
    on_chip = pl.BlockSpec(memory_space=pltpu.VMEM)
    return pl.pallas_call(
        finish_kernel,
        out_shape=(
            jax.ShapeDtypeStruct((2, 2 * half, half), F32),
            jax.ShapeDtypeStruct((2, half, 2 * half), F32),
            jax.ShapeDtypeStruct((2, half), F32),
            jax.ShapeDtypeStruct((2, half), F32),
        ),
        in_specs=[SCALARS] + [HBM] * 2,
        out_specs=(on_chip,) * 4,
        scratch_shapes=[pltpu.VMEM((2 * rows, half), BF16), pltpu.SemaphoreType.DMA((2,))],
        cost_estimate=NO_COST,
        compiler_params=PARAMS,
        name="finish",
    )(flag, mine, other)


def together(*values):
    return lax.optimization_barrier(values)


def local(
    dp_size,
    features,
    tangents,
    weight_in,
    bias_in,
    weight_out,
    bias_out,
    counts,
    cotangent_values,
    cotangent_tangents,
):
    row_count, half = features.shape
    sources = counts.shape[0]
    unit = row_count // 256
    level, first, moved, extra = (unit * part for part in (ROWS, FIRST, MOVED, EXTRA))
    order = chain_order(dp_size)
    bits = dp_size.bit_length() - 1
    dims = (sources, row_count // sources, level, 8 * dp_size)
    side = lax.axis_index("tensor")
    place = lax.axis_index("dp")
    arrays = (features, tangents, cotangent_values, cotangent_tangents)
    middle = (2 * first, level - first - moved)
    last = (2 * (level - moved), moved)

    who, piece = quarter_of(dims, counts, weight_in, weight_out)
    piece_got = swap_tensor(piece)
    bias_got = swap_tensor(jnp.stack([bias_in, bias_out]))
    totals = jnp.where(jnp.arange(dp_size, dtype=jnp.int32) == place, who[TOTAL], 0)
    totals = sum_in_fours(totals, 1, dp_size)
    own1, send1 = pack(dims, who, counts, None, arrays, 0, first)
    send1, piece_got, bias_got = together(send1, piece_got, bias_got)
    got1 = swap_tensor(send1)
    pieces = [piece_got] + [flipped(piece_got, flip, dp_size) for flip in (2, 1, 3)]
    who, own1, totals = together(who, own1, totals)
    own2, send2 = pack(dims, who, counts, None, arrays, *middle)
    got2 = swap_tensor(send2)
    for step in range(2, bits, 2):
        totals = sum_in_fours(totals, 1 << step, dp_size)
    totals, own2 = together(totals, own2)
    plan = make_plan(who, totals, order, level, 2 * first, moved, extra)
    plan, pieces = together(plan, pieces)
    to_left, to_right = export(dims, who, counts, plan, *arrays, moved)
    neighbours = (shift(to_right, order, 1), shift(to_left, order, -1))
    pieces, to_left = together(pieces, to_left)
    weights = assemble(who, weight_in, weight_out, bias_in, bias_out, bias_got, pieces)
    later_counts, weights = together(counts, weights)
    outs = tuple(blank(later_counts, row_count, half, sources))
    who, weights, neighbours, outs = together(who, weights, neighbours, outs)
    own3, send3 = pack(dims, who, counts, plan, arrays, *last, neighbours)
    got3 = swap_tensor(send3)
    own3, weights, got2 = together(own3, weights, got2)

    def blocks(base, plan, arrived, sums, final=False, merged=False):
        results = run_blocks(dims, who, plan, *arrived, weights, sums, base, final, merged)
        count = 3 if merged else 4
        return results[:count], tuple(results[count:])

    def place_all(outs, base, rows, plan, result, got):
        return unpack(dims, who, counts, plan, result[:2], got, outs, base, rows)

    def place_values(outs, base, rows, own, got):
        return (*unpack(dims, who, counts, plan, [own], got, outs[:2], base, rows), *outs[2:])

    def place_grads(outs, base, rows, own, got):
        return (*outs[:2], *unpack(dims, who, counts, plan, [own], got, outs[2:], base, rows))

    result1, sums = blocks(0, plan, (own1, got1), None, merged=True)

    def more(carry):
        return carry[0] < plan[ROUNDS]

    def extra_round(carry):
        number, sums, outs = carry
        done = number * (2 * extra)
        here = plan + jnp.zeros((8,), jnp.int32).at[OVER_FIRST].set(done).at[OVER_LEFT].set(-done)
        own, send = pack(dims, who, counts, here, arrays, OVER, extra)
        result, sums = blocks(OVER, here, (own, swap_tensor(send)), sums, merged=True)
        outs = place_all(outs, OVER, extra, here, result, swap_tensor(result[2]))
        return number + 1, sums, tuple(outs)

    _, sums, outs = lax.while_loop(more, extra_round, (jnp.int32(0), sums, outs))
    result2, sums = blocks(middle[0], plan, (own2, got2), sums, merged=True)
    yd2_got = swap_tensor(result2[2])
    sums, outs = together(sums, outs)
    result3, sums = blocks(last[0], plan, (own3, got3), sums, final=True)
    sums, yd2_got = together(sums, yd2_got)

    kept, *sent = sums
    core, across, *others = groups_of(bits)
    y3_got = swap_tensor(result3[2])
    d3_got = swap_tensor(result3[3])
    came = jnp.stack([flipped(part, 1, dp_size) for part in sent])
    grads = kept + came.astype(F32)
    grads = reduce_step(grads, across, place, dp_size)
    outs = place_all(outs, *middle, plan, result2, yd2_got)
    grads, y3_got, outs = together(grads, y3_got, outs)
    for group in others:
        grads = reduce_step(grads, group, place, dp_size)
    outs = place_values(outs, *last, result3[0], y3_got)
    grads, d3_got, outs = together(grads, d3_got, outs)
    mine = lax.dynamic_index_in_dim(grads, side, 0, keepdims=False)
    other = lax.dynamic_index_in_dim(grads, 1 - side, 0, keepdims=False).astype(BF16)
    total = (mine + swap_tensor(other).astype(F32)).astype(BF16)
    total, yd1_send = together(total, result1[2])
    yd1_got = swap_tensor(yd1_send)
    for bit, many in reversed(others):
        for step in range(bit, bit + many):
            total = gather_step(total, (step, 1), place, dp_size)
    plan, total = together(plan, total)
    to_left, to_right = handback(
        dims, who, plan, result3[:2], (y3_got, d3_got), *last, moved
    )
    back = (shift(to_left, order, -1), shift(to_right, order, 1))
    total = gather_step(total, across, place, dp_size)
    total_got = flipped(total, 1, dp_size)
    outs = place_grads(outs, *last, result3[1], d3_got)
    outs = place_all(outs, 0, first, plan, result1, yd1_got)
    sums = finish((place & 1).astype(jnp.int32)[None], total, total_got)
    outs = unpack(dims, who, counts, plan, back[:1], back[1], outs, None, moved)
    grad_in, grad_out, bias_in_grad, bias_out_grad = sums
    return (*outs, grad_in, bias_in_grad, grad_out, bias_out_grad)


def solution(mesh):
    in_specs = (
        P("dp", "tensor"),
        P(None, "dp", "tensor"),
        P(None, None, "tensor"),
        P(None, "tensor"),
        P(None, "tensor", None),
        P(None, "tensor"),
        P("dp"),
        P("dp", "tensor"),
        P(None, "dp", "tensor"),
    )
    out_specs = (
        P("dp", "tensor"),
        P(None, "dp", "tensor"),
        P("dp", "tensor"),
        P(None, "dp", "tensor"),
        P(None, None, "tensor"),
        P(None, "tensor"),
        P(None, "tensor", None),
        P(None, "tensor"),
    )
    return jax.shard_map(
        functools.partial(local, mesh.shape["dp"]),
        mesh=mesh,
        in_specs=in_specs,
        out_specs=out_specs,
        check_vma=False,
    )
```

```python
import functools
import math

import jax
import jax.numpy as jnp
import numpy as np
from jax import lax
from jax.experimental import pallas as pl
from jax.experimental.pallas import tpu as pltpu
from jax.sharding import PartitionSpec as P

LOG_TWO = math.log(2.0)
GROUP = 16
BF16, F32 = jnp.bfloat16, jnp.float32
SCALARS = pl.BlockSpec(memory_space=pltpu.SMEM)
HBM = pl.BlockSpec(memory_space=pltpu.HBM)
MIB = 1 << 20

ROWS, FIRST, MOVED, EXTRA = 79, 36, 28, 8
OVER = -1

PLACE, SIDE, TOTAL, QUARTER, TAILS = range(5)
ROUNDS, OUT_LEFT, IN_LEFT, OUT_RIGHT, IN_RIGHT, KEPT, OVER_FIRST, OVER_LEFT = range(8)


def aligned(value):
    return pl.multiple_of(value, GROUP)


def round_up(count):
    return (count + GROUP - 1) // GROUP * GROUP


NO_COST = pl.CostEstimate(flops=0, bytes_accessed=1024, transcendentals=0)
SOME_COST = pl.CostEstimate(flops=10**10, bytes_accessed=1024, transcendentals=0)
LAST_COST = pl.CostEstimate(flops=2 * 10**10, bytes_accessed=1024, transcendentals=0)
COST_PER_ROW = 7 * 10**7


PARAMS = pltpu.CompilerParams(vmem_limit_bytes=60 * MIB)


def chain_order(size):
    around = (0, 1, 3, 2)
    order = []
    for block in range(size // 4):
        order += [4 * block + i for i in (around if block % 2 == 0 else around[::-1])]
    return order


def plan_kernel(order, most, early, moved, extra, who, totals, plan, flows):
    size = len(order)

    def most_out(total):
        return jnp.clip((total - early) // 2 // GROUP * GROUP, 0, moved)

    def total_of(i):
        return totals[order[i]]

    flow, rounds = jnp.int32(0), jnp.int32(0)
    flows[0] = flow
    for i in range(size):
        here = total_of(i) + flow
        if i + 1 < size:
            flow = jnp.clip(here - most, -most_out(total_of(i + 1)), most_out(total_of(i)))
        else:
            flow = jnp.int32(0)
        flows[i + 1] = flow
        over = jnp.maximum(here - flow - most, 0)
        rounds = jnp.maximum(rounds, (over + extra - 1) // extra)
    place = who[PLACE]
    left, right, total = flows[place], flows[place + 1], who[TOTAL]
    out_left, out_right = jnp.maximum(-left, 0), jnp.maximum(right, 0)
    over = jnp.maximum(total + left - right - most, 0)
    kept = total - out_left - out_right - over
    plan[ROUNDS] = rounds
    plan[OUT_LEFT] = out_left
    plan[IN_LEFT] = jnp.maximum(left, 0)
    plan[OUT_RIGHT] = out_right
    plan[IN_RIGHT] = jnp.maximum(-right, 0)
    plan[KEPT] = kept
    plan[OVER_FIRST] = kept
    plan[OVER_LEFT] = over


def make_plan(who, totals, order, level, early, moved, extra):
    return pl.pallas_call(
        functools.partial(plan_kernel, order, 2 * level, early, moved, 2 * extra),
        out_shape=jax.ShapeDtypeStruct((8,), jnp.int32),
        in_specs=[SCALARS] * 2,
        out_specs=SCALARS,
        scratch_shapes=[pltpu.SMEM((len(order) + 1,), jnp.int32)],
        cost_estimate=NO_COST,
        name="plan",
    )(who, totals)


def own_piece(limit, plan, base, rows):
    if base == OVER:
        first, size = plan[OVER_FIRST], jnp.clip(plan[OVER_LEFT], 0, 2 * rows)
    else:
        first, size = jnp.int32(base), jnp.clip(limit - base, 0, 2 * rows)
    return first, first + size, size


def moved_pieces(dims, plan, base, rows):
    top = 2 * dims[2] - base
    left, right = plan[IN_LEFT], plan[IN_RIGHT]
    at_left = jnp.where(left > 0, top - left - right, 0)
    at_right = jnp.where(right > 0, top - right, 0)
    return (aligned(at_left), aligned(left)), (aligned(at_right), aligned(right))


def sent_pieces(who, plan):
    left, right, total = plan[OUT_LEFT], plan[OUT_RIGHT], who[TOTAL]
    return (total - right - left, total - right, left), (total - right, total, right)


def whole_groups(count):
    return count // GROUP * GROUP


def each_run(dims, who, counts, piece, visit):
    sources, slot = dims[:2]
    first, end = piece[:2]

    def step(source, start):
        after = start + whole_groups(counts[source])
        begin = jnp.maximum(start, first)
        stop = jnp.minimum(after, end)

        @pl.when(stop > begin)
        def _():
            row = source * slot + begin - start
            visit(aligned(row), aligned(begin - first), aligned(stop - begin))

        return after

    lax.fori_loop(0, sources, step, who[TAILS])


def copies_between(held, streams, place, values, tangents, row, size):
    return (
        (values.at[pl.ds(row, size)], held.at[streams, pl.ds(place, size)]),
        (tangents.at[:, pl.ds(row, size)], held.at[pl.ds(streams + 1, 3), pl.ds(place, size)]),
    )


def wait_for(held, streams, size, sem):
    @pl.when(size > 0)
    def _():
        part = held.at[streams, pl.ds(0, aligned(size))]
        pltpu.make_async_copy(part, part, sem).wait()


def each_tail(dims, counts, visit):
    sources, slot = dims[:2]

    def step(source, found):
        left = counts[source] % GROUP
        row = source * slot + jnp.minimum(whole_groups(counts[source]), slot - GROUP)
        visit(source, aligned(row), left)
        return found + jnp.minimum(left, 1)

    return lax.fori_loop(0, sources, step, jnp.int32(0))


def tail_matrix(dims, counts):
    wide = dims[0] * GROUP
    lane = lax.broadcasted_iota(jnp.int32, (8, wide), 1)
    target = jnp.full((8, wide), -1, jnp.int32)
    start = jnp.int32(0)
    for source in range(dims[0]):
        left = counts[source] % GROUP
        row = lane - source * GROUP
        target = jnp.where((row >= 0) & (row < left), start + row, target)
        start = start + left
    number = lax.broadcasted_iota(jnp.int32, (wide, wide), 0)
    return jnp.where(number == target[:1], 1.0, 0.0).astype(BF16)


def make_who(dims, counts, who):
    place = lax.axis_index("dp")
    around = (place & 3) ^ ((place & 3) >> 1)
    back = (place >> 2) & 1
    who[PLACE] = (place >> 2) * 4 + around * (1 - back) + (3 - around) * back
    who[SIDE] = lax.axis_index("tensor")
    who[QUARTER] = my_quarter()

    def step(source, carry):
        whole, left = carry
        return whole + whole_groups(counts[source]), left + counts[source] % GROUP

    whole, left = lax.fori_loop(0, dims[0], step, (jnp.int32(0), jnp.int32(0)))
    left = (left + GROUP - 1) // GROUP * GROUP
    who[TOTAL] = whole + left
    who[TAILS] = left


def start_copies(held, place, sources, row, size, sem):
    for streams, (values, tangents) in zip((0, 4), sources):
        for copy in copies_between(held, streams, place, values, tangents, row, size):
            pltpu.make_async_copy(*copy, sem).start()


def pack_kernel(dims, base, rows, moving, who, counts, *refs):
    plan = None
    if moving or base == OVER:
        plan, *refs = refs
    sources, refs = (refs[:2], refs[2:4]), refs[4:]
    neighbours = ()
    if moving:
        neighbours, refs = refs[:2], refs[2:]
    keep, send, held, sems, *tails = refs
    side = who[SIDE]
    piece = own_piece(plan[KEPT] if moving else who[TOTAL], plan, base, rows)
    size = piece[2]

    if base == 0:
        ends, packed = tails

        def start_tail(source, row, left):
            start_copies(ends, aligned(source * GROUP), sources, row, GROUP, sems.at[1])

        each_tail(dims, counts, start_tail)
        size = size - who[TAILS]

    def start(row, place, size):
        start_copies(held, place, sources, row, size, sems.at[0])

    each_run(dims, who, counts, piece, start)
    arrivals = []
    if moving:
        pieces = moved_pieces(dims, plan, base, rows)
        for number, neighbour in enumerate(neighbours):
            place, moved = pieces[number]
            copy = pltpu.make_async_copy(
                neighbour.at[:, pl.ds(0, moved)], held.at[:, pl.ds(place, moved)], sems.at[1 + number]
            )
            arrivals.append((moved, copy))
        for moved, copy in arrivals:
            pl.when(moved > 0)(copy.start)
    if base == 0:
        matrix = tail_matrix(dims, counts)
        wait_for(ends, slice(0, 8), jnp.int32(dims[0] * GROUP), sems.at[1])
        for stream in range(8):
            packed[stream] = dot(matrix, ends[stream]).astype(BF16)

        def put(group, carry):
            here = pl.ds(aligned(group * GROUP), GROUP)
            held[:, here, :] = packed[:, here, :]
            return carry

        lax.fori_loop(0, who[TAILS] // GROUP, put, 0)
    wait_for(held, slice(0, 8), size, sems.at[0])
    for moved, copy in arrivals:
        pl.when(moved > 0)(copy.wait)
    out = [
        pltpu.make_async_copy(
            held.at[:, pl.ds(aligned(part * rows), rows)], target, sems.at[5 + number]
        )
        for number, (part, target) in enumerate(((1 - side, send), (side, keep)))
    ]
    for copy in out:
        copy.start()
    for copy in out:
        copy.wait()


def pack(dims, who, counts, plan, arrays, base, rows, neighbours=()):
    half = arrays[0].shape[1]
    shape = jax.ShapeDtypeStruct((8, rows, half), BF16)
    plans = (plan,) if neighbours or base == OVER else ()
    tails = [pltpu.VMEM((8, dims[0] * GROUP, half), BF16)] * 2 if base == 0 else []
    return pl.pallas_call(
        functools.partial(pack_kernel, dims, base, rows, len(neighbours) > 0),
        out_shape=(shape, shape),
        in_specs=[SCALARS] * (2 + len(plans)) + [HBM] * (4 + len(neighbours)),
        out_specs=(HBM, HBM),
        scratch_shapes=[pltpu.VMEM((8, 2 * rows, half), BF16), pltpu.SemaphoreType.DMA((7,))] + tails,
        cost_estimate=NO_COST,
        compiler_params=PARAMS,
        name="pack",
    )(who, counts, *plans, *arrays, *neighbours)


def export_kernel(dims, moved, who, counts, plan, x, x3, g, g3, *refs):
    targets, (held, sems) = refs[:2], refs[2:]
    pieces = sent_pieces(who, plan)
    for number, piece in enumerate(pieces):

        def start(row, place, size, number=number):
            place = aligned(number * moved + place)
            start_copies(held, place, ((x, x3), (g, g3)), row, size, sems.at[number])

        @pl.when(piece[2] > 0)
        def _(piece=piece, start=start):
            each_run(dims, who, counts, piece, start)

    for number, piece in enumerate(pieces):
        wait_for(held, slice(0, 8), piece[2], sems.at[number])
    out = [
        pltpu.make_async_copy(
            held.at[:, pl.ds(number * moved, moved)], target, sems.at[2 + number]
        )
        for number, target in enumerate(targets)
    ]
    for copy in out:
        copy.start()
    for copy in out:
        copy.wait()


def export(dims, who, counts, plan, x, x3, g, g3, moved):
    half = x.shape[1]
    return pl.pallas_call(
        functools.partial(export_kernel, dims, moved),
        out_shape=(jax.ShapeDtypeStruct((8, moved, half), BF16),) * 2,
        in_specs=[SCALARS] * 3 + [HBM] * 4,
        out_specs=(HBM,) * 2,
        scratch_shapes=[pltpu.VMEM((8, 2 * moved, half), BF16), pltpu.SemaphoreType.DMA((4,))],
        cost_estimate=NO_COST,
        compiler_params=PARAMS,
        name="export",
    )(who, counts, plan, x, x3, g, g3)


def load_results(held, rows, side, mine, theirs, sems):
    loads = [(0, 1 - side, part) for part in theirs[:1]] + [(4, 1 - side, part) for part in theirs[1:]]
    loads += [(4 * number, side, part) for number, part in enumerate(mine)]
    loads = [
        pltpu.make_async_copy(
            origin,
            held.at[pl.ds(first, origin.shape[0]), pl.ds(aligned(part * rows), rows)],
            sems.at[number],
        )
        for number, (first, part, origin) in enumerate(loads)
    ]
    for load in loads:
        load.start()
    for load in loads:
        load.wait()


def handback_kernel(dims, base, rows, who, plan, *refs):
    mine, theirs, targets, (held, sems) = refs[:2], refs[2:4], refs[4:6], refs[6:]
    load_results(held, rows, who[SIDE], mine, theirs, sems)
    copies = []
    pieces = moved_pieces(dims, plan, base, rows)
    for number, ((place, size), target) in enumerate(zip(pieces, targets)):
        copy = pltpu.make_async_copy(
            held.at[:, pl.ds(place, size)], target.at[:, pl.ds(0, size)], sems.at[4 + number]
        )
        copies.append((size, copy))
    for size, copy in copies:
        pl.when(size > 0)(copy.start)
    for size, copy in copies:
        pl.when(size > 0)(copy.wait)


def handback(dims, who, plan, mine, theirs, base, rows, moved):
    half = mine[0].shape[2]
    shape = jax.ShapeDtypeStruct((8, moved, half), BF16)
    return pl.pallas_call(
        functools.partial(handback_kernel, dims, base, rows),
        out_shape=(shape, shape),
        in_specs=[SCALARS] * 2 + [HBM] * 4,
        out_specs=(HBM, HBM),
        scratch_shapes=[pltpu.VMEM((8, 2 * rows, half), BF16), pltpu.SemaphoreType.DMA((6,))],
        cost_estimate=SOME_COST,
        compiler_params=PARAMS,
        name="handback",
    )(who, plan, *mine, *theirs)


def unpack_kernel(dims, base, rows, streams, parts, who, counts, plan, *refs):
    pairs = streams // 4
    mine, theirs, refs = refs[:parts], refs[parts], refs[parts + 1 :]
    outs, (held, sems, *tails) = refs[2 * pairs : 4 * pairs], refs[4 * pairs :]
    load_results(held, rows, 1 if base is None else who[SIDE], mine, [theirs], sems)
    pieces = sent_pieces(who, plan)
    if base is not None:
        pieces = (own_piece(plan[KEPT], plan, base, rows),)
    sizes = [piece[2] for piece in pieces]
    if base == 0:
        sizes = [sizes[0] - who[TAILS]]

    def start_out(origin, place, row, size, sem):
        for number in range(pairs):
            copies = copies_between(
                origin, 4 * number, place, outs[2 * number], outs[2 * number + 1], row, size
            )
            for there, here in copies:
                pltpu.make_async_copy(here, there, sem).start()

    for number, piece in enumerate(pieces):

        def start(row, place, size, number=number):
            start_out(held, aligned(number * rows + place), row, size, sems.at[3 + number])

        @pl.when(piece[2] > 0)
        def _(piece=piece, start=start):
            each_run(dims, who, counts, piece, start)

    if base == 0:
        (ends,) = tails
        matrix = tail_matrix(dims, counts)
        for stream in range(streams):
            packed = held[stream, : dims[0] * GROUP, :]
            ends[stream] = dot(matrix, packed, TN).astype(BF16)

        def start_tail(source, row, left):
            @pl.when(left > 0)
            def _():
                start_out(ends, aligned(source * GROUP), row, GROUP, sems.at[4])

        found = each_tail(dims, counts, start_tail)
        wait_for(ends, slice(0, streams), found * GROUP, sems.at[4])
    for number, size in enumerate(sizes):
        wait_for(held, slice(0, streams), size, sems.at[3 + number])


def unpack(dims, who, counts, plan, mine, theirs, outs, base, rows):
    half = outs[0].shape[1]
    streams = theirs.shape[0]
    tails = [pltpu.VMEM((streams, dims[0] * GROUP, half), BF16)] if base == 0 else []
    first = 4 + len(mine)
    return pl.pallas_call(
        functools.partial(unpack_kernel, dims, base, rows, streams, len(mine)),
        out_shape=[jax.ShapeDtypeStruct(out.shape, BF16) for out in outs],
        in_specs=[SCALARS] * 3 + [HBM] * (len(mine) + 1 + len(outs)),
        out_specs=[HBM] * len(outs),
        input_output_aliases={first + number: number for number in range(len(outs))},
        scratch_shapes=[
            pltpu.VMEM((streams, 2 * rows, half), BF16),
            pltpu.SemaphoreType.DMA((5,)),
        ]
        + tails,
        cost_estimate=LAST_COST if base == 0 else NO_COST,
        compiler_params=PARAMS,
        name="unpack",
    )(who, counts, plan, *mine, theirs, *outs)


def blank_kernel(sources, slot, counts, values, tangents, other_values, other_tangents, zeros, sem):
    zeros[...] = jnp.zeros_like(zeros)

    def step(source, total):
        padded = round_up(counts[source])
        size = aligned(slot - padded)
        row = aligned(source * slot + padded)

        @pl.when(size > 0)
        def _():
            for low, high in ((values, tangents), (other_values, other_tangents)):
                for here, there in (
                    (zeros.at[0, pl.ds(0, size)], low.at[pl.ds(row, size)]),
                    (zeros.at[:, pl.ds(0, size)], high.at[:, pl.ds(row, size)]),
                ):
                    pltpu.make_async_copy(here, there, sem).start()

        return total + size

    total = lax.fori_loop(0, sources, step, jnp.int32(0))
    for low, high in ((values, tangents), (other_values, other_tangents)):

        @pl.when(total > 0)
        def _():
            low_part, high_part = low.at[pl.ds(0, aligned(total))], high.at[:, pl.ds(0, aligned(total))]
            pltpu.make_async_copy(low_part, low_part, sem).wait()
            pltpu.make_async_copy(high_part, high_part, sem).wait()


def blank(counts, row_count, half, sources):
    slot = row_count // sources
    values = jax.ShapeDtypeStruct((row_count, half), BF16)
    tangents = jax.ShapeDtypeStruct((3, row_count, half), BF16)
    return pl.pallas_call(
        functools.partial(blank_kernel, sources, slot),
        out_shape=(values, tangents, values, tangents),
        in_specs=[SCALARS],
        out_specs=(HBM, HBM, HBM, HBM),
        scratch_shapes=[pltpu.VMEM((3, slot, half), BF16), pltpu.SemaphoreType.DMA],
        cost_estimate=NO_COST,
        compiler_params=PARAMS,
        name="blank",
    )(counts)


NN = (((1,), (0,)), ((), ()))
TN = (((0,), (0,)), ((), ()))


def dot(a, b, dims=NN):
    return lax.dot_general(a, b, dims, preferred_element_type=F32)


def blocks_kernel(
    dims,
    base,
    rows,
    tile,
    first,
    final,
    merged,
    who,
    own,
    got,
    w_in,
    w_out,
    w_in_t,
    w_out_t,
    bias,
    *rest,
):
    if base != 0:
        plan, *rest = rest
    if first:
        grads_before = bias_before = None
    else:
        grads_before, bias_before, *rest = rest
    y_own, d_own, *rest = rest
    if merged:
        send, *rest = rest
        y_send, d_send = send.at[pl.ds(0, 4)], send.at[pl.ds(4, 4)]
    else:
        y_send, d_send, *rest = rest
    if final:
        kept, *rest = rest
        sent, rest = rest[:2], rest[2:]
    grads, biases, x_low, acts, slopes, lin = rest
    step = pl.program_id(0)
    side = who[SIDE]
    wide = w_in.shape[1]
    half = wide // 2

    @pl.when(step == 0)
    def _():
        if first:
            grads[...] = jnp.zeros_like(grads)
            biases[...] = jnp.zeros_like(biases)
        else:
            grads[...] = grads_before[...]
            biases[...] = bias_before[...]

    packed = side * rows + step * tile + lax.broadcasted_iota(jnp.int32, (tile, 128), 0)
    if base == OVER:
        filled = packed < plan[OVER_LEFT]
    elif base == 0:
        filled = packed < who[TOTAL]
    else:
        packed = packed + base
        top = 2 * dims[2] - plan[IN_LEFT] - plan[IN_RIGHT]
        filled = (packed < plan[KEPT]) | (packed >= top)
    filled = jnp.where(filled, 1.0, 0.0)
    is_filled = jnp.concatenate([filled] * (wide // 128), axis=1) > 0.0

    def load(stream):
        mine, theirs = own[stream].astype(F32), got[stream].astype(F32)
        left = jnp.where(side == 0, mine, theirs)
        right = jnp.where(side == 0, theirs, mine)
        return jnp.where(is_filled, jnp.concatenate([left, right], axis=1), 0.0)

    def store(own, send, stream, value):
        left, right = value[:, :half].astype(BF16), value[:, half:].astype(BF16)
        own[stream] = jnp.where(side == 0, left, right)
        send[stream] = jnp.where(side == 0, right, left)

    def add_bias(place, value):
        biases[place] += jnp.sum(value.reshape(tile // 8, 8, wide), axis=0)

    x = [load(stream) for stream in range(4)]
    for block in range(2):
        for stream in range(4):
            x_low[block, stream * tile : (stream + 1) * tile] = x[stream].astype(BF16)
        pre = dot(x_low[block], w_in[block])
        z = pre[:tile] + bias[0, block][None, :]
        small = jnp.exp(-jnp.abs(z))
        whole = 1.0 / (1.0 + small)
        slope = jnp.where(z >= 0.0, whole, small * whole)
        slopes[block] = slope
        acts[block, :tile] = (jnp.maximum(z, 0.0) + jnp.log1p(small) - LOG_TWO).astype(BF16)
        for stream in range(1, 4):
            part = pre[stream * tile : (stream + 1) * tile]
            lin[block, stream - 1] = part
            acts[block, stream * tile : (stream + 1) * tile] = (slope * part).astype(BF16)
        out = dot(acts[block], w_out[block])
        x = [x[stream] + out[stream * tile : (stream + 1) * tile] for stream in range(4)]
        x[0] = x[0] + bias[1, block][None, :]
    for stream in range(4):
        store(y_own, y_send, stream, x[stream])

    g = [load(4 + stream) for stream in range(4)]
    for block in (1, 0):
        add_bias(2 + block, g[0])
        g_low = jnp.concatenate([part.astype(BF16) for part in g], axis=0)
        value = dot(acts[block], g_low, TN)
        for part in range(2):
            place = 2 * wide + block * wide + part * half
            grads[0, place : place + half, :] += value[:half, part * half : (part + 1) * half]
            grads[1, place : place + half, :] += value[half:, part * half : (part + 1) * half]
        mixed = dot(g_low, w_out_t[block])
        slope = slopes[block]
        total = jnp.zeros((tile, wide), F32)
        lower = []
        for stream in range(1, 4):
            part = mixed[stream * tile : (stream + 1) * tile]
            total = total + part * lin[block, stream - 1]
            lower.append((part * slope).astype(BF16))
        g_pre = (mixed[:tile] * slope + slope * (1.0 - slope) * total).astype(BF16)
        add_bias(block, g_pre.astype(F32))
        stack = jnp.concatenate([g_pre] + lower, axis=0)
        value = dot(x_low[block], stack, TN)
        for part in range(2):
            grads[part, block * wide : (block + 1) * wide, :] += value[:, part * half : (part + 1) * half]
        back = dot(stack, w_in_t[block])
        g = [g[stream] + back[stream * tile : (stream + 1) * tile] for stream in range(4)]
    for stream in range(4):
        store(d_own, d_send, stream, g[stream])

    if final:

        @pl.when(step == rows // tile - 1)
        def _():
            total = jnp.sum(biases[...], axis=1)
            for part in range(2):
                grads[part, 4 * wide : 4 * wide + 4, :] = total[:, part * half : (part + 1) * half]
            flag = who[QUARTER] >> 1
            size = kept.shape[1]
            kept[...] = grads[:, pl.ds(aligned(flag * size), size), :]
            for part in range(2):
                other = grads[part, pl.ds(aligned((1 - flag) * size), size), :]
                sent[part][...] = other.astype(BF16)


def tile_of(rows):
    return max(tile for tile in range(GROUP, 193, GROUP) if rows % tile == 0)


def run_blocks(dims, who, plan, own, got, weights, sums, base, final, merged):
    rows, half = own.shape[1:]
    wide = 2 * half
    tile = tile_of(rows)
    first = sums is None
    piece = pl.BlockSpec((8, tile, half), lambda i: (0, i, 0))

    def whole(array):
        return pl.BlockSpec(
            array.shape, lambda i, rank=len(array.shape): (0,) * rank, pipeline_mode=pl.Buffered(1)
        )

    sum_rows = 4 * wide + dims[3]
    sums_held = [((2, sum_rows, half), F32), ((4, 8, wide), F32)]
    if final:
        results = [((2, sum_rows // 2, half), F32)] + [((sum_rows // 2, half), BF16)] * 2
        scratch = [pltpu.VMEM(*item) for item in sums_held]
    else:
        results, scratch = sums_held, []
    results = [jax.ShapeDtypeStruct(*item) for item in results]
    sizes = (4, 4, 8) if merged else (4, 4, 4, 4)
    out_shapes = [jax.ShapeDtypeStruct((size, rows, half), BF16) for size in sizes]
    out_pieces = [pl.BlockSpec((size, tile, half), lambda i: (0, i, 0)) for size in sizes]
    plans = () if base == 0 else (plan,)
    extra = () if first else sums
    operands = (who, own, got, *weights, *plans, *extra)
    aliases = {}
    if not first and not final:
        aliases = {len(operands) - 2 + i: len(sizes) + i for i in range(2)}
    return pl.pallas_call(
        functools.partial(blocks_kernel, dims, base, rows, tile, first, final, merged),
        grid=(rows // tile,),
        out_shape=out_shapes + results,
        in_specs=[SCALARS]
        + [piece] * 2
        + [whole(item) for item in weights]
        + [SCALARS] * len(plans)
        + [whole(item) for item in extra],
        out_specs=out_pieces + [whole(item) for item in results],
        input_output_aliases=aliases,
        scratch_shapes=scratch
        + [
            pltpu.VMEM((2, 4 * tile, wide), BF16),
            pltpu.VMEM((2, 4 * tile, wide), BF16),
            pltpu.VMEM((2, tile, wide), F32),
            pltpu.VMEM((2, 3, tile, wide), F32),
        ],
        cost_estimate=pl.CostEstimate(
            flops=rows * COST_PER_ROW if base == 0 else 0, bytes_accessed=1024, transcendentals=0
        ),
        compiler_params=PARAMS,
        name="blocks",
    )(*operands)


def swap_tensor(value):
    return lax.ppermute(value, "tensor", [(0, 1), (1, 0)])


def shift(value, order, step):
    pairs = list(zip(order[:-1], order[1:]))
    return lax.ppermute(value, "dp", pairs if step == 1 else [(b, a) for a, b in pairs])


def in_order(flag, mine, other, axis):
    return jnp.where(
        flag == 0, jnp.concatenate([mine, other], axis), jnp.concatenate([other, mine], axis)
    )


def my_quarter():
    place = lax.axis_index("dp")
    return (place & 1) * 2 + ((place >> 1) & 1)


def quarter_kernel(dims, counts, w_in, w_out, who, piece, sems):
    half = w_in.shape[2]
    mine = my_quarter()
    make_who(dims, counts, who)
    for number in range(4):

        @pl.when(mine == number)
        def _(number=number):
            if number < 2:
                copies = [pltpu.make_async_copy(w_in.at[number], piece, sems.at[0])]
            else:
                copies = [
                    pltpu.make_async_copy(
                        w_out.at[number - 2, :, pl.ds(part * half, half)],
                        piece.at[pl.ds(part * half, half)],
                        sems.at[part],
                    )
                    for part in range(2)
                ]
            for copy in copies:
                copy.start()
            for copy in copies:
                copy.wait()


def quarter_of(dims, counts, weight_in, weight_out):
    on_chip = pl.BlockSpec(memory_space=pltpu.VMEM)
    return pl.pallas_call(
        functools.partial(quarter_kernel, dims),
        out_shape=(
            jax.ShapeDtypeStruct((8,), jnp.int32),
            jax.ShapeDtypeStruct(weight_in.shape[1:], BF16),
        ),
        in_specs=[SCALARS] + [on_chip] * 2,
        out_specs=(SCALARS, on_chip),
        scratch_shapes=[pltpu.SemaphoreType.DMA((2,))],
        cost_estimate=NO_COST,
        name="quarter",
    )(counts, weight_in, weight_out)


def assemble_kernel(
    who, w_in, w_out, b_in, b_out, b_got, *refs
):
    pieces, (in_all, out_all, in_turned, out_turned, b_all, held, sems) = refs[:4], refs[4:]
    side, own = who[SIDE], who[QUARTER]
    half = w_in.shape[2]
    copies = [
        pltpu.make_async_copy(piece, held.at[own ^ number], sems.at[number])
        for number, piece in enumerate(pieces)
    ]
    for copy in copies:
        copy.start()
    for copy in copies:
        copy.wait()

    def ordered(mine, other, axis):
        return jnp.where(
            side == 0,
            jnp.concatenate([mine, other], axis),
            jnp.concatenate([other, mine], axis),
        )

    for block in range(2):
        value = ordered(w_in[block], held[block], 1)
        in_all[block] = value
        in_turned[block] = value.T
        other = jnp.concatenate([held[2 + block, :half], held[2 + block, half:]], axis=1)
        value = ordered(w_out[block], other, 0)
        out_all[block] = value
        out_turned[block] = value.T
    for number, mine in enumerate((b_in, b_out)):
        b_all[number] = ordered(mine[...], b_got[number], 1)


def assemble(who, weight_in, weight_out, bias_in, bias_out, bias_got, pieces):
    blocks, wide, half = weight_in.shape
    whole = jax.ShapeDtypeStruct((blocks, wide, wide), BF16)
    on_chip = pl.BlockSpec(memory_space=pltpu.VMEM)
    return pl.pallas_call(
        assemble_kernel,
        out_shape=(whole,) * 4 + (jax.ShapeDtypeStruct((2, blocks, wide), F32),),
        in_specs=[SCALARS] + [on_chip] * 5 + [HBM] * 4,
        out_specs=(on_chip,) * 5,
        scratch_shapes=[pltpu.VMEM((4, wide, half), BF16), pltpu.SemaphoreType.DMA((4,))],
        cost_estimate=NO_COST,
        compiler_params=PARAMS,
        name="assemble",
    )(who, weight_in, weight_out, bias_in, bias_out, bias_got, *pieces)


def flipped(value, flip, size):
    return lax.ppermute(value, "dp", [(i, i ^ flip) for i in range(size)])


def groups_of(bits):
    return [(0, 1), (1, 1)] + [(bit, min(2, bits - bit)) for bit in range(2, bits, 2)]


def reduce_step(grads, group, place, size):
    bit, many = group
    mine = (place >> bit) & ((1 << many) - 1)
    rows = grads.shape[1] >> many
    kept = lax.dynamic_slice_in_dim(grads, mine * rows, rows, 1)
    for flip in range(1, 1 << many):
        sent = lax.dynamic_slice_in_dim(grads, (mine ^ flip) * rows, rows, 1).astype(BF16)
        kept = kept + flipped(sent, flip << bit, size).astype(F32)
    return kept


def join_kernel(mine, *refs):
    parts, (whole, sems) = refs[:-2], refs[-2:]
    rows = parts[0].shape[0]
    copies = [
        pltpu.make_async_copy(
            part, whole.at[pl.ds(aligned((mine[0] ^ flip) * rows), rows)], sems.at[flip]
        )
        for flip, part in enumerate(parts)
    ]
    for copy in copies:
        copy.start()
    for copy in copies:
        copy.wait()


def gather_step(total, group, place, size):
    bit, many = group
    mine = (place >> bit) & ((1 << many) - 1)
    parts = [total] + [flipped(total, flip << bit, size) for flip in range(1, 1 << many)]
    rows, half = total.shape
    return pl.pallas_call(
        join_kernel,
        out_shape=jax.ShapeDtypeStruct((rows << many, half), BF16),
        in_specs=[SCALARS] + [HBM] * len(parts),
        out_specs=pl.BlockSpec(memory_space=pltpu.VMEM),
        scratch_shapes=[pltpu.SemaphoreType.DMA((len(parts),))],
        cost_estimate=NO_COST,
        name="join",
    )(mine.astype(jnp.int32)[None], *parts)


def sum_in_fours(values, step, size):
    flips = (step, 2 * step, 3 * step) if 2 * step < size else (step,)
    return values + sum(
        flipped(values, flip, size) for flip in flips
    )


def finish_kernel(flag, mine, other, grad_in, grad_out, bias_in, bias_out, held, sems):
    rows, half = mine.shape
    copies = [
        pltpu.make_async_copy(part, held.at[pl.ds(aligned(which * rows), rows)], sems.at[number])
        for number, (which, part) in enumerate(((flag[0], mine), (1 - flag[0], other)))
    ]
    for copy in copies:
        copy.start()
    for copy in copies:
        copy.wait()
    wide = 2 * half
    for block in range(2):
        grad_in[block] = held[block * wide : (block + 1) * wide, :].astype(F32)
        for part in range(2):
            first = (2 + block) * wide + part * half
            grad_out[block, :, part * half : (part + 1) * half] = held[first : first + half, :].astype(F32)
    last = held[4 * wide : 4 * wide + GROUP, :].astype(F32)
    bias_in[...] = last[:2]
    bias_out[...] = last[2:4]


def finish(flag, mine, other):
    rows, half = mine.shape
    on_chip = pl.BlockSpec(memory_space=pltpu.VMEM)
    return pl.pallas_call(
        finish_kernel,
        out_shape=(
            jax.ShapeDtypeStruct((2, 2 * half, half), F32),
            jax.ShapeDtypeStruct((2, half, 2 * half), F32),
            jax.ShapeDtypeStruct((2, half), F32),
            jax.ShapeDtypeStruct((2, half), F32),
        ),
        in_specs=[SCALARS] + [HBM] * 2,
        out_specs=(on_chip,) * 4,
        scratch_shapes=[pltpu.VMEM((2 * rows, half), BF16), pltpu.SemaphoreType.DMA((2,))],
        cost_estimate=NO_COST,
        compiler_params=PARAMS,
        name="finish",
    )(flag, mine, other)


def together(*values):
    return lax.optimization_barrier(values)


def local(
    dp_size,
    features,
    tangents,
    weight_in,
    bias_in,
    weight_out,
    bias_out,
    counts,
    cotangent_values,
    cotangent_tangents,
):
    row_count, half = features.shape
    sources = counts.shape[0]
    unit = row_count // 256
    level, first, moved, extra = (unit * part for part in (ROWS, FIRST, MOVED, EXTRA))
    order = chain_order(dp_size)
    bits = dp_size.bit_length() - 1
    dims = (sources, row_count // sources, level, 8 * dp_size)
    side = lax.axis_index("tensor")
    place = lax.axis_index("dp")
    arrays = (features, tangents, cotangent_values, cotangent_tangents)
    middle = (2 * first, level - first - moved)
    last = (2 * (level - moved), moved)

    who, piece = quarter_of(dims, counts, weight_in, weight_out)
    piece_got = swap_tensor(piece)
    bias_got = swap_tensor(jnp.stack([bias_in, bias_out]))
    totals = jnp.where(jnp.arange(dp_size, dtype=jnp.int32) == place, who[TOTAL], 0)
    totals = sum_in_fours(totals, 1, dp_size)
    own1, send1 = pack(dims, who, counts, None, arrays, 0, first)
    send1, piece_got, bias_got = together(send1, piece_got, bias_got)
    got1 = swap_tensor(send1)
    pieces = [piece_got] + [flipped(piece_got, flip, dp_size) for flip in (2, 1, 3)]
    who, own1, totals = together(who, own1, totals)
    own2, send2 = pack(dims, who, counts, None, arrays, *middle)
    got2 = swap_tensor(send2)
    for step in range(2, bits, 2):
        totals = sum_in_fours(totals, 1 << step, dp_size)
    totals, own2 = together(totals, own2)
    plan = make_plan(who, totals, order, level, 2 * first, moved, extra)
    plan, pieces = together(plan, pieces)
    to_left, to_right = export(dims, who, counts, plan, *arrays, moved)
    neighbours = (shift(to_right, order, 1), shift(to_left, order, -1))
    pieces, to_left = together(pieces, to_left)
    weights = assemble(who, weight_in, weight_out, bias_in, bias_out, bias_got, pieces)
    later_counts, weights = together(counts, weights)
    outs = tuple(blank(later_counts, row_count, half, sources))
    who, weights, neighbours, outs = together(who, weights, neighbours, outs)
    own3, send3 = pack(dims, who, counts, plan, arrays, *last, neighbours)
    got3 = swap_tensor(send3)
    own3, weights, got2 = together(own3, weights, got2)

    def blocks(base, plan, arrived, sums, final=False, merged=False):
        results = run_blocks(dims, who, plan, *arrived, weights, sums, base, final, merged)
        count = 3 if merged else 4
        return results[:count], tuple(results[count:])

    def place_all(outs, base, rows, plan, result, got):
        return unpack(dims, who, counts, plan, result[:2], got, outs, base, rows)

    def place_values(outs, base, rows, own, got):
        return (*unpack(dims, who, counts, plan, [own], got, outs[:2], base, rows), *outs[2:])

    def place_grads(outs, base, rows, own, got):
        return (*outs[:2], *unpack(dims, who, counts, plan, [own], got, outs[2:], base, rows))

    result1, sums = blocks(0, plan, (own1, got1), None, merged=True)

    def more(carry):
        return carry[0] < plan[ROUNDS]

    def extra_round(carry):
        number, sums, outs = carry
        done = number * (2 * extra)
        here = plan + jnp.zeros((8,), jnp.int32).at[OVER_FIRST].set(done).at[OVER_LEFT].set(-done)
        own, send = pack(dims, who, counts, here, arrays, OVER, extra)
        result, sums = blocks(OVER, here, (own, swap_tensor(send)), sums, merged=True)
        outs = place_all(outs, OVER, extra, here, result, swap_tensor(result[2]))
        return number + 1, sums, tuple(outs)

    _, sums, outs = lax.while_loop(more, extra_round, (jnp.int32(0), sums, outs))
    result2, sums = blocks(middle[0], plan, (own2, got2), sums, merged=True)
    yd2_got = swap_tensor(result2[2])
    sums, outs = together(sums, outs)
    result3, sums = blocks(last[0], plan, (own3, got3), sums, final=True)
    sums, yd2_got = together(sums, yd2_got)

    kept, *sent = sums
    core, across, *others = groups_of(bits)
    y3_got = swap_tensor(result3[2])
    d3_got = swap_tensor(result3[3])
    came = jnp.stack([flipped(part, 1, dp_size) for part in sent])
    grads = kept + came.astype(F32)
    grads = reduce_step(grads, across, place, dp_size)
    outs = place_all(outs, *middle, plan, result2, yd2_got)
    grads, y3_got, outs = together(grads, y3_got, outs)
    for group in others:
        grads = reduce_step(grads, group, place, dp_size)
    outs = place_values(outs, *last, result3[0], y3_got)
    grads, d3_got, outs = together(grads, d3_got, outs)
    mine = lax.dynamic_index_in_dim(grads, side, 0, keepdims=False)
    other = lax.dynamic_index_in_dim(grads, 1 - side, 0, keepdims=False).astype(BF16)
    total = (mine + swap_tensor(other).astype(F32)).astype(BF16)
    total, yd1_send = together(total, result1[2])
    yd1_got = swap_tensor(yd1_send)
    for bit, many in reversed(others):
        for step in range(bit, bit + many):
            total = gather_step(total, (step, 1), place, dp_size)
    plan, total = together(plan, total)
    to_left, to_right = handback(
        dims, who, plan, result3[:2], (y3_got, d3_got), *last, moved
    )
    back = (shift(to_left, order, -1), shift(to_right, order, 1))
    total = gather_step(total, across, place, dp_size)
    total_got = flipped(total, 1, dp_size)
    outs = place_grads(outs, *last, result3[1], d3_got)
    outs = place_all(outs, 0, first, plan, result1, yd1_got)
    sums = finish((place & 1).astype(jnp.int32)[None], total, total_got)
    outs = unpack(dims, who, counts, plan, back[:1], back[1], outs, None, moved)
    grad_in, grad_out, bias_in_grad, bias_out_grad = sums
    return (*outs, grad_in, bias_in_grad, grad_out, bias_out_grad)


def solution(mesh):
    in_specs = (
        P("dp", "tensor"),
        P(None, "dp", "tensor"),
        P(None, None, "tensor"),
        P(None, "tensor"),
        P(None, "tensor", None),
        P(None, "tensor"),
        P("dp"),
        P("dp", "tensor"),
        P(None, "dp", "tensor"),
    )
    out_specs = (
        P("dp", "tensor"),
        P(None, "dp", "tensor"),
        P("dp", "tensor"),
        P(None, "dp", "tensor"),
        P(None, None, "tensor"),
        P(None, "tensor"),
        P(None, "tensor", None),
        P(None, "tensor"),
    )
    return jax.shard_map(
        functools.partial(local, mesh.shape["dp"]),
        mesh=mesh,
        in_specs=in_specs,
        out_specs=out_specs,
        check_vma=False,
    )
```

```python
import functools
import math

import jax
import jax.numpy as jnp
import numpy as np
from jax import lax
from jax.experimental import pallas as pl
from jax.experimental.pallas import tpu as pltpu
from jax.sharding import PartitionSpec as P

LOG_TWO = math.log(2.0)
GROUP = 16
BF16, F32 = jnp.bfloat16, jnp.float32
SCALARS = pl.BlockSpec(memory_space=pltpu.SMEM)
HBM = pl.BlockSpec(memory_space=pltpu.HBM)
MIB = 1 << 20

ROWS, FIRST, MOVED, EXTRA = 79, 36, 28, 8
OVER = -1

PLACE, SIDE, TOTAL, QUARTER, TAILS = range(5)
ROUNDS, OUT_LEFT, IN_LEFT, OUT_RIGHT, IN_RIGHT, KEPT, OVER_FIRST, OVER_LEFT = range(8)


def aligned(value):
    return pl.multiple_of(value, GROUP)


def round_up(count):
    return (count + GROUP - 1) // GROUP * GROUP


NO_COST = pl.CostEstimate(flops=0, bytes_accessed=1024, transcendentals=0)
SOME_COST = pl.CostEstimate(flops=10**10, bytes_accessed=1024, transcendentals=0)
LAST_COST = pl.CostEstimate(flops=2 * 10**10, bytes_accessed=1024, transcendentals=0)
COST_PER_ROW = 7 * 10**7


PARAMS = pltpu.CompilerParams(vmem_limit_bytes=60 * MIB)


def chain_order(size):
    around = (0, 1, 3, 2)
    order = []
    for block in range(size // 4):
        order += [4 * block + i for i in (around if block % 2 == 0 else around[::-1])]
    return order


def plan_kernel(order, most, early, moved, extra, who, totals, plan, flows):
    size = len(order)

    def most_out(total):
        return jnp.clip((total - early) // 2 // GROUP * GROUP, 0, moved)

    def total_of(i):
        return totals[order[i]]

    flow, rounds = jnp.int32(0), jnp.int32(0)
    flows[0] = flow
    for i in range(size):
        here = total_of(i) + flow
        if i + 1 < size:
            flow = jnp.clip(here - most, -most_out(total_of(i + 1)), most_out(total_of(i)))
        else:
            flow = jnp.int32(0)
        flows[i + 1] = flow
        over = jnp.maximum(here - flow - most, 0)
        rounds = jnp.maximum(rounds, (over + extra - 1) // extra)
    place = who[PLACE]
    left, right, total = flows[place], flows[place + 1], who[TOTAL]
    out_left, out_right = jnp.maximum(-left, 0), jnp.maximum(right, 0)
    over = jnp.maximum(total + left - right - most, 0)
    kept = total - out_left - out_right - over
    plan[ROUNDS] = rounds
    plan[OUT_LEFT] = out_left
    plan[IN_LEFT] = jnp.maximum(left, 0)
    plan[OUT_RIGHT] = out_right
    plan[IN_RIGHT] = jnp.maximum(-right, 0)
    plan[KEPT] = kept
    plan[OVER_FIRST] = kept
    plan[OVER_LEFT] = over


def make_plan(who, totals, order, level, early, moved, extra):
    return pl.pallas_call(
        functools.partial(plan_kernel, order, 2 * level, early, moved, 2 * extra),
        out_shape=jax.ShapeDtypeStruct((8,), jnp.int32),
        in_specs=[SCALARS] * 2,
        out_specs=SCALARS,
        scratch_shapes=[pltpu.SMEM((len(order) + 1,), jnp.int32)],
        cost_estimate=NO_COST,
        name="plan",
    )(who, totals)


def own_piece(limit, plan, base, rows):
    if base == OVER:
        first, size = plan[OVER_FIRST], jnp.clip(plan[OVER_LEFT], 0, 2 * rows)
    else:
        first, size = jnp.int32(base), jnp.clip(limit - base, 0, 2 * rows)
    return first, first + size, size


def moved_pieces(dims, plan, base, rows):
    top = 2 * dims[2] - base
    left, right = plan[IN_LEFT], plan[IN_RIGHT]
    at_left = jnp.where(left > 0, top - left - right, 0)
    at_right = jnp.where(right > 0, top - right, 0)
    return (aligned(at_left), aligned(left)), (aligned(at_right), aligned(right))


def sent_pieces(who, plan):
    left, right, total = plan[OUT_LEFT], plan[OUT_RIGHT], who[TOTAL]
    return (total - right - left, total - right, left), (total - right, total, right)


def whole_groups(count):
    return count // GROUP * GROUP


def each_run(dims, who, counts, piece, visit):
    sources, slot = dims[:2]
    first, end = piece[:2]

    def step(source, start):
        after = start + whole_groups(counts[source])
        begin = jnp.maximum(start, first)
        stop = jnp.minimum(after, end)

        @pl.when(stop > begin)
        def _():
            row = source * slot + begin - start
            visit(aligned(row), aligned(begin - first), aligned(stop - begin))

        return after

    lax.fori_loop(0, sources, step, who[TAILS])


def copies_between(held, streams, place, values, tangents, row, size):
    return (
        (values.at[pl.ds(row, size)], held.at[streams, pl.ds(place, size)]),
        (tangents.at[:, pl.ds(row, size)], held.at[pl.ds(streams + 1, 3), pl.ds(place, size)]),
    )


def wait_for(held, streams, size, sem):
    @pl.when(size > 0)
    def _():
        part = held.at[streams, pl.ds(0, aligned(size))]
        pltpu.make_async_copy(part, part, sem).wait()


def each_tail(dims, counts, visit):
    sources, slot = dims[:2]

    def step(source, found):
        left = counts[source] % GROUP
        row = source * slot + jnp.minimum(whole_groups(counts[source]), slot - GROUP)
        visit(source, aligned(row), left)
        return found + jnp.minimum(left, 1)

    return lax.fori_loop(0, sources, step, jnp.int32(0))


def tail_matrix(dims, counts):
    wide = dims[0] * GROUP
    lane = lax.broadcasted_iota(jnp.int32, (8, wide), 1)
    target = jnp.full((8, wide), -1, jnp.int32)
    start = jnp.int32(0)
    for source in range(dims[0]):
        left = counts[source] % GROUP
        row = lane - source * GROUP
        target = jnp.where((row >= 0) & (row < left), start + row, target)
        start = start + left
    number = lax.broadcasted_iota(jnp.int32, (wide, wide), 0)
    return jnp.where(number == target[:1], 1.0, 0.0).astype(BF16)


def make_who(dims, counts, who):
    place = lax.axis_index("dp")
    around = (place & 3) ^ ((place & 3) >> 1)
    back = (place >> 2) & 1
    who[PLACE] = (place >> 2) * 4 + around * (1 - back) + (3 - around) * back
    who[SIDE] = lax.axis_index("tensor")
    who[QUARTER] = my_quarter()

    def step(source, carry):
        whole, left = carry
        return whole + whole_groups(counts[source]), left + counts[source] % GROUP

    whole, left = lax.fori_loop(0, dims[0], step, (jnp.int32(0), jnp.int32(0)))
    left = (left + GROUP - 1) // GROUP * GROUP
    who[TOTAL] = whole + left
    who[TAILS] = left


def start_copies(held, place, sources, row, size, sem):
    for streams, (values, tangents) in zip((0, 4), sources):
        for copy in copies_between(held, streams, place, values, tangents, row, size):
            pltpu.make_async_copy(*copy, sem).start()


def pack_kernel(dims, base, rows, moving, who, counts, *refs):
    plan = None
    if moving or base == OVER:
        plan, *refs = refs
    sources, refs = (refs[:2], refs[2:4]), refs[4:]
    neighbours = ()
    if moving:
        neighbours, refs = refs[:2], refs[2:]
    keep, send, held, sems, *tails = refs
    side = who[SIDE]
    piece = own_piece(plan[KEPT] if moving else who[TOTAL], plan, base, rows)
    size = piece[2]

    if base == 0:
        ends, packed = tails

        def start_tail(source, row, left):
            start_copies(ends, aligned(source * GROUP), sources, row, GROUP, sems.at[1])

        each_tail(dims, counts, start_tail)
        size = size - who[TAILS]

    def start(row, place, size):
        start_copies(held, place, sources, row, size, sems.at[0])

    each_run(dims, who, counts, piece, start)
    arrivals = []
    if moving:
        pieces = moved_pieces(dims, plan, base, rows)
        for number, neighbour in enumerate(neighbours):
            place, moved = pieces[number]
            copy = pltpu.make_async_copy(
                neighbour.at[:, pl.ds(0, moved)], held.at[:, pl.ds(place, moved)], sems.at[1 + number]
            )
            arrivals.append((moved, copy))
        for moved, copy in arrivals:
            pl.when(moved > 0)(copy.start)
    if base == 0:
        matrix = tail_matrix(dims, counts)
        wait_for(ends, slice(0, 8), jnp.int32(dims[0] * GROUP), sems.at[1])
        for stream in range(8):
            packed[stream] = dot(matrix, ends[stream]).astype(BF16)

        def put(group, carry):
            here = pl.ds(aligned(group * GROUP), GROUP)
            held[:, here, :] = packed[:, here, :]
            return carry

        lax.fori_loop(0, who[TAILS] // GROUP, put, 0)
    wait_for(held, slice(0, 8), size, sems.at[0])
    for moved, copy in arrivals:
        pl.when(moved > 0)(copy.wait)
    out = [
        pltpu.make_async_copy(
            held.at[:, pl.ds(aligned(part * rows), rows)], target, sems.at[5 + number]
        )
        for number, (part, target) in enumerate(((1 - side, send), (side, keep)))
    ]
    for copy in out:
        copy.start()
    for copy in out:
        copy.wait()


def pack(dims, who, counts, plan, arrays, base, rows, neighbours=()):
    half = arrays[0].shape[1]
    shape = jax.ShapeDtypeStruct((8, rows, half), BF16)
    plans = (plan,) if neighbours or base == OVER else ()
    tails = [pltpu.VMEM((8, dims[0] * GROUP, half), BF16)] * 2 if base == 0 else []
    return pl.pallas_call(
        functools.partial(pack_kernel, dims, base, rows, len(neighbours) > 0),
        out_shape=(shape, shape),
        in_specs=[SCALARS] * (2 + len(plans)) + [HBM] * (4 + len(neighbours)),
        out_specs=(HBM, HBM),
        scratch_shapes=[pltpu.VMEM((8, 2 * rows, half), BF16), pltpu.SemaphoreType.DMA((7,))] + tails,
        cost_estimate=NO_COST,
        compiler_params=PARAMS,
        name="pack",
    )(who, counts, *plans, *arrays, *neighbours)


def export_kernel(dims, moved, who, counts, plan, x, x3, g, g3, *refs):
    targets, (held, sems) = refs[:2], refs[2:]
    pieces = sent_pieces(who, plan)
    for number, piece in enumerate(pieces):

        def start(row, place, size, number=number):
            place = aligned(number * moved + place)
            start_copies(held, place, ((x, x3), (g, g3)), row, size, sems.at[number])

        @pl.when(piece[2] > 0)
        def _(piece=piece, start=start):
            each_run(dims, who, counts, piece, start)

    for number, piece in enumerate(pieces):
        wait_for(held, slice(0, 8), piece[2], sems.at[number])
    out = [
        pltpu.make_async_copy(
            held.at[:, pl.ds(number * moved, moved)], target, sems.at[2 + number]
        )
        for number, target in enumerate(targets)
    ]
    for copy in out:
        copy.start()
    for copy in out:
        copy.wait()


def export(dims, who, counts, plan, x, x3, g, g3, moved):
    half = x.shape[1]
    return pl.pallas_call(
        functools.partial(export_kernel, dims, moved),
        out_shape=(jax.ShapeDtypeStruct((8, moved, half), BF16),) * 2,
        in_specs=[SCALARS] * 3 + [HBM] * 4,
        out_specs=(HBM,) * 2,
        scratch_shapes=[pltpu.VMEM((8, 2 * moved, half), BF16), pltpu.SemaphoreType.DMA((4,))],
        cost_estimate=NO_COST,
        compiler_params=PARAMS,
        name="export",
    )(who, counts, plan, x, x3, g, g3)


def load_results(held, rows, side, mine, theirs, sems):
    loads = [(0, 1 - side, part) for part in theirs[:1]] + [(4, 1 - side, part) for part in theirs[1:]]
    loads += [(4 * number, side, part) for number, part in enumerate(mine)]
    loads = [
        pltpu.make_async_copy(
            origin,
            held.at[pl.ds(first, origin.shape[0]), pl.ds(aligned(part * rows), rows)],
            sems.at[number],
        )
        for number, (first, part, origin) in enumerate(loads)
    ]
    for load in loads:
        load.start()
    for load in loads:
        load.wait()


def handback_kernel(dims, base, rows, who, plan, *refs):
    mine, theirs, targets, (held, sems) = refs[:2], refs[2:4], refs[4:6], refs[6:]
    load_results(held, rows, who[SIDE], mine, theirs, sems)
    copies = []
    pieces = moved_pieces(dims, plan, base, rows)
    for number, ((place, size), target) in enumerate(zip(pieces, targets)):
        copy = pltpu.make_async_copy(
            held.at[:, pl.ds(place, size)], target.at[:, pl.ds(0, size)], sems.at[4 + number]
        )
        copies.append((size, copy))
    for size, copy in copies:
        pl.when(size > 0)(copy.start)
    for size, copy in copies:
        pl.when(size > 0)(copy.wait)


def handback(dims, who, plan, mine, theirs, base, rows, moved):
    half = mine[0].shape[2]
    shape = jax.ShapeDtypeStruct((8, moved, half), BF16)
    return pl.pallas_call(
        functools.partial(handback_kernel, dims, base, rows),
        out_shape=(shape, shape),
        in_specs=[SCALARS] * 2 + [HBM] * 4,
        out_specs=(HBM, HBM),
        scratch_shapes=[pltpu.VMEM((8, 2 * rows, half), BF16), pltpu.SemaphoreType.DMA((6,))],
        cost_estimate=SOME_COST,
        compiler_params=PARAMS,
        name="handback",
    )(who, plan, *mine, *theirs)


def unpack_kernel(dims, base, rows, streams, parts, who, counts, plan, *refs):
    pairs = streams // 4
    mine, theirs, refs = refs[:parts], refs[parts], refs[parts + 1 :]
    outs, (held, sems, *tails) = refs[2 * pairs : 4 * pairs], refs[4 * pairs :]
    load_results(held, rows, 1 if base is None else who[SIDE], mine, [theirs], sems)
    pieces = sent_pieces(who, plan)
    if base is not None:
        pieces = (own_piece(plan[KEPT], plan, base, rows),)
    sizes = [piece[2] for piece in pieces]
    if base == 0:
        sizes = [sizes[0] - who[TAILS]]

    def start_out(origin, place, row, size, sem):
        for number in range(pairs):
            copies = copies_between(
                origin, 4 * number, place, outs[2 * number], outs[2 * number + 1], row, size
            )
            for there, here in copies:
                pltpu.make_async_copy(here, there, sem).start()

    for number, piece in enumerate(pieces):

        def start(row, place, size, number=number):
            start_out(held, aligned(number * rows + place), row, size, sems.at[3 + number])

        @pl.when(piece[2] > 0)
        def _(piece=piece, start=start):
            each_run(dims, who, counts, piece, start)

    if base == 0:
        (ends,) = tails
        matrix = tail_matrix(dims, counts)
        for stream in range(streams):
            packed = held[stream, : dims[0] * GROUP, :]
            ends[stream] = dot(matrix, packed, TN).astype(BF16)

        def start_tail(source, row, left):
            @pl.when(left > 0)
            def _():
                start_out(ends, aligned(source * GROUP), row, GROUP, sems.at[4])

        found = each_tail(dims, counts, start_tail)
        wait_for(ends, slice(0, streams), found * GROUP, sems.at[4])
    for number, size in enumerate(sizes):
        wait_for(held, slice(0, streams), size, sems.at[3 + number])


def unpack(dims, who, counts, plan, mine, theirs, outs, base, rows):
    half = outs[0].shape[1]
    streams = theirs.shape[0]
    tails = [pltpu.VMEM((streams, dims[0] * GROUP, half), BF16)] if base == 0 else []
    first = 4 + len(mine)
    return pl.pallas_call(
        functools.partial(unpack_kernel, dims, base, rows, streams, len(mine)),
        out_shape=[jax.ShapeDtypeStruct(out.shape, BF16) for out in outs],
        in_specs=[SCALARS] * 3 + [HBM] * (len(mine) + 1 + len(outs)),
        out_specs=[HBM] * len(outs),
        input_output_aliases={first + number: number for number in range(len(outs))},
        scratch_shapes=[
            pltpu.VMEM((streams, 2 * rows, half), BF16),
            pltpu.SemaphoreType.DMA((5,)),
        ]
        + tails,
        cost_estimate=LAST_COST if base == 0 else NO_COST,
        compiler_params=PARAMS,
        name="unpack",
    )(who, counts, plan, *mine, theirs, *outs)


def unpack_part_kernel(dims, base, rows, parts, own, who, counts, plan, *refs):
    arrays, refs = refs[:parts], refs[parts:]
    outs, (held, ends, sems) = refs[4:8], refs[8:]
    part = who[SIDE] if own else 1 - who[SIDE]
    loads = [
        pltpu.make_async_copy(array, held.at[pl.ds(4 * number, array.shape[0])], sems.at[number])
        for number, array in enumerate(arrays)
    ]
    for load in loads:
        load.start()
    for load in loads:
        load.wait()
    first = base + part * rows
    size = jnp.clip(plan[KEPT] - first, 0, rows)

    def start_out(origin, place, row, size, sem):
        for number in range(2):
            copies = copies_between(
                origin, 4 * number, place, outs[2 * number], outs[2 * number + 1], row, size
            )
            for there, here in copies:
                pltpu.make_async_copy(here, there, sem).start()

    def start(row, place, size):
        start_out(held, place, row, size, sems.at[2])

    each_run(dims, who, counts, (first, first + size, size), start)

    @pl.when(part == 0)
    def _():
        matrix = tail_matrix(dims, counts)
        for stream in range(8):
            packed = held[stream, : dims[0] * GROUP, :]
            ends[stream] = dot(matrix, packed, TN).astype(BF16)

        def start_tail(source, row, left):
            @pl.when(left > 0)
            def _():
                start_out(ends, aligned(source * GROUP), row, GROUP, sems.at[3])

        found = each_tail(dims, counts, start_tail)
        wait_for(ends, slice(0, 8), found * GROUP, sems.at[3])

    wait_for(held, slice(0, 8), size - jnp.where(part == 0, who[TAILS], 0), sems.at[2])


def unpack_part(dims, who, counts, plan, arrays, outs, base, rows, own):
    half = outs[0].shape[1]
    first = 3 + len(arrays)
    return pl.pallas_call(
        functools.partial(unpack_part_kernel, dims, base, rows, len(arrays), own),
        out_shape=[jax.ShapeDtypeStruct(out.shape, BF16) for out in outs],
        in_specs=[SCALARS] * 3 + [HBM] * (len(arrays) + len(outs)),
        out_specs=[HBM] * len(outs),
        input_output_aliases={first + number: number for number in range(len(outs))},
        scratch_shapes=[
            pltpu.VMEM((8, rows, half), BF16),
            pltpu.VMEM((8, dims[0] * GROUP, half), BF16),
            pltpu.SemaphoreType.DMA((4,)),
        ],
        cost_estimate=NO_COST if own else LAST_COST,
        compiler_params=PARAMS,
        name="unpack_part",
    )(who, counts, plan, *arrays, *outs)


def blank_kernel(sources, slot, counts, values, tangents, other_values, other_tangents, zeros, sem):
    zeros[...] = jnp.zeros_like(zeros)

    def step(source, total):
        padded = round_up(counts[source])
        size = aligned(slot - padded)
        row = aligned(source * slot + padded)

        @pl.when(size > 0)
        def _():
            for low, high in ((values, tangents), (other_values, other_tangents)):
                for here, there in (
                    (zeros.at[0, pl.ds(0, size)], low.at[pl.ds(row, size)]),
                    (zeros.at[:, pl.ds(0, size)], high.at[:, pl.ds(row, size)]),
                ):
                    pltpu.make_async_copy(here, there, sem).start()

        return total + size

    total = lax.fori_loop(0, sources, step, jnp.int32(0))
    for low, high in ((values, tangents), (other_values, other_tangents)):

        @pl.when(total > 0)
        def _():
            low_part, high_part = low.at[pl.ds(0, aligned(total))], high.at[:, pl.ds(0, aligned(total))]
            pltpu.make_async_copy(low_part, low_part, sem).wait()
            pltpu.make_async_copy(high_part, high_part, sem).wait()


def blank(counts, row_count, half, sources):
    slot = row_count // sources
    values = jax.ShapeDtypeStruct((row_count, half), BF16)
    tangents = jax.ShapeDtypeStruct((3, row_count, half), BF16)
    return pl.pallas_call(
        functools.partial(blank_kernel, sources, slot),
        out_shape=(values, tangents, values, tangents),
        in_specs=[SCALARS],
        out_specs=(HBM, HBM, HBM, HBM),
        scratch_shapes=[pltpu.VMEM((3, slot, half), BF16), pltpu.SemaphoreType.DMA],
        cost_estimate=NO_COST,
        compiler_params=PARAMS,
        name="blank",
    )(counts)


NN = (((1,), (0,)), ((), ()))
TN = (((0,), (0,)), ((), ()))


def dot(a, b, dims=NN):
    return lax.dot_general(a, b, dims, preferred_element_type=F32)


def blocks_kernel(
    dims,
    base,
    rows,
    tile,
    first,
    final,
    merged,
    who,
    own,
    got,
    w_in,
    w_out,
    w_in_t,
    w_out_t,
    bias,
    *rest,
):
    if base != 0:
        plan, *rest = rest
    if first:
        grads_before = bias_before = None
    else:
        grads_before, bias_before, *rest = rest
    y_own, d_own, *rest = rest
    if merged:
        send, *rest = rest
        y_send, d_send = send.at[pl.ds(0, 4)], send.at[pl.ds(4, 4)]
    else:
        y_send, d_send, *rest = rest
    if final:
        kept, *rest = rest
        sent, rest = rest[:2], rest[2:]
    grads, biases, x_low, acts, slopes, lin = rest
    step = pl.program_id(0)
    side = who[SIDE]
    wide = w_in.shape[1]
    half = wide // 2

    @pl.when(step == 0)
    def _():
        if first:
            grads[...] = jnp.zeros_like(grads)
            biases[...] = jnp.zeros_like(biases)
        else:
            grads[...] = grads_before[...]
            biases[...] = bias_before[...]

    packed = side * rows + step * tile + lax.broadcasted_iota(jnp.int32, (tile, 128), 0)
    if base == OVER:
        filled = packed < plan[OVER_LEFT]
    elif base == 0:
        filled = packed < who[TOTAL]
    else:
        packed = packed + base
        top = 2 * dims[2] - plan[IN_LEFT] - plan[IN_RIGHT]
        filled = (packed < plan[KEPT]) | (packed >= top)
    filled = jnp.where(filled, 1.0, 0.0)
    is_filled = jnp.concatenate([filled] * (wide // 128), axis=1) > 0.0

    def load(stream):
        mine, theirs = own[stream].astype(F32), got[stream].astype(F32)
        left = jnp.where(side == 0, mine, theirs)
        right = jnp.where(side == 0, theirs, mine)
        return jnp.where(is_filled, jnp.concatenate([left, right], axis=1), 0.0)

    def store(own, send, stream, value):
        left, right = value[:, :half].astype(BF16), value[:, half:].astype(BF16)
        own[stream] = jnp.where(side == 0, left, right)
        send[stream] = jnp.where(side == 0, right, left)

    def add_bias(place, value):
        biases[place] += jnp.sum(value.reshape(tile // 8, 8, wide), axis=0)

    x = [load(stream) for stream in range(4)]
    for block in range(2):
        for stream in range(4):
            x_low[block, stream * tile : (stream + 1) * tile] = x[stream].astype(BF16)
        pre = dot(x_low[block], w_in[block])
        z = pre[:tile] + bias[0, block][None, :]
        small = jnp.exp(-jnp.abs(z))
        whole = 1.0 / (1.0 + small)
        slope = jnp.where(z >= 0.0, whole, small * whole)
        slopes[block] = slope
        acts[block, :tile] = (jnp.maximum(z, 0.0) + jnp.log1p(small) - LOG_TWO).astype(BF16)
        for stream in range(1, 4):
            part = pre[stream * tile : (stream + 1) * tile]
            lin[block, stream - 1] = part
            acts[block, stream * tile : (stream + 1) * tile] = (slope * part).astype(BF16)
        out = dot(acts[block], w_out[block])
        x = [x[stream] + out[stream * tile : (stream + 1) * tile] for stream in range(4)]
        x[0] = x[0] + bias[1, block][None, :]
    for stream in range(4):
        store(y_own, y_send, stream, x[stream])

    g = [load(4 + stream) for stream in range(4)]
    for block in (1, 0):
        add_bias(2 + block, g[0])
        g_low = jnp.concatenate([part.astype(BF16) for part in g], axis=0)
        value = dot(acts[block], g_low, TN)
        for part in range(2):
            place = 2 * wide + block * wide + part * half
            grads[0, place : place + half, :] += value[:half, part * half : (part + 1) * half]
            grads[1, place : place + half, :] += value[half:, part * half : (part + 1) * half]
        mixed = dot(g_low, w_out_t[block])
        slope = slopes[block]
        total = jnp.zeros((tile, wide), F32)
        lower = []
        for stream in range(1, 4):
            part = mixed[stream * tile : (stream + 1) * tile]
            total = total + part * lin[block, stream - 1]
            lower.append((part * slope).astype(BF16))
        g_pre = (mixed[:tile] * slope + slope * (1.0 - slope) * total).astype(BF16)
        add_bias(block, g_pre.astype(F32))
        stack = jnp.concatenate([g_pre] + lower, axis=0)
        value = dot(x_low[block], stack, TN)
        for part in range(2):
            grads[part, block * wide : (block + 1) * wide, :] += value[:, part * half : (part + 1) * half]
        back = dot(stack, w_in_t[block])
        g = [g[stream] + back[stream * tile : (stream + 1) * tile] for stream in range(4)]
    for stream in range(4):
        store(d_own, d_send, stream, g[stream])

    if final:

        @pl.when(step == rows // tile - 1)
        def _():
            total = jnp.sum(biases[...], axis=1)
            for part in range(2):
                grads[part, 4 * wide : 4 * wide + 4, :] = total[:, part * half : (part + 1) * half]
            flag = who[QUARTER] >> 1
            size = kept.shape[1]
            kept[...] = grads[:, pl.ds(aligned(flag * size), size), :]
            for part in range(2):
                other = grads[part, pl.ds(aligned((1 - flag) * size), size), :]
                sent[part][...] = other.astype(BF16)


def tile_of(rows):
    return max(tile for tile in range(GROUP, 193, GROUP) if rows % tile == 0)


def run_blocks(dims, who, plan, own, got, weights, sums, base, final, merged):
    rows, half = own.shape[1:]
    wide = 2 * half
    tile = tile_of(rows)
    first = sums is None
    piece = pl.BlockSpec((8, tile, half), lambda i: (0, i, 0))

    def whole(array):
        return pl.BlockSpec(
            array.shape, lambda i, rank=len(array.shape): (0,) * rank, pipeline_mode=pl.Buffered(1)
        )

    sum_rows = 4 * wide + dims[3]
    sums_held = [((2, sum_rows, half), F32), ((4, 8, wide), F32)]
    if final:
        results = [((2, sum_rows // 2, half), F32)] + [((sum_rows // 2, half), BF16)] * 2
        scratch = [pltpu.VMEM(*item) for item in sums_held]
    else:
        results, scratch = sums_held, []
    results = [jax.ShapeDtypeStruct(*item) for item in results]
    sizes = (4, 4, 8) if merged else (4, 4, 4, 4)
    out_shapes = [jax.ShapeDtypeStruct((size, rows, half), BF16) for size in sizes]
    out_pieces = [pl.BlockSpec((size, tile, half), lambda i: (0, i, 0)) for size in sizes]
    plans = () if base == 0 else (plan,)
    extra = () if first else sums
    operands = (who, own, got, *weights, *plans, *extra)
    aliases = {}
    if not first and not final:
        aliases = {len(operands) - 2 + i: len(sizes) + i for i in range(2)}
    return pl.pallas_call(
        functools.partial(blocks_kernel, dims, base, rows, tile, first, final, merged),
        grid=(rows // tile,),
        out_shape=out_shapes + results,
        in_specs=[SCALARS]
        + [piece] * 2
        + [whole(item) for item in weights]
        + [SCALARS] * len(plans)
        + [whole(item) for item in extra],
        out_specs=out_pieces + [whole(item) for item in results],
        input_output_aliases=aliases,
        scratch_shapes=scratch
        + [
            pltpu.VMEM((2, 4 * tile, wide), BF16),
            pltpu.VMEM((2, 4 * tile, wide), BF16),
            pltpu.VMEM((2, tile, wide), F32),
            pltpu.VMEM((2, 3, tile, wide), F32),
        ],
        cost_estimate=pl.CostEstimate(
            flops=rows * COST_PER_ROW if base == 0 else 0, bytes_accessed=1024, transcendentals=0
        ),
        compiler_params=PARAMS,
        name="blocks",
    )(*operands)


def swap_tensor(value):
    return lax.ppermute(value, "tensor", [(0, 1), (1, 0)])


def shift(value, order, step):
    pairs = list(zip(order[:-1], order[1:]))
    return lax.ppermute(value, "dp", pairs if step == 1 else [(b, a) for a, b in pairs])


def in_order(flag, mine, other, axis):
    return jnp.where(
        flag == 0, jnp.concatenate([mine, other], axis), jnp.concatenate([other, mine], axis)
    )


def my_quarter():
    place = lax.axis_index("dp")
    return (place & 1) * 2 + ((place >> 1) & 1)


def quarter_kernel(dims, counts, w_in, w_out, who, piece, sems):
    half = w_in.shape[2]
    mine = my_quarter()
    make_who(dims, counts, who)
    for number in range(4):

        @pl.when(mine == number)
        def _(number=number):
            if number < 2:
                copies = [pltpu.make_async_copy(w_in.at[number], piece, sems.at[0])]
            else:
                copies = [
                    pltpu.make_async_copy(
                        w_out.at[number - 2, :, pl.ds(part * half, half)],
                        piece.at[pl.ds(part * half, half)],
                        sems.at[part],
                    )
                    for part in range(2)
                ]
            for copy in copies:
                copy.start()
            for copy in copies:
                copy.wait()


def quarter_of(dims, counts, weight_in, weight_out):
    on_chip = pl.BlockSpec(memory_space=pltpu.VMEM)
    return pl.pallas_call(
        functools.partial(quarter_kernel, dims),
        out_shape=(
            jax.ShapeDtypeStruct((8,), jnp.int32),
            jax.ShapeDtypeStruct(weight_in.shape[1:], BF16),
        ),
        in_specs=[SCALARS] + [on_chip] * 2,
        out_specs=(SCALARS, on_chip),
        scratch_shapes=[pltpu.SemaphoreType.DMA((2,))],
        cost_estimate=NO_COST,
        name="quarter",
    )(counts, weight_in, weight_out)


def assemble_kernel(
    who, w_in, w_out, b_in, b_out, b_got, *refs
):
    pieces, (in_all, out_all, in_turned, out_turned, b_all, held, sems) = refs[:4], refs[4:]
    side, own = who[SIDE], who[QUARTER]
    half = w_in.shape[2]
    copies = [
        pltpu.make_async_copy(piece, held.at[own ^ number], sems.at[number])
        for number, piece in enumerate(pieces)
    ]
    for copy in copies:
        copy.start()
    for copy in copies:
        copy.wait()

    def ordered(mine, other, axis):
        return jnp.where(
            side == 0,
            jnp.concatenate([mine, other], axis),
            jnp.concatenate([other, mine], axis),
        )

    for block in range(2):
        value = ordered(w_in[block], held[block], 1)
        in_all[block] = value
        in_turned[block] = value.T
        other = jnp.concatenate([held[2 + block, :half], held[2 + block, half:]], axis=1)
        value = ordered(w_out[block], other, 0)
        out_all[block] = value
        out_turned[block] = value.T
    for number, mine in enumerate((b_in, b_out)):
        b_all[number] = ordered(mine[...], b_got[number], 1)


def assemble(who, weight_in, weight_out, bias_in, bias_out, bias_got, pieces):
    blocks, wide, half = weight_in.shape
    whole = jax.ShapeDtypeStruct((blocks, wide, wide), BF16)
    on_chip = pl.BlockSpec(memory_space=pltpu.VMEM)
    return pl.pallas_call(
        assemble_kernel,
        out_shape=(whole,) * 4 + (jax.ShapeDtypeStruct((2, blocks, wide), F32),),
        in_specs=[SCALARS] + [on_chip] * 5 + [HBM] * 4,
        out_specs=(on_chip,) * 5,
        scratch_shapes=[pltpu.VMEM((4, wide, half), BF16), pltpu.SemaphoreType.DMA((4,))],
        cost_estimate=NO_COST,
        compiler_params=PARAMS,
        name="assemble",
    )(who, weight_in, weight_out, bias_in, bias_out, bias_got, *pieces)


def flipped(value, flip, size):
    return lax.ppermute(value, "dp", [(i, i ^ flip) for i in range(size)])


def groups_of(bits):
    return [(0, 1), (1, 1)] + [(bit, min(2, bits - bit)) for bit in range(2, bits, 2)]


def reduce_step(grads, group, place, size):
    bit, many = group
    mine = (place >> bit) & ((1 << many) - 1)
    rows = grads.shape[1] >> many
    kept = lax.dynamic_slice_in_dim(grads, mine * rows, rows, 1)
    for flip in range(1, 1 << many):
        sent = lax.dynamic_slice_in_dim(grads, (mine ^ flip) * rows, rows, 1).astype(BF16)
        kept = kept + flipped(sent, flip << bit, size).astype(F32)
    return kept


def join_kernel(mine, *refs):
    parts, (whole, sems) = refs[:-2], refs[-2:]
    rows = parts[0].shape[0]
    copies = [
        pltpu.make_async_copy(
            part, whole.at[pl.ds(aligned((mine[0] ^ flip) * rows), rows)], sems.at[flip]
        )
        for flip, part in enumerate(parts)
    ]
    for copy in copies:
        copy.start()
    for copy in copies:
        copy.wait()


def gather_step(total, group, place, size):
    bit, many = group
    mine = (place >> bit) & ((1 << many) - 1)
    parts = [total] + [flipped(total, flip << bit, size) for flip in range(1, 1 << many)]
    rows, half = total.shape
    return pl.pallas_call(
        join_kernel,
        out_shape=jax.ShapeDtypeStruct((rows << many, half), BF16),
        in_specs=[SCALARS] + [HBM] * len(parts),
        out_specs=pl.BlockSpec(memory_space=pltpu.VMEM),
        scratch_shapes=[pltpu.SemaphoreType.DMA((len(parts),))],
        cost_estimate=NO_COST,
        name="join",
    )(mine.astype(jnp.int32)[None], *parts)


def sum_in_fours(values, step, size):
    flips = (step, 2 * step, 3 * step) if 2 * step < size else (step,)
    return values + sum(
        flipped(values, flip, size) for flip in flips
    )


def finish_kernel(flag, mine, other, grad_in, grad_out, bias_in, bias_out, held, sems):
    rows, half = mine.shape
    copies = [
        pltpu.make_async_copy(part, held.at[pl.ds(aligned(which * rows), rows)], sems.at[number])
        for number, (which, part) in enumerate(((flag[0], mine), (1 - flag[0], other)))
    ]
    for copy in copies:
        copy.start()
    for copy in copies:
        copy.wait()
    wide = 2 * half
    for block in range(2):
        grad_in[block] = held[block * wide : (block + 1) * wide, :].astype(F32)
        for part in range(2):
            first = (2 + block) * wide + part * half
            grad_out[block, :, part * half : (part + 1) * half] = held[first : first + half, :].astype(F32)
    last = held[4 * wide : 4 * wide + GROUP, :].astype(F32)
    bias_in[...] = last[:2]
    bias_out[...] = last[2:4]


def finish(flag, mine, other):
    rows, half = mine.shape
    on_chip = pl.BlockSpec(memory_space=pltpu.VMEM)
    return pl.pallas_call(
        finish_kernel,
        out_shape=(
            jax.ShapeDtypeStruct((2, 2 * half, half), F32),
            jax.ShapeDtypeStruct((2, half, 2 * half), F32),
            jax.ShapeDtypeStruct((2, half), F32),
            jax.ShapeDtypeStruct((2, half), F32),
        ),
        in_specs=[SCALARS] + [HBM] * 2,
        out_specs=(on_chip,) * 4,
        scratch_shapes=[pltpu.VMEM((2 * rows, half), BF16), pltpu.SemaphoreType.DMA((2,))],
        cost_estimate=NO_COST,
        compiler_params=PARAMS,
        name="finish",
    )(flag, mine, other)


def together(*values):
    return lax.optimization_barrier(values)


def local(
    dp_size,
    features,
    tangents,
    weight_in,
    bias_in,
    weight_out,
    bias_out,
    counts,
    cotangent_values,
    cotangent_tangents,
):
    row_count, half = features.shape
    sources = counts.shape[0]
    unit = row_count // 256
    level, first, moved, extra = (unit * part for part in (ROWS, FIRST, MOVED, EXTRA))
    order = chain_order(dp_size)
    bits = dp_size.bit_length() - 1
    dims = (sources, row_count // sources, level, 8 * dp_size)
    side = lax.axis_index("tensor")
    place = lax.axis_index("dp")
    arrays = (features, tangents, cotangent_values, cotangent_tangents)
    middle = (2 * first, level - first - moved)
    last = (2 * (level - moved), moved)

    who, piece = quarter_of(dims, counts, weight_in, weight_out)
    piece_got = swap_tensor(piece)
    bias_got = swap_tensor(jnp.stack([bias_in, bias_out]))
    totals = jnp.where(jnp.arange(dp_size, dtype=jnp.int32) == place, who[TOTAL], 0)
    totals = sum_in_fours(totals, 1, dp_size)
    own1, send1 = pack(dims, who, counts, None, arrays, 0, first)
    send1, piece_got, bias_got = together(send1, piece_got, bias_got)
    got1 = swap_tensor(send1)
    pieces = [piece_got] + [flipped(piece_got, flip, dp_size) for flip in (2, 1, 3)]
    who, own1, totals = together(who, own1, totals)
    own2, send2 = pack(dims, who, counts, None, arrays, *middle)
    got2 = swap_tensor(send2)
    for step in range(2, bits, 2):
        totals = sum_in_fours(totals, 1 << step, dp_size)
    totals, own2 = together(totals, own2)
    plan = make_plan(who, totals, order, level, 2 * first, moved, extra)
    plan, pieces = together(plan, pieces)
    to_left, to_right = export(dims, who, counts, plan, *arrays, moved)
    neighbours = (shift(to_right, order, 1), shift(to_left, order, -1))
    pieces, to_left = together(pieces, to_left)
    weights = assemble(who, weight_in, weight_out, bias_in, bias_out, bias_got, pieces)
    later_counts, weights = together(counts, weights)
    outs = tuple(blank(later_counts, row_count, half, sources))
    who, weights, neighbours, outs = together(who, weights, neighbours, outs)
    own3, send3 = pack(dims, who, counts, plan, arrays, *last, neighbours)
    got3 = swap_tensor(send3)
    own3, weights, got2 = together(own3, weights, got2)

    def blocks(base, plan, arrived, sums, final=False, merged=False):
        results = run_blocks(dims, who, plan, *arrived, weights, sums, base, final, merged)
        count = 3 if merged else 4
        return results[:count], tuple(results[count:])

    def place_all(outs, base, rows, plan, result, got):
        return unpack(dims, who, counts, plan, result[:2], got, outs, base, rows)

    def place_values(outs, base, rows, own, got):
        return (*unpack(dims, who, counts, plan, [own], got, outs[:2], base, rows), *outs[2:])

    def place_grads(outs, base, rows, own, got):
        return (*outs[:2], *unpack(dims, who, counts, plan, [own], got, outs[2:], base, rows))

    result1, sums = blocks(0, plan, (own1, got1), None, merged=True)

    def more(carry):
        return carry[0] < plan[ROUNDS]

    def extra_round(carry):
        number, sums, outs = carry
        done = number * (2 * extra)
        here = plan + jnp.zeros((8,), jnp.int32).at[OVER_FIRST].set(done).at[OVER_LEFT].set(-done)
        own, send = pack(dims, who, counts, here, arrays, OVER, extra)
        result, sums = blocks(OVER, here, (own, swap_tensor(send)), sums, merged=True)
        outs = place_all(outs, OVER, extra, here, result, swap_tensor(result[2]))
        return number + 1, sums, tuple(outs)

    _, sums, outs = lax.while_loop(more, extra_round, (jnp.int32(0), sums, outs))
    result2, sums = blocks(middle[0], plan, (own2, got2), sums, merged=True)
    yd2_got = swap_tensor(result2[2])
    sums, outs = together(sums, outs)
    result3, sums = blocks(last[0], plan, (own3, got3), sums, final=True)
    sums, yd2_got = together(sums, yd2_got)

    kept, *sent = sums
    core, across, *others = groups_of(bits)
    y3_got = swap_tensor(result3[2])
    d3_got = swap_tensor(result3[3])
    came = jnp.stack([flipped(part, 1, dp_size) for part in sent])
    grads = kept + came.astype(F32)
    grads = reduce_step(grads, across, place, dp_size)
    outs = place_all(outs, *middle, plan, result2, yd2_got)
    grads, y3_got, outs = together(grads, y3_got, outs)
    for group in others:
        grads = reduce_step(grads, group, place, dp_size)
    outs = place_values(outs, *last, result3[0], y3_got)
    grads, d3_got, outs = together(grads, d3_got, outs)
    mine = lax.dynamic_index_in_dim(grads, side, 0, keepdims=False)
    other = lax.dynamic_index_in_dim(grads, 1 - side, 0, keepdims=False).astype(BF16)
    total = (mine + swap_tensor(other).astype(F32)).astype(BF16)
    total, yd1_send = together(total, result1[2])
    yd1_got = swap_tensor(yd1_send)
    for bit, many in reversed(others):
        for step in range(bit, bit + many):
            total = gather_step(total, (step, 1), place, dp_size)
    plan, total = together(plan, total)
    to_left, to_right = handback(
        dims, who, plan, result3[:2], (y3_got, d3_got), *last, moved
    )
    back = (shift(to_left, order, -1), shift(to_right, order, 1))
    total = gather_step(total, across, place, dp_size)
    outs = place_grads(outs, *last, result3[1], d3_got)
    outs = unpack_part(dims, who, counts, plan, result1[:2], outs, 0, first, True)
    total, outs = together(total, outs)
    total_got = flipped(total, 1, dp_size)
    outs = unpack_part(dims, who, counts, plan, [yd1_got], outs, 0, first, False)
    sums = finish((place & 1).astype(jnp.int32)[None], total, total_got)
    outs = unpack(dims, who, counts, plan, back[:1], back[1], outs, None, moved)
    grad_in, grad_out, bias_in_grad, bias_out_grad = sums
    return (*outs, grad_in, bias_in_grad, grad_out, bias_out_grad)


def solution(mesh):
    in_specs = (
        P("dp", "tensor"),
        P(None, "dp", "tensor"),
        P(None, None, "tensor"),
        P(None, "tensor"),
        P(None, "tensor", None),
        P(None, "tensor"),
        P("dp"),
        P("dp", "tensor"),
        P(None, "dp", "tensor"),
    )
    out_specs = (
        P("dp", "tensor"),
        P(None, "dp", "tensor"),
        P("dp", "tensor"),
        P(None, "dp", "tensor"),
        P(None, None, "tensor"),
        P(None, "tensor"),
        P(None, "tensor", None),
        P(None, "tensor"),
    )
    return jax.shard_map(
        functools.partial(local, mesh.shape["dp"]),
        mesh=mesh,
        in_specs=in_specs,
        out_specs=out_specs,
        check_vma=False,
    )
```
